32 devices in a mesh: dp: 2 (over core), fsdp: 4 (over z), tile: 4 (over y, x).
Axes of the slice: x: 2, y: 2, z: 4, core: 2. Of those that a mesh axis runs over, the one named last changes fastest.
Arguments:
- tokens: bfloat16 [8, 8, 128, 1536], P(('dp', 'fsdp'), None, 'tile'), may hold values from -6 to 6
- norm_gain: float32 [1536], replicated, may hold values from 0.25 to 1.75
- query_key_value_weight: bfloat16 [1536, 2304], P('fsdp'), may hold values from -5 to 5
- out_weight: bfloat16 [768, 1536], P('fsdp'), may hold values from -0.21875 to 0.21875
- head_weight: bfloat16 [1536, 320], P('fsdp'), may hold values from -0.15625 to 0.15625
- coarse: float32 [8, 20, 8, 128], P(('dp', 'fsdp'), None, None, 'tile'), may hold values from -36 to 36
- grad_fine: float32 [8, 20, 32, 512], P(('dp', 'fsdp'), None, None, 'tile'), may hold values from -0.6 to 0.6
Outputs:
- fine_grid: float32 [8, 20, 32, 512], P(('dp', 'fsdp'), None, None, 'tile')
- grad_tokens: bfloat16 [8, 8, 128, 1536], P(('dp', 'fsdp'), None, 'tile')
- grad_head: float32 [1536, 320], P('fsdp')
The draws below stay inside these ranges and needn't reach their ends.
All inputs are finite; a program needn't handle non-finite values.
Results may differ from the reference program's by a relative error of at most 0.0059.
Values may be sent and summed in bfloat16 or wider, within the bound.
A program may use at most 64 MiB of HBM per device.

```python
import jax
import jax.numpy as jnp
from jax import lax

D = 1536
HEADS = 8
HEAD_DIM = 96
VARS = 20
MARGIN = 8
LAT = 8
LON_DEV = 32
INNER = 768
HEAD_OUT = 320
LON = 128
SAMPLES = 8
N_TILE = 4


def draw_query_key_value_weight(key, part):
    base_key = jax.random.fold_in(key, 101)
    entries = jax.random.normal(base_key, (D, 3 * INNER), jnp.float32) * D ** (-0.5)
    entries = jnp.clip(entries, -6.0 * D ** (-0.5), 6.0 * D ** (-0.5))
    return jnp.clip(entries, -5.0, 5.0).astype(jnp.bfloat16)


def steps_of(rng, shape, split, low, top_value):
    loudness, own = 1.0, jax.random.fold_in(rng, 6)
    for position, shards_of in split:
        steps = jnp.exp(jax.random.uniform(jax.random.fold_in(own, position), (shards_of,), jnp.float32, low / len(split), top_value / len(split)))
        loudness = loudness * jnp.repeat(steps, shape[position] // shards_of).reshape([-1 if axis == position else 1 for axis in range(len(shape))])
    return loudness


def scatter_about(key, shape, spread, reach, split=(), held_as=jnp.bfloat16):
    array = jax.random.normal(key, shape, jnp.float32) * spread
    if len(split) > 0:
        array = steps_of(key, shape, split, -0.22, 0.18) * array
    return jnp.clip(array, min=-reach, max=reach).astype(held_as)


def setup_inputs(seed: int = 0) -> dict:
    arg_keys = jax.random.split(jax.random.key(seed), 8)
    tokens = scatter_about(arg_keys[0], (SAMPLES, LAT, LON, D), 1.0, 6.0, ((0, 8), (2, 4)))
    norm_gain = jnp.clip(1.0 + 0.15 * jax.random.normal(arg_keys[1], (D,), jnp.float32), 0.25, 1.75)
    query_key_value_weight = draw_query_key_value_weight(jax.random.fold_in(arg_keys[7], 71), 0)
    out_weight = scatter_about(arg_keys[3], (INNER, D), INNER ** -0.5, 0.21875, ((0, 4),))
    head_weight = scatter_about(arg_keys[4], (D, HEAD_OUT), D ** -0.5, 0.15625, ((0, 4),))
    coarse = scatter_about(arg_keys[5], (SAMPLES, VARS, LAT, LON), 6.0, 36.0, ((0, 8), (3, 4)), jnp.float32)
    grad_fine = scatter_about(arg_keys[6], (SAMPLES, VARS, 4 * LAT, 4 * LON), 0.1, 0.6, ((0, 8), (3, 4)), jnp.float32)
    return {"tokens": tokens, "norm_gain": norm_gain, "query_key_value_weight": query_key_value_weight, "out_weight": out_weight, "head_weight": head_weight, "coarse": coarse, "grad_fine": grad_fine}


EPSILON = 1e-05

def layer_norm(values, norm_gain):
    average = lax.optimization_barrier(jnp.mean(values, axis=-1, keepdims=True))
    centred = values - average
    variance = lax.optimization_barrier(jnp.mean(centred * centred, axis=-1, keepdims=True))
    inverse_dev = lax.rsqrt(variance + EPSILON)
    return (centred * inverse_dev, inverse_dev)

def norm_backward(grad_normed, standard, inverse_dev, norm_gain):
    grad_standard = grad_normed * norm_gain
    first_mean = lax.optimization_barrier(jnp.mean(grad_standard, axis=-1, keepdims=True))
    second_mean = lax.optimization_barrier(jnp.mean(grad_standard * standard, axis=-1, keepdims=True))
    return inverse_dev * (grad_standard - first_mean - standard * second_mean)

def widen(values):
    return lax.optimization_barrier(values.astype(jnp.bfloat16)).astype(jnp.float32)

def attend_tile(queries, keys_values, grad_attended):
    query_count = queries.shape[0]
    key_count = keys_values.shape[0]
    score_scale = HEAD_DIM ** (-0.5)
    query_heads = queries.reshape(query_count, HEADS, HEAD_DIM).astype(jnp.float32)
    key_heads = keys_values[:, :INNER].reshape(key_count, HEADS, HEAD_DIM).astype(jnp.float32)
    value_heads = keys_values[:, INNER:].reshape(key_count, HEADS, HEAD_DIM).astype(jnp.float32)
    scores = jnp.einsum('qhd,khd->hqk', query_heads, key_heads) * score_scale
    biggest = lax.optimization_barrier(jnp.max(scores, axis=-1, keepdims=True))
    exponent = jnp.exp(scores - biggest)
    softmax_out = exponent / lax.optimization_barrier(jnp.sum(exponent, axis=-1, keepdims=True))
    softmax_low = widen(softmax_out)
    attended = jnp.einsum('hqk,khd->qhd', softmax_low, value_heads).astype(jnp.bfloat16)
    grad_heads = grad_attended.reshape(query_count, HEADS, HEAD_DIM).astype(jnp.float32)
    grad_values = jnp.einsum('hqk,qhd->khd', softmax_low, grad_heads)
    grad_weights = jnp.einsum('qhd,khd->hqk', grad_heads, value_heads)
    weighted = lax.optimization_barrier(jnp.sum(softmax_out * grad_weights, axis=-1, keepdims=True))
    grad_scores = widen(softmax_out * (grad_weights - weighted))
    grad_queries = (jnp.einsum('hqk,khd->qhd', grad_scores, key_heads) * score_scale).astype(jnp.bfloat16)
    grad_keys = jnp.einsum('hqk,qhd->khd', grad_scores, query_heads) * score_scale
    pair_gradient_rows = jnp.concatenate([grad_keys.reshape(key_count, INNER), grad_values.reshape(key_count, INNER)], axis=1)
    return (attended.reshape(query_count, INNER), grad_queries.reshape(query_count, INNER), pair_gradient_rows)

def interp_matrix(count, periodic):
    fine_index = jnp.arange(4 * count, dtype=jnp.int32)
    coarse_cell = fine_index // 4
    phase_index = fine_index % 4
    lower_shift = (phase_index < 2).astype(jnp.int32)
    lower_cell = coarse_cell - lower_shift
    upper_weight = (2 * phase_index - 3 + 8 * lower_shift).astype(jnp.float32) / 8.0
    if periodic:
        upper_cell = (lower_cell + 1) % count
        lower_cell = lower_cell % count
    else:
        upper_cell = jnp.clip(lower_cell + 1, 0, count - 1)
        lower_cell = jnp.clip(lower_cell, 0, count - 1)
    columns = jnp.arange(count, dtype=jnp.int32)
    lower_part = jnp.where(columns[None, :] == lower_cell[:, None], 1.0 - upper_weight[:, None], 0.0)
    upper_portion = jnp.where(columns[None, :] == upper_cell[:, None], upper_weight[:, None], 0.0)
    return (lower_part + upper_portion).astype(jnp.float32)

def one_sample(tokens, coarse, grad_fine, norm_gain, query_key_value_weight, out_weight, head_weight):
    flattened_rows = tokens.reshape(LAT * LON, D).astype(jnp.float32)
    standard, inverse_dev = layer_norm(flattened_rows, norm_gain)
    normed = (standard * norm_gain).astype(jnp.bfloat16)
    projected = jnp.dot(normed, query_key_value_weight, preferred_element_type=jnp.float32).astype(jnp.bfloat16)
    projected = projected.reshape(LAT, LON, 3 * INNER)
    grad_rows = grad_fine.reshape(VARS, LAT, 4, LON, 4).transpose(1, 3, 0, 2, 4).reshape(LAT * LON, HEAD_OUT)
    grad_rows = grad_rows.astype(jnp.bfloat16)
    grad_hidden = jnp.dot(grad_rows, head_weight.T, preferred_element_type=jnp.float32)
    grad_attended = jnp.dot(grad_hidden.astype(jnp.bfloat16), out_weight.T, preferred_element_type=jnp.float32)
    grad_attended = grad_attended.astype(jnp.bfloat16).reshape(LAT, LON, INNER)

    def per_tile(current_tile_index):
        first_col = current_tile_index * LON_DEV
        queries = lax.dynamic_slice_in_dim(projected[:, :, :INNER], first_col, LON_DEV, 1)
        columns = (first_col - MARGIN + jnp.arange(LON_DEV + 2 * MARGIN, dtype=jnp.int32)) % LON
        columns = columns.astype(jnp.int32)
        keys_values = jnp.take(projected[:, :, INNER:], columns, axis=1)
        grad_tile = lax.dynamic_slice_in_dim(grad_attended, first_col, LON_DEV, 1)
        attended, grad_queries, pair_gradient_rows = attend_tile(queries.reshape(-1, INNER), keys_values.reshape(-1, 2 * INNER), grad_tile.reshape(-1, INNER))
        return (attended.reshape(LAT, LON_DEV, INNER), grad_queries.reshape(LAT, LON_DEV, INNER), pair_gradient_rows.reshape(LAT, LON_DEV + 2 * MARGIN, 2 * INNER), columns)
    attended, grad_queries, pair_gradient_rows, columns = lax.map(per_tile, jnp.arange(N_TILE, dtype=jnp.int32))
    attended = attended.transpose(1, 0, 2, 3).reshape(LAT * LON, INNER)
    grad_queries = grad_queries.transpose(1, 0, 2, 3).reshape(LAT * LON, INNER)
    pair_total = jnp.zeros((LAT, LON, 2 * INNER), jnp.float32).at[:, columns].add(pair_gradient_rows.transpose(1, 0, 2, 3))
    mixed_out = jnp.dot(attended, out_weight, preferred_element_type=jnp.float32)
    hidden = (flattened_rows + mixed_out).astype(jnp.bfloat16)
    head_out = jnp.dot(hidden, head_weight, preferred_element_type=jnp.float32)
    fine_head = head_out.reshape(LAT, LON, VARS, 4, 4).transpose(2, 0, 3, 1, 4).reshape(VARS, 4 * LAT, 4 * LON)
    latitude_matrix = interp_matrix(LAT, False)
    lon_matrix = interp_matrix(LON, True)
    incomplete_grid = jnp.einsum('lj,kji->kli', latitude_matrix, coarse, precision=lax.Precision.HIGHEST)
    residual = jnp.einsum('vrb,cb->vrc', incomplete_grid, lon_matrix, precision=lax.Precision.HIGHEST)
    fine_grid = fine_head + residual
    head_term = jnp.dot(hidden.T, grad_rows, preferred_element_type=jnp.float32)
    grad_all = jnp.concatenate([grad_queries, pair_total.reshape(LAT * LON, 2 * INNER).astype(jnp.bfloat16)], axis=1)
    grad_normed = jnp.dot(grad_all, query_key_value_weight.T, preferred_element_type=jnp.float32)
    grad_input = grad_hidden + norm_backward(grad_normed, standard, inverse_dev, norm_gain)
    return (fine_grid, grad_input.astype(jnp.bfloat16).reshape(LAT, LON, D), head_term)

def reference(tokens, norm_gain, query_key_value_weight, out_weight, head_weight, coarse, grad_fine):

    def sample_step(running, inputs):
        fine_grid, grad_input, head_term = one_sample(inputs[0], inputs[1], inputs[2], norm_gain, query_key_value_weight, out_weight, head_weight)
        return (running + head_term, (fine_grid, grad_input))
    grad_head, outputs = lax.scan(sample_step, jnp.zeros((D, HEAD_OUT), jnp.float32), (tokens, coarse, grad_fine))
    return (outputs[0], outputs[1], grad_head)
```

```python
import functools

import jax
import jax.numpy as jnp
from jax import lax
from jax.experimental import pallas as pl
from jax.experimental.pallas import tpu as pltpu
from jax.sharding import PartitionSpec as P

D = 1536
HEADS = 8
HEAD_DIM = 96
VARS = 20
MARGIN = 8
INNER = 768
HEAD_OUT = 320


EPSILON = 1e-05


def with_halo(shard, sides, width):
    for axis, dim in sides:
        devices, length = (lax.axis_size(axis), shard.shape[dim])
        up = [(i, (i + 1) % devices) for i in range(devices)]
        down = [(j, i) for i, j in up]
        last = lax.slice_in_dim(shard, length - width, length, axis=dim)
        leading = lax.slice_in_dim(shard, 0, width, axis=dim)
        before = lax.ppermute(last, axis, up)
        after = lax.ppermute(leading, axis, down)
        shard = jnp.concatenate([before, shard, after], axis=dim)
    return shard


def from_behind(value, axis, steps):
    count = lax.axis_size(axis)
    pairs = [(source, (source + steps) % count) for source in range(count)]
    return lax.ppermute(value, axis, pairs)


def layer_norm(values):
    average = jnp.mean(values, axis=-1, keepdims=True)
    centred = values - average
    variance = jnp.mean(centred * centred, axis=-1, keepdims=True)
    inverse_dev = lax.rsqrt(variance + EPSILON)
    return (centred * inverse_dev, inverse_dev)


def norm_backward(grad_normed, standard, inverse_dev, norm_gain):
    grad_standard = grad_normed * norm_gain
    first_mean = jnp.mean(grad_standard, axis=-1, keepdims=True)
    second_mean = jnp.mean(grad_standard * standard, axis=-1, keepdims=True)
    return inverse_dev * (grad_standard - first_mean - standard * second_mean)


def attend_forward(queries, keys_values):
    query_count = queries.shape[0]
    key_count = keys_values.shape[0]
    score_scale = HEAD_DIM ** (-0.5)
    query_heads = queries.reshape(query_count, HEADS, HEAD_DIM)
    key_heads = keys_values[:, :INNER].reshape(key_count, HEADS, HEAD_DIM)
    value_heads = keys_values[:, INNER:].reshape(key_count, HEADS, HEAD_DIM)
    scores = (
        jnp.einsum("qhd,khd->hqk", query_heads, key_heads, preferred_element_type=jnp.float32)
        * score_scale
    )
    biggest = jnp.max(scores, axis=-1, keepdims=True)
    exponent = jnp.exp(scores - biggest)
    softmax_out = exponent / jnp.sum(exponent, axis=-1, keepdims=True)
    softmax_low = softmax_out.astype(jnp.bfloat16)
    attended = jnp.einsum(
        "hqk,khd->qhd", softmax_low, value_heads, preferred_element_type=jnp.float32
    )
    return (attended.astype(jnp.bfloat16).reshape(query_count, INNER), softmax_out)


def attend_backward(softmax_out, queries, keys_values, grad_attended):
    query_count = queries.shape[0]
    key_count = keys_values.shape[0]
    score_scale = HEAD_DIM ** (-0.5)
    query_heads = queries.reshape(query_count, HEADS, HEAD_DIM)
    key_heads = keys_values[:, :INNER].reshape(key_count, HEADS, HEAD_DIM)
    value_heads = keys_values[:, INNER:].reshape(key_count, HEADS, HEAD_DIM)
    grad_heads = grad_attended.reshape(query_count, HEADS, HEAD_DIM)
    softmax_low = softmax_out.astype(jnp.bfloat16)
    grad_values = jnp.einsum(
        "hqk,qhd->khd", softmax_low, grad_heads, preferred_element_type=jnp.float32
    )
    grad_weights = jnp.einsum(
        "qhd,khd->hqk", grad_heads, value_heads, preferred_element_type=jnp.float32
    )
    weighted = jnp.sum(softmax_out * grad_weights, axis=-1, keepdims=True)
    grad_scores = (softmax_out * (grad_weights - weighted)).astype(jnp.bfloat16)
    grad_queries = (
        jnp.einsum("hqk,khd->qhd", grad_scores, key_heads, preferred_element_type=jnp.float32)
        * score_scale
    )
    grad_keys = (
        jnp.einsum("hqk,qhd->khd", grad_scores, query_heads, preferred_element_type=jnp.float32)
        * score_scale
    )
    pair_gradient_rows = jnp.concatenate(
        [grad_keys.reshape(key_count, INNER), grad_values.reshape(key_count, INNER)], axis=1
    )
    return (grad_queries.astype(jnp.bfloat16).reshape(query_count, INNER), pair_gradient_rows)


def interp_weights(fine_index):
    coarse_cell = fine_index // 4
    phase_index = fine_index % 4
    lower_shift = (phase_index < 2).astype(jnp.int32)
    upper_weight = (2 * phase_index - 3 + 8 * lower_shift).astype(jnp.float32) / 8.0
    return (coarse_cell - lower_shift, upper_weight)


def build_matrix(lower_cell, upper_cell, upper_weight, count):
    columns = jnp.arange(count, dtype=jnp.int32)
    lower_part = jnp.where(
        columns[None, :] == lower_cell[:, None], 1.0 - upper_weight[:, None], 0.0
    )
    upper_portion = jnp.where(columns[None, :] == upper_cell[:, None], upper_weight[:, None], 0.0)
    return lower_part + upper_portion


def contract_last(left_side, right_side):
    return lax.dot_general(
        left_side, right_side, (((1,), (1,)), ((), ())), preferred_element_type=jnp.float32
    )


def dot_nt(left_side, right_side):
    return lax.dot_general(
        left_side, right_side, (((1,), (1,)), ((), ())), preferred_element_type=jnp.float32
    )


def dot_tn(left_side, right_side):
    return lax.dot_general(
        left_side, right_side, (((0,), (0,)), ((), ())), preferred_element_type=jnp.float32
    )


def dot_nn(left_side, right_side):
    return jnp.dot(left_side, right_side, preferred_element_type=jnp.float32)


HEAD, OUT0, OUT1, KEY, VALUE, QUERY0, QUERY1 = range(7)
ROUTES = (0, 0, 1, 0, 1, 0, 1)
HALF = INNER // 2
GROUP = 4
GROUP_WIDTH = GROUP * HEAD_DIM


def block_kernel(
    fsdp,
    lat_rows,
    lon_cols,
    tokens_ref,
    gain_ref,
    qkv_ref,
    out_ref,
    head_ref,
    grad_rows_ref,
    head_out_ref,
    grad_tokens_ref,
    grad_head_ref,
    w_head,
    w_out0,
    w_out1,
    w_key,
    w_value,
    w_query0,
    w_query1,
    standard_ref,
    normed_ref,
    q_ref,
    k_ref,
    v_ref,
    p_ref,
    att_ref,
    ga_ref,
    gh_ref,
    hidden_ref,
    gq_ref,
    gk_ref,
    gv_ref,
    gn_ref,
    halo_out,
    grad_halo_out,
    grad_halo_in,
    term_ref,
    rs0,
    snd1,
    rs1,
    acc1,
    snd2,
    rs2,
    acc2,
    snd3,
    rs3,
    full_grad,
    local_sem,
    w_send,
    w_recv,
    halo_send,
    halo_recv,
    rs_send,
    rs_recv,
):
    row_count = lat_rows * lon_cols
    halo_rows = lat_rows * MARGIN
    core = lax.axis_index("dp")
    me = lax.axis_index("fsdp")
    tile = lax.axis_index("tile")
    tiles = lax.axis_size("tile")
    ty, tx = tile // 2, tile % 2
    x_side = {"tile": tile + 1 - 2 * tx}
    y_side = {"tile": (tile + 2) % tiles}
    sibling = {"dp": 1 - core}
    right = {"tile": (tile + 1) % tiles}
    left = {"tile": (tile + tiles - 1) % tiles}

    barrier = pltpu.get_barrier_semaphore()
    partners = [{"tile": (tile + i) % tiles} for i in range(1, 4)]
    partners += [{"fsdp": (me + i) % fsdp} for i in range(1, fsdp)]
    partners += [sibling]
    for partner in partners:
        pl.semaphore_signal(barrier, inc=1, device_id=partner, device_id_type=pl.DeviceIdType.MESH)
    pl.semaphore_wait(barrier, len(partners))

    weights = (w_head, w_out0, w_out1, w_key, w_value, w_query0, w_query1)

    def own_piece(chunk):
        if chunk == HEAD:
            return head_ref.at[core, ty, tx]
        if chunk == OUT0:
            return out_ref.at[ty, tx, :, pl.ds(pl.multiple_of(core * 2 * HALF, 128), HALF)]
        if chunk == OUT1:
            return out_ref.at[ty, tx, :, pl.ds(pl.multiple_of(core * 2 * HALF + HALF, 128), HALF)]
        start, size = {
            KEY: (INNER, INNER),
            VALUE: (2 * INNER, INNER),
            QUERY0: (0, HALF),
            QUERY1: (HALF, HALF),
        }[chunk]
        return qkv_ref.at[core, ty, tx, :, pl.ds(start, size)]

    def remote(src, dst, send, recv, device):
        return pltpu.make_async_remote_copy(
            src_ref=src,
            dst_ref=dst,
            send_sem=send,
            recv_sem=recv,
            device_id=device,
            device_id_type=pl.DeviceIdType.MESH,
        )

    def weight_copy(chunk, stage, k):
        full = weights[chunk]
        send, recv = w_send.at[chunk, stage, k - 1], w_recv.at[chunk, stage, k - 1]
        source = (me + fsdp - k) % fsdp
        if stage == 0:
            return remote(
                own_piece(chunk),
                full.at[me, core, ty, tx],
                send,
                recv,
                {"fsdp": (me + k) % fsdp},
            )
        if stage == 1:
            part = full.at[source, core, ty, tx]
            device = x_side if ROUTES[chunk] == 0 else y_side
        elif stage == 2:
            if ROUTES[chunk] == 0:
                part, device = full.at[source, core, ty], y_side
            else:
                part, device = full.at[source, core, :, tx], x_side
        else:
            part, device = full.at[source, core], sibling
        return remote(part, part, send, recv, device)

    def advance(chunk, stage):
        for k in range(1, fsdp):
            if stage > 0:
                weight_copy(chunk, stage - 1, k).wait_recv()
            if stage < 4:
                weight_copy(chunk, stage, k).start()

    def local_copies():
        pairs = [(head_ref, w_head.at[me])]
        for d in range(2):
            for half, full in enumerate((w_out0, w_out1)):
                start = d * 2 * HALF + half * HALF
                pairs.append((out_ref.at[:, :, :, pl.ds(start, HALF)], full.at[me, d]))
        for full, start, size in (
            (w_key, INNER, INNER),
            (w_value, 2 * INNER, INNER),
            (w_query0, 0, HALF),
            (w_query1, HALF, HALF),
        ):
            pairs.append((qkv_ref.at[:, :, :, :, pl.ds(start, size)], full.at[me]))
        return [
            pltpu.make_async_copy(src, dst, local_sem.at[i]) for i, (src, dst) in enumerate(pairs)
        ]

    for chunk in range(7):
        advance(chunk, 0)
    copies = local_copies()
    for copy in copies:
        copy.start()

    scale = HEAD_DIM ** (-0.5)

    values = tokens_ref[...].astype(jnp.float32)
    average = jnp.mean(values, axis=-1, keepdims=True)
    centred = values - average
    variance = jnp.mean(centred * centred, axis=-1, keepdims=True)
    inverse_dev = lax.rsqrt(variance + EPSILON)
    standard = centred * inverse_dev
    standard_ref[...] = standard
    normed_ref[...] = (standard * gain_ref[...]).astype(jnp.bfloat16)

    def mat(ref, columns):
        return ref[...].reshape(-1, columns)

    advance(HEAD, 1)
    advance(OUT0, 1)
    advance(OUT1, 1)
    advance(HEAD, 2)
    advance(OUT0, 2)
    advance(OUT1, 2)
    advance(KEY, 1)
    advance(VALUE, 1)
    advance(HEAD, 3)
    advance(OUT0, 3)
    advance(OUT1, 3)
    advance(QUERY0, 1)
    advance(QUERY1, 1)
    advance(KEY, 2)
    advance(VALUE, 2)
    for copy in copies:
        copy.wait()
    advance(HEAD, 4)
    depth = w_head.shape[1] * 4 * w_head.shape[4]

    def grad_hidden_step(f, _):
        rows = w_head[f].reshape(depth, HEAD_OUT)
        gh_ref[:, pl.ds(pl.multiple_of(f * depth, 128), depth)] = dot_nt(grad_rows_ref[...], rows)
        return 0

    lax.fori_loop(0, fsdp, grad_hidden_step, 0)
    advance(OUT0, 4)
    advance(OUT1, 4)
    out_parts = [(d, half) for d in range(2) for half in range(2)]

    def out_block(d, half):
        full = (w_out0, w_out1)[half]
        return full[:, d].reshape(INNER, HALF)

    def out_columns(d, half):
        return pl.ds(d * 2 * HALF + half * HALF, HALF)

    grad_attended = jnp.zeros((row_count, INNER), jnp.float32)
    for d, half in out_parts:
        low = gh_ref[:, out_columns(d, half)].astype(jnp.bfloat16)
        grad_attended = grad_attended + dot_nt(low, out_block(d, half))
    ga_ref[...] = grad_attended.astype(jnp.bfloat16)

    advance(KEY, 3)
    advance(VALUE, 3)
    advance(QUERY0, 2)
    advance(QUERY1, 2)

    def edge(rows, first):
        shaped = rows.reshape(lat_rows, lon_cols, rows.shape[-1])
        part = shaped[:, :MARGIN] if first else shaped[:, lon_cols - MARGIN :]
        return part.reshape(halo_rows, rows.shape[-1])

    def halo_copy(which, side):
        full = (k_ref, v_ref)[which]
        dst = full.at[pl.ds(row_count + side * halo_rows, halo_rows)]
        return remote(
            halo_out.at[which, side],
            dst,
            halo_send.at[which, side],
            halo_recv.at[which, side],
            (right, left)[side],
        )

    step_columns = 256

    def project(full, which):
        target = (k_ref, v_ref)[which]

        def step(j, _):
            columns = pl.ds(pl.multiple_of(j * step_columns, 128), step_columns)
            rows = full[:, :, :, :, :, columns].reshape(-1, step_columns)
            product = dot_nn(normed_ref[...], rows)
            target[pl.ds(0, row_count), columns] = product.astype(jnp.bfloat16)
            halo_out[which, 0, :, columns] = edge(product, False).astype(jnp.bfloat16)
            halo_out[which, 1, :, columns] = edge(product, True).astype(jnp.bfloat16)
            return 0

        lax.fori_loop(0, INNER // step_columns, step, 0)
        for side in range(2):
            halo_copy(which, side).start()

    advance(KEY, 4)
    project(w_key, 0)
    advance(QUERY0, 3)
    advance(QUERY1, 3)
    advance(VALUE, 4)
    project(w_value, 1)
    advance(QUERY0, 4)
    q_ref[:, pl.ds(0, HALF)] = dot_nn(normed_ref[...], mat(w_query0, HALF)).astype(jnp.bfloat16)
    advance(QUERY1, 4)
    q_ref[:, pl.ds(HALF, HALF)] = dot_nn(normed_ref[...], mat(w_query1, HALF)).astype(jnp.bfloat16)
    for which in range(2):
        for side in range(2):
            halo_copy(which, side).wait_recv()

    def windows():
        for i in range(GROUP):
            low, high = i * HEAD_DIM, (i + 1) * HEAD_DIM
            start, stop = low // 128 * 128, -(-high // 128) * 128
            lanes = lax.broadcasted_iota(jnp.int32, (1, stop - start), 1) + start
            mask = ((lanes >= low) & (lanes < high)).astype(jnp.float32)
            yield i, start, stop, mask

    def forward(g, _):
        columns = pl.ds(pl.multiple_of(g * GROUP_WIDTH, 128), GROUP_WIDTH)
        queries, keys, vals = q_ref[:, columns], k_ref[:, columns], v_ref[:, columns]
        parts = [None] * (GROUP_WIDTH // 128)
        for i, start, stop, mask in windows():
            masked = queries[:, start:stop] * mask.astype(jnp.bfloat16)
            scores = dot_nt(masked, keys[:, start:stop]) * scale
            biggest = jnp.max(scores, axis=-1, keepdims=True)
            exponent = jnp.exp(scores - biggest)
            softmax = exponent / jnp.sum(exponent, axis=-1, keepdims=True)
            p_ref[g * GROUP + i] = softmax
            product = dot_nn(softmax.astype(jnp.bfloat16), vals[:, start:stop]) * mask
            add_parts(parts, start, product)
        att_ref[:, columns] = jnp.concatenate(parts, axis=1).astype(jnp.bfloat16)
        return 0

    def add_parts(parts, start, product):
        for j in range(product.shape[1] // 128):
            piece = product[:, j * 128 : (j + 1) * 128]
            at = start // 128 + j
            parts[at] = piece if parts[at] is None else parts[at] + piece

    lax.fori_loop(0, HEADS // GROUP, forward, 0)
    for d, half in out_parts:
        columns = out_columns(d, half)
        mixed = dot_nn(att_ref[...], out_block(d, half))
        hidden_ref[:, columns] = (tokens_ref[:, columns].astype(jnp.float32) + mixed).astype(
            jnp.bfloat16
        )

    def term_step(f, _):
        part = hidden_ref[:, pl.ds(pl.multiple_of(f * depth, 128), depth)]
        term_ref[f] = dot_tn(part, grad_rows_ref[...]).reshape(term_ref.shape[1:])
        return 0

    lax.fori_loop(0, fsdp, term_step, 0)

    core_copy = remote(term_ref.at[:, 1 - core], rs0, rs_send.at[0], rs_recv.at[0], sibling)
    y_copy = remote(snd1, rs1, rs_send.at[1], rs_recv.at[1], y_side)
    x_copy = remote(snd2, rs2, rs_send.at[2], rs_recv.at[2], x_side)
    z_copies = [
        remote(
            snd3.at[(me + k) % fsdp],
            rs3.at[k - 1],
            rs_send.at[5 + k],
            rs_recv.at[5 + k],
            {"fsdp": (me + k) % fsdp},
        )
        for k in range(1, fsdp)
    ]
    back = [
        remote(full_grad.at[core, ty, tx], full_grad.at[core, ty, tx], rs_send.at[3], rs_recv.at[3], x_side),
        remote(full_grad.at[core, ty], full_grad.at[core, ty], rs_send.at[4], rs_recv.at[4], y_side),
        remote(full_grad.at[core], full_grad.at[core], rs_send.at[5], rs_recv.at[5], sibling),
    ]

    core_copy.start()
    head_out_ref[...] = dot_nn(hidden_ref[...], mat(w_head, HEAD_OUT))

    def backward(g, _):
        columns = pl.ds(pl.multiple_of(g * GROUP_WIDTH, 128), GROUP_WIDTH)
        queries, keys, vals = q_ref[:, columns], k_ref[:, columns], v_ref[:, columns]
        grads = ga_ref[:, columns]
        query_parts = [None] * (GROUP_WIDTH // 128)
        key_parts = [None] * (GROUP_WIDTH // 128)
        value_parts = [None] * (GROUP_WIDTH // 128)
        for i, start, stop, mask in windows():
            softmax = p_ref[g * GROUP + i]
            masked = grads[:, start:stop] * mask.astype(jnp.bfloat16)
            weights_grad = dot_nt(masked, vals[:, start:stop])
            weighted = jnp.sum(softmax * weights_grad, axis=-1, keepdims=True)
            grad_scores = (softmax * (weights_grad - weighted)).astype(jnp.bfloat16)
            add_parts(query_parts, start, dot_nn(grad_scores, keys[:, start:stop]) * (mask * scale))
            add_parts(
                key_parts, start, dot_tn(grad_scores, queries[:, start:stop]) * (mask * scale)
            )
            add_parts(
                value_parts,
                start,
                dot_tn(softmax.astype(jnp.bfloat16), grads[:, start:stop]) * mask,
            )
        gq_ref[:, columns] = jnp.concatenate(query_parts, axis=1).astype(jnp.bfloat16)
        gk_ref[:, columns] = jnp.concatenate(key_parts, axis=1)
        gv_ref[:, columns] = jnp.concatenate(value_parts, axis=1)
        return 0

    lax.fori_loop(0, 1, backward, 0)

    core_copy.wait_recv()
    snd1[...] = (term_ref[:, core, 1 - ty] + rs0[:, 1 - ty]).astype(jnp.bfloat16)
    y_copy.start()
    acc1[...] = term_ref[:, core, ty] + rs0[:, ty]

    lax.fori_loop(1, HEADS // GROUP, backward, 0)

    def grad_halo_copy(which, side):
        return remote(
            grad_halo_out.at[which, side],
            grad_halo_in.at[which, side],
            halo_send.at[2 + which, side],
            halo_recv.at[2 + which, side],
            (left, right)[side],
        )

    for which, full in enumerate((gk_ref, gv_ref)):
        for side in range(2):
            rows = full[pl.ds(row_count + side * halo_rows, halo_rows), :]
            grad_halo_out[which, side] = rows.astype(jnp.bfloat16)
            grad_halo_copy(which, side).start()

    y_copy.wait_recv()
    snd2[...] = (acc1[:, 1 - tx] + rs1[:, 1 - tx].astype(jnp.float32)).astype(jnp.bfloat16)
    x_copy.start()
    acc2[...] = acc1[:, tx] + rs1[:, tx].astype(jnp.float32)

    def columns_of(f):
        return pl.ds(pl.multiple_of(f * depth, 128), depth)

    def grad_query_step(f, _):
        total = dot_nt(gq_ref[:, pl.ds(0, HALF)], w_query0[f].reshape(depth, HALF))
        total += dot_nt(gq_ref[:, pl.ds(HALF, HALF)], w_query1[f].reshape(depth, HALF))
        gn_ref[:, columns_of(f)] = total
        return 0

    lax.fori_loop(0, fsdp, grad_query_step, 0)

    x_copy.wait_recv()
    acc2[...] = acc2[...] + rs2[...].astype(jnp.float32)
    snd3[...] = acc2[...].astype(jnp.bfloat16)
    for copy in z_copies:
        copy.start()

    def own_cells(which):
        full = (gk_ref, gv_ref)[which]
        for side in range(2):
            grad_halo_copy(which, side).wait_recv()
        rows = full[pl.ds(0, row_count), :].reshape(lat_rows, lon_cols, INNER)
        shape = (lat_rows, MARGIN, INNER)
        last = grad_halo_in[which, 0].astype(jnp.float32).reshape(shape)
        first = grad_halo_in[which, 1].astype(jnp.float32).reshape(shape)
        rows = jnp.concatenate(
            [
                rows[:, :MARGIN] + first,
                rows[:, MARGIN : lon_cols - MARGIN],
                rows[:, lon_cols - MARGIN :] + last,
            ],
            axis=1,
        )
        return rows.reshape(row_count, INNER).astype(jnp.bfloat16)

    def add_pair(which, full):
        k_ref[pl.ds(0, row_count), :] = own_cells(which)

        def step(f, _):
            columns = columns_of(f)
            gn_ref[:, columns] += dot_nt(
                k_ref[pl.ds(0, row_count), :], full[f].reshape(depth, INNER)
            )
            return 0

        lax.fori_loop(0, fsdp, step, 0)

    add_pair(0, w_key)
    for copy in z_copies:
        copy.wait_recv()
    summed = acc2[me]
    for k in range(1, fsdp):
        summed = summed + rs3[k - 1].astype(jnp.float32)
    full_grad[core, ty, tx] = summed
    back[0].start()
    add_pair(1, w_value)
    back[0].wait_recv()
    back[1].start()

    values = tokens_ref[...].astype(jnp.float32)
    average = jnp.mean(values, axis=-1, keepdims=True)
    centred = values - average
    inverse_dev = lax.rsqrt(jnp.mean(centred * centred, axis=-1, keepdims=True) + EPSILON)
    grad_input = norm_backward(gn_ref[...], standard_ref[...], inverse_dev, gain_ref[...])
    grad_tokens_ref[...] = (gh_ref[...] + grad_input).astype(jnp.bfloat16)

    back[1].wait_recv()
    back[2].start()
    back[2].wait_recv()
    grad_head_ref[...] = full_grad[...]

    for chunk in range(7):
        for stage in range(4):
            for k in range(1, fsdp):
                weight_copy(chunk, stage, k).wait_send()
    for which in range(2):
        for side in range(2):
            halo_copy(which, side).wait_send()
            grad_halo_copy(which, side).wait_send()
    for copy in [core_copy, y_copy, x_copy] + z_copies + back:
        copy.wait_send()


def fused_block(tokens, norm_gain, qkv, out_weight, head_weight, grad_rows, lat_rows, lon_cols):
    fsdp = lax.axis_size("fsdp")
    row_count = lat_rows * lon_cols
    halo_rows = lat_rows * MARGIN
    key_count = row_count + 2 * halo_rows
    piece = qkv.shape[0] // 8
    out_piece = out_weight.shape[0] // 4
    bf16, f32 = jnp.bfloat16, jnp.float32
    vmem = pl.BlockSpec(memory_space=pltpu.VMEM)
    hbm = pl.BlockSpec(memory_space=pl.ANY)

    def full(rows, columns):
        return pltpu.VMEM((fsdp, 2, 2, 2, rows, columns), bf16)

    head_out, grad_tokens, grad_head = pl.pallas_call(
        functools.partial(block_kernel, fsdp, lat_rows, lon_cols),
        out_shape=(
            jax.ShapeDtypeStruct((row_count, HEAD_OUT), f32),
            jax.ShapeDtypeStruct((row_count, D), bf16),
            jax.ShapeDtypeStruct((2, 2, 2, piece, HEAD_OUT), f32),
        ),
        in_specs=[vmem, vmem, hbm, hbm, hbm, vmem],
        out_specs=(vmem, vmem, vmem),
        scratch_shapes=[
            full(piece, HEAD_OUT),
            full(out_piece, HALF),
            full(out_piece, HALF),
            full(piece, INNER),
            full(piece, INNER),
            full(piece, HALF),
            full(piece, HALF),
            pltpu.VMEM((row_count, D), f32),
            pltpu.VMEM((row_count, D), bf16),
            pltpu.VMEM((row_count, INNER), bf16),
            pltpu.VMEM((key_count, INNER), bf16),
            pltpu.VMEM((key_count, INNER), bf16),
            pltpu.VMEM((HEADS, row_count, key_count), f32),
            pltpu.VMEM((row_count, INNER), bf16),
            pltpu.VMEM((row_count, INNER), bf16),
            pltpu.VMEM((row_count, D), f32),
            pltpu.VMEM((row_count, D), bf16),
            pltpu.VMEM((row_count, INNER), bf16),
            pltpu.VMEM((key_count, INNER), f32),
            pltpu.VMEM((key_count, INNER), f32),
            pltpu.VMEM((row_count, D), f32),
            pltpu.VMEM((2, 2, halo_rows, INNER), bf16),
            pltpu.VMEM((2, 2, halo_rows, INNER), bf16),
            pltpu.VMEM((2, 2, halo_rows, INNER), bf16),
            pltpu.VMEM((fsdp, 2, 2, 2, piece, HEAD_OUT), f32),
            pltpu.VMEM((fsdp, 2, 2, piece, HEAD_OUT), f32),
            pltpu.VMEM((fsdp, 2, piece, HEAD_OUT), bf16),
            pltpu.VMEM((fsdp, 2, piece, HEAD_OUT), bf16),
            pltpu.VMEM((fsdp, 2, piece, HEAD_OUT), f32),
            pltpu.VMEM((fsdp, piece, HEAD_OUT), bf16),
            pltpu.VMEM((fsdp, piece, HEAD_OUT), bf16),
            pltpu.VMEM((fsdp, piece, HEAD_OUT), f32),
            pltpu.VMEM((fsdp, piece, HEAD_OUT), bf16),
            pltpu.VMEM((fsdp - 1, piece, HEAD_OUT), bf16),
            pltpu.VMEM((2, 2, 2, piece, HEAD_OUT), f32),
            pltpu.SemaphoreType.DMA((9,)),
            pltpu.SemaphoreType.DMA((7, 4, fsdp - 1)),
            pltpu.SemaphoreType.DMA((7, 4, fsdp - 1)),
            pltpu.SemaphoreType.DMA((4, 2)),
            pltpu.SemaphoreType.DMA((4, 2)),
            pltpu.SemaphoreType.DMA((5 + fsdp,)),
            pltpu.SemaphoreType.DMA((5 + fsdp,)),
        ],
        compiler_params=pltpu.CompilerParams(
            collective_id=0, has_side_effects=True, vmem_limit_bytes=56 * 1024 * 1024
        ),
        cost_estimate=pl.CostEstimate(
            flops=int(7e9), bytes_accessed=int(1e7), transcendentals=row_count * key_count * HEADS
        ),
    )(
        tokens,
        norm_gain.reshape(1, D),
        qkv.reshape(2, 2, 2, piece, qkv.shape[1]),
        out_weight.reshape(2, 2, out_piece, D),
        head_weight.reshape(2, 2, 2, piece, HEAD_OUT),
        grad_rows,
    )
    return head_out, grad_tokens, grad_head.reshape(8 * piece, HEAD_OUT)


def fine_residual(coarse, lat_rows, lon_cols):
    coarse_padded_grid = with_halo(coarse, (("tile", 2),), 1)
    lat_lower, lat_upper_weight = interp_weights(jnp.arange(4 * lat_rows, dtype=jnp.int32))
    latitude_matrix = build_matrix(
        jnp.clip(lat_lower, 0, lat_rows - 1),
        jnp.clip(lat_lower + 1, 0, lat_rows - 1),
        lat_upper_weight,
        lat_rows,
    )
    lon_lower, lon_upper_weight = interp_weights(jnp.arange(4 * lon_cols, dtype=jnp.int32))
    lon_matrix = build_matrix(lon_lower + 1, lon_lower + 2, lon_upper_weight, lon_cols + 2)
    incomplete_grid = jnp.einsum(
        "lj,kji->kli", latitude_matrix, coarse_padded_grid, precision=lax.Precision.HIGHEST
    )
    return jnp.einsum(
        "vrb,cb->vrc", incomplete_grid, lon_matrix, precision=lax.Precision.HIGHEST
    )


def fused_shards(
    tokens, norm_gain, query_key_value_weight, out_weight, head_weight, coarse, grad_fine
):
    lat_rows = tokens.shape[1]
    lon_cols = tokens.shape[2]
    row_count = lat_rows * lon_cols
    grad_rows = (
        grad_fine[0]
        .astype(jnp.bfloat16)
        .reshape(VARS, lat_rows, 4, lon_cols, 4)
        .transpose(1, 3, 0, 2, 4)
        .reshape(row_count, HEAD_OUT)
    )
    residual = fine_residual(coarse[0], lat_rows, lon_cols)
    head_out, grad_tokens, grad_head = fused_block(
        tokens[0].reshape(row_count, D),
        norm_gain,
        query_key_value_weight,
        out_weight,
        head_weight,
        grad_rows,
        lat_rows,
        lon_cols,
    )
    fine_head = (
        head_out.reshape(lat_rows, lon_cols, VARS, 4, 4)
        .transpose(2, 0, 3, 1, 4)
        .reshape(VARS, 4 * lat_rows, 4 * lon_cols)
    )
    fine_grid = fine_head + residual
    return (fine_grid[None], grad_tokens.reshape(1, lat_rows, lon_cols, D), grad_head)


def fits_pieces(mesh):
    dp, fsdp, tile = (mesh.shape[axis] for axis in ("dp", "fsdp", "tile"))
    if dp != 2 or tile != 4 or fsdp < 2:
        return False
    return D % (fsdp * 128) == 0 and INNER % (fsdp * 64) == 0


def shards(tokens, norm_gain, query_key_value_weight, out_weight, head_weight, coarse, grad_fine):
    lat_rows = tokens.shape[1]
    lon_cols = tokens.shape[2]
    row_count = lat_rows * lon_cols
    flattened_rows = tokens[0].reshape(row_count, D).astype(jnp.float32)
    standard, inverse_dev = layer_norm(flattened_rows)
    normed = (standard * norm_gain).astype(jnp.bfloat16)
    full_qkv = lax.all_gather(query_key_value_weight, "fsdp", axis=0, tiled=True)
    projected = jnp.dot(normed, full_qkv, preferred_element_type=jnp.float32).astype(jnp.bfloat16)
    queries = projected[:, :INNER]
    pairs_local = projected[:, INNER:]
    margin_pairs = with_halo(
        pairs_local.reshape(lat_rows, lon_cols, 2 * INNER), (("tile", 1),), MARGIN
    )
    keys_values = margin_pairs.reshape(lat_rows * (lon_cols + 2 * MARGIN), 2 * INNER)
    attended, softmax_out = attend_forward(queries, keys_values)
    full_out = lax.all_gather(out_weight, "fsdp", axis=0, tiled=True)
    mixed_out = jnp.dot(attended, full_out, preferred_element_type=jnp.float32)
    hidden = (flattened_rows + mixed_out).astype(jnp.bfloat16)
    full_head = lax.all_gather(head_weight, "fsdp", axis=0, tiled=True)
    head_out = jnp.dot(hidden, full_head, preferred_element_type=jnp.float32)
    fine_head = (
        head_out.reshape(lat_rows, lon_cols, VARS, 4, 4)
        .transpose(2, 0, 3, 1, 4)
        .reshape(VARS, 4 * lat_rows, 4 * lon_cols)
    )
    coarse_padded_grid = with_halo(coarse[0], (("tile", 2),), 1)
    lat_lower, lat_upper_weight = interp_weights(jnp.arange(4 * lat_rows, dtype=jnp.int32))
    latitude_matrix = build_matrix(
        jnp.clip(lat_lower, 0, lat_rows - 1),
        jnp.clip(lat_lower + 1, 0, lat_rows - 1),
        lat_upper_weight,
        lat_rows,
    )
    lon_lower, lon_upper_weight = interp_weights(jnp.arange(4 * lon_cols, dtype=jnp.int32))
    lon_matrix = build_matrix(lon_lower + 1, lon_lower + 2, lon_upper_weight, lon_cols + 2)
    incomplete_grid = jnp.einsum(
        "lj,kji->kli", latitude_matrix, coarse_padded_grid, precision=lax.Precision.HIGHEST
    )
    residual = jnp.einsum(
        "vrb,cb->vrc", incomplete_grid, lon_matrix, precision=lax.Precision.HIGHEST
    )
    fine_grid = fine_head + residual
    grad_rows = (
        grad_fine[0]
        .reshape(VARS, lat_rows, 4, lon_cols, 4)
        .transpose(1, 3, 0, 2, 4)
        .reshape(row_count, HEAD_OUT)
    )
    grad_rows = grad_rows.astype(jnp.bfloat16)
    head_term = lax.dot_general(
        hidden, grad_rows, (((0,), (0,)), ((), ())), preferred_element_type=jnp.float32
    )
    head_block = lax.psum_scatter(head_term, "fsdp", scatter_dimension=0, tiled=True)
    grad_head = lax.psum(head_block, ("dp", "tile"))
    grad_hidden = contract_last(grad_rows, full_head)
    grad_attended = contract_last(grad_hidden.astype(jnp.bfloat16), full_out).astype(jnp.bfloat16)
    grad_queries, pair_gradient_rows = attend_backward(
        softmax_out, queries, keys_values, grad_attended
    )
    pair_gradient_rows = pair_gradient_rows.reshape(lat_rows, lon_cols + 2 * MARGIN, 2 * INNER)
    from_left = from_behind(pair_gradient_rows[:, lon_cols + MARGIN :], "tile", 1)
    from_right = from_behind(pair_gradient_rows[:, :MARGIN], "tile", -1)
    own_cells = pair_gradient_rows[:, MARGIN : MARGIN + lon_cols]
    own_cells = own_cells + jnp.pad(from_left, ((0, 0), (0, lon_cols - MARGIN), (0, 0)))
    own_cells = own_cells + jnp.pad(from_right, ((0, 0), (lon_cols - MARGIN, 0), (0, 0)))
    grad_all = jnp.concatenate(
        [grad_queries, own_cells.reshape(row_count, 2 * INNER).astype(jnp.bfloat16)], axis=1
    )
    grad_normed = contract_last(grad_all, full_qkv)
    grad_input = grad_hidden + norm_backward(grad_normed, standard, inverse_dev, norm_gain)
    grad_tokens = grad_input.astype(jnp.bfloat16).reshape(1, lat_rows, lon_cols, D)
    return (fine_grid[None], grad_tokens, grad_head)


def solution(mesh):
    placed = (
        P(("dp", "fsdp"), None, "tile", None),
        P(),
        P("fsdp", None),
        P("fsdp", None),
        P("fsdp", None),
        P(("dp", "fsdp"), None, None, "tile"),
        P(("dp", "fsdp"), None, None, "tile"),
    )
    return jax.shard_map(
        fused_shards if fits_pieces(mesh) else shards,
        mesh=mesh,
        in_specs=placed,
        out_specs=(
            P(("dp", "fsdp"), None, None, "tile"),
            P(("dp", "fsdp"), None, "tile", None),
            P("fsdp", None),
        ),
        check_vma=False,
    )
```

```python
import functools

import jax
import jax.numpy as jnp
from jax import lax
from jax.experimental import pallas as pl
from jax.experimental.pallas import tpu as pltpu
from jax.sharding import PartitionSpec as P

D = 1536
HEADS = 8
HEAD_DIM = 96
VARS = 20
MARGIN = 8
INNER = 768
HEAD_OUT = 320


EPSILON = 1e-05


def with_halo(shard, sides, width):
    for axis, dim in sides:
        devices, length = (lax.axis_size(axis), shard.shape[dim])
        up = [(i, (i + 1) % devices) for i in range(devices)]
        down = [(j, i) for i, j in up]
        last = lax.slice_in_dim(shard, length - width, length, axis=dim)
        leading = lax.slice_in_dim(shard, 0, width, axis=dim)
        before = lax.ppermute(last, axis, up)
        after = lax.ppermute(leading, axis, down)
        shard = jnp.concatenate([before, shard, after], axis=dim)
    return shard


def from_behind(value, axis, steps):
    count = lax.axis_size(axis)
    pairs = [(source, (source + steps) % count) for source in range(count)]
    return lax.ppermute(value, axis, pairs)


def layer_norm(values):
    average = jnp.mean(values, axis=-1, keepdims=True)
    centred = values - average
    variance = jnp.mean(centred * centred, axis=-1, keepdims=True)
    inverse_dev = lax.rsqrt(variance + EPSILON)
    return (centred * inverse_dev, inverse_dev)


def norm_backward(grad_normed, standard, inverse_dev, norm_gain):
    grad_standard = grad_normed * norm_gain
    first_mean = jnp.mean(grad_standard, axis=-1, keepdims=True)
    second_mean = jnp.mean(grad_standard * standard, axis=-1, keepdims=True)
    return inverse_dev * (grad_standard - first_mean - standard * second_mean)


def attend_forward(queries, keys_values):
    query_count = queries.shape[0]
    key_count = keys_values.shape[0]
    score_scale = HEAD_DIM ** (-0.5)
    query_heads = queries.reshape(query_count, HEADS, HEAD_DIM)
    key_heads = keys_values[:, :INNER].reshape(key_count, HEADS, HEAD_DIM)
    value_heads = keys_values[:, INNER:].reshape(key_count, HEADS, HEAD_DIM)
    scores = (
        jnp.einsum("qhd,khd->hqk", query_heads, key_heads, preferred_element_type=jnp.float32)
        * score_scale
    )
    biggest = jnp.max(scores, axis=-1, keepdims=True)
    exponent = jnp.exp(scores - biggest)
    softmax_out = exponent / jnp.sum(exponent, axis=-1, keepdims=True)
    softmax_low = softmax_out.astype(jnp.bfloat16)
    attended = jnp.einsum(
        "hqk,khd->qhd", softmax_low, value_heads, preferred_element_type=jnp.float32
    )
    return (attended.astype(jnp.bfloat16).reshape(query_count, INNER), softmax_out)


def attend_backward(softmax_out, queries, keys_values, grad_attended):
    query_count = queries.shape[0]
    key_count = keys_values.shape[0]
    score_scale = HEAD_DIM ** (-0.5)
    query_heads = queries.reshape(query_count, HEADS, HEAD_DIM)
    key_heads = keys_values[:, :INNER].reshape(key_count, HEADS, HEAD_DIM)
    value_heads = keys_values[:, INNER:].reshape(key_count, HEADS, HEAD_DIM)
    grad_heads = grad_attended.reshape(query_count, HEADS, HEAD_DIM)
    softmax_low = softmax_out.astype(jnp.bfloat16)
    grad_values = jnp.einsum(
        "hqk,qhd->khd", softmax_low, grad_heads, preferred_element_type=jnp.float32
    )
    grad_weights = jnp.einsum(
        "qhd,khd->hqk", grad_heads, value_heads, preferred_element_type=jnp.float32
    )
    weighted = jnp.sum(softmax_out * grad_weights, axis=-1, keepdims=True)
    grad_scores = (softmax_out * (grad_weights - weighted)).astype(jnp.bfloat16)
    grad_queries = (
        jnp.einsum("hqk,khd->qhd", grad_scores, key_heads, preferred_element_type=jnp.float32)
        * score_scale
    )
    grad_keys = (
        jnp.einsum("hqk,qhd->khd", grad_scores, query_heads, preferred_element_type=jnp.float32)
        * score_scale
    )
    pair_gradient_rows = jnp.concatenate(
        [grad_keys.reshape(key_count, INNER), grad_values.reshape(key_count, INNER)], axis=1
    )
    return (grad_queries.astype(jnp.bfloat16).reshape(query_count, INNER), pair_gradient_rows)


def interp_weights(fine_index):
    coarse_cell = fine_index // 4
    phase_index = fine_index % 4
    lower_shift = (phase_index < 2).astype(jnp.int32)
    upper_weight = (2 * phase_index - 3 + 8 * lower_shift).astype(jnp.float32) / 8.0
    return (coarse_cell - lower_shift, upper_weight)


def build_matrix(lower_cell, upper_cell, upper_weight, count):
    columns = jnp.arange(count, dtype=jnp.int32)
    lower_part = jnp.where(
        columns[None, :] == lower_cell[:, None], 1.0 - upper_weight[:, None], 0.0
    )
    upper_portion = jnp.where(columns[None, :] == upper_cell[:, None], upper_weight[:, None], 0.0)
    return lower_part + upper_portion


def contract_last(left_side, right_side):
    return lax.dot_general(
        left_side, right_side, (((1,), (1,)), ((), ())), preferred_element_type=jnp.float32
    )


def dot_nt(left_side, right_side):
    return lax.dot_general(
        left_side, right_side, (((1,), (1,)), ((), ())), preferred_element_type=jnp.float32
    )


def dot_tn(left_side, right_side):
    return lax.dot_general(
        left_side, right_side, (((0,), (0,)), ((), ())), preferred_element_type=jnp.float32
    )


def dot_nn(left_side, right_side):
    return jnp.dot(left_side, right_side, preferred_element_type=jnp.float32)


OUT0, OUT1, HEAD = range(3)
KEY, VALUE, QUERY = range(3)
CHUNKS = 9
ROUTES = (0, 1, 0, 0, 1, 0, 1, 0, 1)
HALF = INNER // 2
GROUPS = 2
GROUP = HEADS // GROUPS
PADDED = 32


def split_dot(dot, left_side, right_side):
    first = left_side.astype(jnp.bfloat16)
    remainder = left_side - first.astype(jnp.float32)
    second = remainder.astype(jnp.bfloat16)
    third = (remainder - second.astype(jnp.float32)).astype(jnp.bfloat16)
    return dot(third, right_side) + dot(second, right_side) + dot(first, right_side)


def spread(rows, columns, where):
    row = lax.broadcasted_iota(jnp.int32, (rows, columns), 0)
    column = lax.broadcasted_iota(jnp.int32, (rows, columns), 1)
    return where(row, column)


def block_kernel(
    fsdp,
    lat_rows,
    lon_cols,
    tokens_ref,
    gain_ref,
    qkv_ref,
    out_ref,
    head_ref,
    coarse_ref,
    fine_grad_ref,
    fine_ref,
    grad_tokens_ref,
    grad_head_ref,
    w_out0,
    w_out1,
    w_head,
    w_key0,
    w_value0,
    w_query0,
    w_key1,
    w_value1,
    w_query1,
    standard_ref,
    normed_ref,
    q_ref,
    k_ref,
    v_ref,
    p_ref,
    att_ref,
    ga_ref,
    gh_ref,
    hidden_ref,
    gq_ref,
    gk_ref,
    gv_ref,
    gn_ref,
    rows_ref,
    shuffled_ref,
    residual_ref,
    coarse_pad,
    w_head_shuffled,
    halo_out,
    grad_halo_out,
    grad_halo_in,
    term_ref,
    rs0,
    snd1,
    rs1,
    acc1,
    snd2,
    rs2,
    acc2,
    rs3,
    full_grad,
    local_sem,
    w_send,
    w_recv,
    halo_send,
    halo_recv,
    coarse_send,
    coarse_recv,
    rs_send,
    rs_recv,
):
    row_count = lat_rows * lon_cols
    halo_rows = lat_rows * MARGIN
    fine_cols = 4 * lon_cols
    core = lax.axis_index("dp")
    me = lax.axis_index("fsdp")
    tile = lax.axis_index("tile")
    tiles = lax.axis_size("tile")
    ty, tx = tile // 2, tile % 2
    x_side = {"tile": tile + 1 - 2 * tx}
    y_side = {"tile": (tile + 2) % tiles}
    sibling = {"dp": 1 - core}
    right = {"tile": (tile + 1) % tiles}
    left = {"tile": (tile + tiles - 1) % tiles}
    weights = (w_out0, w_out1, w_head, w_key0, w_value0, w_query0, w_key1, w_value1, w_query1)
    depth = w_head.shape[1] * 4 * w_head.shape[4]
    bf16, f32 = jnp.bfloat16, jnp.float32

    def qkv_chunk(group, which):
        return 3 + 3 * group + which

    def qkv_columns(chunk):
        group, which = (chunk - 3) // 3, (chunk - 3) % 3
        return pl.ds({KEY: 1, VALUE: 2, QUERY: 0}[which] * INNER + group * HALF, HALF)

    def own_piece(chunk):
        if chunk == HEAD:
            return w_head.at[me, core, ty, tx]
        if chunk in (OUT0, OUT1):
            start = core * 2 * HALF + (chunk - OUT0) * HALF
            return out_ref.at[ty, tx, :, pl.ds(pl.multiple_of(start, 128), HALF)]
        return qkv_ref.at[core, ty, tx, :, qkv_columns(chunk)]

    def remote(src, dst, send, recv, device):
        return pltpu.make_async_remote_copy(
            src_ref=src,
            dst_ref=dst,
            send_sem=send,
            recv_sem=recv,
            device_id=device,
            device_id_type=pl.DeviceIdType.MESH,
        )

    def weight_copy(chunk, stage, k):
        full = weights[chunk]
        send, recv = w_send.at[chunk, stage, k - 1], w_recv.at[chunk, stage, k - 1]
        source = (me + fsdp - k) % fsdp
        if stage == 0:
            device = {"fsdp": (me + k) % fsdp}
            return remote(own_piece(chunk), full.at[me, core, ty, tx], send, recv, device)
        if stage == 1:
            part = full.at[source, core, ty, tx]
            device = x_side if ROUTES[chunk] == 0 else y_side
        elif stage == 2:
            if ROUTES[chunk] == 0:
                part, device = full.at[source, core, ty], y_side
            else:
                part, device = full.at[source, core, :, tx], x_side
        else:
            part, device = full.at[source, core], sibling
        return remote(part, part, send, recv, device)

    def advance(*steps):
        for chunk, stage in steps:
            for k in range(1, fsdp):
                if stage > 0:
                    weight_copy(chunk, stage - 1, k).wait_recv()
                if stage < 4:
                    weight_copy(chunk, stage, k).start()

    def local_copies():
        pairs = []
        for d in range(2):
            for half, full in enumerate((w_out0, w_out1)):
                start = d * 2 * HALF + half * HALF
                pairs.append((out_ref.at[:, :, :, pl.ds(start, HALF)], full.at[me, d]))
        for chunk in range(3, CHUNKS):
            pairs.append((qkv_ref.at[:, :, :, :, qkv_columns(chunk)], weights[chunk].at[me]))
        return [
            pltpu.make_async_copy(src, dst, local_sem.at[i]) for i, (src, dst) in enumerate(pairs)
        ]

    copies = local_copies()
    for copy in copies:
        copy.start()
    eye = spread(depth, depth, lambda r, c: (r == c).astype(f32)).astype(bf16)
    w_head[me] = dot_nt(eye, head_ref[...]).astype(bf16).reshape(w_head.shape[1:])
    coarse_pad[pl.ds(MARGIN, lon_cols), :] = coarse_ref[...]

    barrier = pltpu.get_barrier_semaphore()
    partners = [{"tile": (tile + i) % tiles} for i in range(1, 4)]
    partners += [{"fsdp": (me + i) % fsdp} for i in range(1, fsdp)]
    partners += [sibling]
    for partner in partners:
        pl.semaphore_signal(barrier, inc=1, device_id=partner, device_id_type=pl.DeviceIdType.MESH)
    pl.semaphore_wait(barrier, len(partners))

    advance(*[(chunk, 0) for chunk in range(CHUNKS)])
    coarse_copies = [
        remote(
            coarse_pad.at[pl.ds(lon_cols, MARGIN)],
            coarse_pad.at[pl.ds(0, MARGIN)],
            coarse_send.at[0],
            coarse_recv.at[0],
            right,
        ),
        remote(
            coarse_pad.at[pl.ds(MARGIN, MARGIN)],
            coarse_pad.at[pl.ds(MARGIN + lon_cols, MARGIN)],
            coarse_send.at[1],
            coarse_recv.at[1],
            left,
        ),
    ]
    for copy in coarse_copies:
        copy.start()

    scale = HEAD_DIM ** (-0.5)

    def normalised():
        return layer_norm(tokens_ref[...].astype(f32))

    standard, _ = normalised()
    standard_ref[...] = standard
    normed_ref[...] = (standard * gain_ref[...]).astype(bf16)

    advance((OUT0, 1), (OUT1, 1), (HEAD, 1))

    def cell_rows(i, a):
        return pl.ds((i * 4 + a) * PADDED, VARS)

    def fine_rows(i, a):
        return pl.ds(4 * i + a, VARS, stride=4 * lat_rows)

    shuffled_ref[...] = jnp.zeros_like(shuffled_ref)
    for i in range(lat_rows):
        for a in range(4):
            shuffled_ref[cell_rows(i, a), :] = fine_grad_ref[fine_rows(i, a), :]
    by_phase = spread(
        fine_cols, fine_cols, lambda r, c: (r == 4 * (c % lon_cols) + c // lon_cols).astype(f32)
    ).astype(bf16)
    to_phase = spread(
        fine_cols, fine_cols, lambda r, c: (c == 4 * (r % lon_cols) + r // lon_cols).astype(f32)
    ).astype(bf16)
    to_feature = spread(
        16 * PADDED,
        HEAD_OUT,
        lambda r, c: (
            c == 16 * (r % PADDED) + 4 * (r // PADDED % 4) + r // (4 * PADDED)
        ).astype(f32),
    ).astype(bf16)
    width = 4 * PADDED
    turned = dot_nn(shuffled_ref[...].astype(bf16), by_phase).T
    turned = jnp.concatenate(
        [
            jnp.concatenate(
                [
                    turned[b * lon_cols : (b + 1) * lon_cols, i * width : (i + 1) * width]
                    for b in range(4)
                ],
                axis=1,
            )
            for i in range(lat_rows)
        ],
        axis=0,
    )
    rows_ref[...] = dot_nn(turned.astype(bf16), to_feature).astype(bf16)

    advance((OUT0, 2), (OUT1, 2), (HEAD, 2))
    advance((3, 1), (4, 1))
    advance((OUT0, 3), (OUT1, 3), (HEAD, 3))
    advance((5, 1), (3, 2), (4, 2))
    for copy in copies:
        copy.wait()

    def columns_of(f):
        return pl.ds(pl.multiple_of(f * depth, 128), depth)

    advance((HEAD, 4))

    def grad_hidden_step(f, _):
        rows = w_head[f].reshape(depth, HEAD_OUT)
        gh_ref[:, columns_of(f)] = dot_nt(rows_ref[...], rows)
        w_head_shuffled[pl.ds(pl.multiple_of(f * depth, 128), depth), :] = dot_nt(
            rows, to_feature
        ).astype(bf16)
        return 0

    lax.fori_loop(0, fsdp, grad_hidden_step, 0)
    advance((6, 1), (5, 2), (3, 3), (4, 3))
    advance((OUT0, 4), (OUT1, 4))
    out_parts = [(d, half) for d in range(2) for half in range(2)]

    def out_block(d, half):
        full = (w_out0, w_out1)[half]
        return full[:, d].reshape(INNER, HALF)

    def out_columns(d, half):
        return pl.ds(d * 2 * HALF + half * HALF, HALF)

    grad_attended = jnp.zeros((row_count, INNER), f32)
    for d, half in out_parts:
        low = gh_ref[:, out_columns(d, half)].astype(bf16)
        grad_attended = grad_attended + dot_nt(low, out_block(d, half))
    ga_ref[...] = grad_attended.astype(bf16)

    advance((7, 1), (6, 2), (5, 3))

    for copy in coarse_copies:
        copy.wait_recv()

    def lon_weight(row, column):
        phase = column % 4
        lower_shift = (phase < 2).astype(jnp.int32)
        upper_weight = (2 * phase - 3 + 8 * lower_shift).astype(f32) / 8.0
        lower_cell = column // 4 - lower_shift + MARGIN
        return jnp.where(row == lower_cell, 1.0 - upper_weight, 0.0) + jnp.where(
            row == lower_cell + 1, upper_weight, 0.0
        )

    lon_matrix = spread(coarse_pad.shape[0], fine_cols, lon_weight).astype(bf16)
    incomplete = split_dot(dot_nn, coarse_pad[...].T, lon_matrix)
    for i in range(lat_rows):
        for a in range(4):
            low = i - 1 if a < 2 else i
            upper_weight = (5 / 8, 7 / 8, 1 / 8, 3 / 8)[a]
            lower, upper = (
                incomplete[cell * PADDED : (cell + 1) * PADDED]
                for cell in (max(low, 0), min(low + 1, lat_rows - 1))
            )
            residual_ref[pl.ds((i * 4 + a) * PADDED, PADDED), :] = (
                lower * (1.0 - upper_weight) + upper * upper_weight
            )

    def edge(rows, first):
        shaped = rows.reshape(lat_rows, lon_cols, rows.shape[-1])
        part = shaped[:, :MARGIN] if first else shaped[:, lon_cols - MARGIN :]
        return part.reshape(halo_rows, rows.shape[-1])

    def halo_copy(group, which, side):
        full = (k_ref, v_ref)[which]
        index = (0, group, which, side)
        return remote(
            halo_out.at[group, which, side],
            full.at[group, pl.ds(row_count + side * halo_rows, halo_rows)],
            halo_send.at[index],
            halo_recv.at[index],
            (right, left)[side],
        )

    def grad_halo_copy(group, which, side):
        index = (1, group, which, side)
        return remote(
            grad_halo_out.at[group, which, side],
            grad_halo_in.at[group, which, side],
            halo_send.at[index],
            halo_recv.at[index],
            (left, right)[side],
        )

    def project(group, which):
        full = weights[qkv_chunk(group, which)]
        product = dot_nn(normed_ref[...], full[...].reshape(-1, HALF))
        if which == QUERY:
            q_ref[group] = product.astype(bf16)
            return
        (k_ref, v_ref)[which][group, pl.ds(0, row_count)] = product.astype(bf16)
        for side in range(2):
            halo_out[group, which, side] = edge(product, side == 1).astype(bf16)
            halo_copy(group, which, side).start()

    def await_halos(group):
        for which in range(2):
            for side in range(2):
                halo_copy(group, which, side).wait_recv()

    def window(i):
        low, high = i * HEAD_DIM, (i + 1) * HEAD_DIM
        start, stop = low // 128 * 128, -(-high // 128) * 128
        lanes = lax.broadcasted_iota(jnp.int32, (1, stop - start), 1) + start
        return start, stop, ((lanes >= low) & (lanes < high)).astype(f32)

    def add_parts(parts, start, product):
        for j in range(product.shape[1] // 128):
            piece = product[:, j * 128 : (j + 1) * 128]
            at = start // 128 + j
            parts[at] = piece if parts[at] is None else parts[at] + piece

    def no_parts():
        return [None] * (HALF // 128)

    def forward(group, between=()):
        parts = no_parts()
        for i in range(GROUP):
            start, stop, mask = window(i)
            masked = q_ref[group, :, start:stop] * mask.astype(bf16)
            scores = dot_nt(masked, k_ref[group, :, start:stop]) * scale
            biggest = jnp.max(scores, axis=-1, keepdims=True)
            exponent = jnp.exp(scores - biggest)
            softmax = exponent / jnp.sum(exponent, axis=-1, keepdims=True)
            p_ref[group * GROUP + i] = softmax
            add_parts(parts, start, dot_nn(softmax.astype(bf16), v_ref[group, :, start:stop]) * mask)
            if i < len(between):
                between[i]()
        att_ref[:, pl.ds(group * HALF, HALF)] = jnp.concatenate(parts, axis=1).astype(bf16)

    def backward(group, between=()):
        query_parts, key_parts, value_parts = no_parts(), no_parts(), no_parts()
        for i in range(GROUP):
            start, stop, mask = window(i)
            softmax = p_ref[group * GROUP + i]
            grads = ga_ref[:, group * HALF + start : group * HALF + stop]
            weights_grad = dot_nt(grads * mask.astype(bf16), v_ref[group, :, start:stop])
            weighted = jnp.sum(softmax * weights_grad, axis=-1, keepdims=True)
            grad_scores = (softmax * (weights_grad - weighted)).astype(bf16)
            scaled = mask * scale
            add_parts(query_parts, start, dot_nn(grad_scores, k_ref[group, :, start:stop]) * scaled)
            add_parts(key_parts, start, dot_tn(grad_scores, q_ref[group, :, start:stop]) * scaled)
            add_parts(value_parts, start, dot_tn(softmax.astype(bf16), grads) * mask)
            if i < len(between):
                between[i]()
        gq_ref[group] = jnp.concatenate(query_parts, axis=1).astype(bf16)
        gk_ref[group] = jnp.concatenate(key_parts, axis=1)
        gv_ref[group] = jnp.concatenate(value_parts, axis=1)
        for which, full in enumerate((gk_ref, gv_ref)):
            for side in range(2):
                rows = full[group, pl.ds(row_count + side * halo_rows, halo_rows), :]
                grad_halo_out[group, which, side] = rows.astype(bf16)
                grad_halo_copy(group, which, side).start()

    def own_cells(group, which):
        full = (gk_ref, gv_ref)[which]
        for side in range(2):
            grad_halo_copy(group, which, side).wait_recv()
        rows = full[group, pl.ds(0, row_count), :].reshape(lat_rows, lon_cols, HALF)
        shape = (lat_rows, MARGIN, HALF)
        last = grad_halo_in[group, which, 0].astype(f32).reshape(shape)
        first = grad_halo_in[group, which, 1].astype(f32).reshape(shape)
        rows = jnp.concatenate(
            [
                rows[:, :MARGIN] + first,
                rows[:, MARGIN : lon_cols - MARGIN],
                rows[:, lon_cols - MARGIN :] + last,
            ],
            axis=1,
        )
        return rows.reshape(row_count, HALF).astype(bf16)

    def add_grad_normed(group, which, first=False):
        full = weights[qkv_chunk(group, which)]
        if which != QUERY:
            (k_ref, v_ref)[which][group, pl.ds(0, row_count)] = own_cells(group, which)

        def step(f, _):
            if which == QUERY:
                rows = gq_ref[group]
            else:
                rows = (k_ref, v_ref)[which][group, pl.ds(0, row_count)]
            product = dot_nt(rows, full[f].reshape(depth, HALF))
            if first:
                gn_ref[:, columns_of(f)] = product
            else:
                gn_ref[:, columns_of(f)] += product
            return 0

        lax.fori_loop(0, fsdp, step, 0)

    advance((3, 4))
    project(0, KEY)
    advance((8, 1), (7, 2), (6, 3), (4, 4))
    project(0, VALUE)
    advance((5, 4))
    project(0, QUERY)
    advance((8, 2), (7, 3))
    await_halos(0)
    forward(0, (lambda: None, lambda: advance((8, 3))))
    advance((6, 4))
    project(1, KEY)
    advance((7, 4))
    project(1, VALUE)
    backward(0)
    advance((8, 4))
    project(1, QUERY)
    await_halos(1)
    forward(1)
    for d, half in out_parts:
        columns = out_columns(d, half)
        mixed = dot_nn(att_ref[...], out_block(d, half))
        hidden_ref[:, columns] = (tokens_ref[:, columns].astype(f32) + mixed).astype(bf16)

    def term_step(f, _):
        term_ref[f] = dot_tn(rows_ref[...], hidden_ref[:, columns_of(f)]).reshape(
            term_ref.shape[1:]
        )
        return 0

    lax.fori_loop(0, fsdp, term_step, 0)

    core_copy = remote(term_ref.at[:, 1 - core], rs0, rs_send.at[0], rs_recv.at[0], sibling)
    y_copy = remote(snd1, rs1, rs_send.at[1], rs_recv.at[1], y_side)
    x_copy = remote(snd2, rs2, rs_send.at[2], rs_recv.at[2], x_side)
    z_copies = [
        remote(
            acc2.at[(me + k) % fsdp],
            rs3.at[k - 1],
            rs_send.at[5 + k],
            rs_recv.at[5 + k],
            {"fsdp": (me + k) % fsdp},
        )
        for k in range(1, fsdp)
    ]
    back_parts = [full_grad.at[core, ty, tx], full_grad.at[core, ty], full_grad.at[core]]
    back = [
        remote(part, part, rs_send.at[3 + i], rs_recv.at[3 + i], device)
        for i, (part, device) in enumerate(zip(back_parts, (x_side, y_side, sibling)))
    ]

    def reduce_y():
        core_copy.wait_recv()
        theirs = term_ref[:, core, 1 - ty] + rs0[:, 1 - ty]
        snd1[...] = theirs.reshape(snd1.shape).astype(bf16)
        y_copy.start()
        acc1[...] = term_ref[:, core, ty] + rs0[:, ty]

    def reduce_x():
        y_copy.wait_recv()
        acc1[...] = acc1[...] + rs1[...].astype(f32).reshape(acc1.shape)
        snd2[...] = acc1[:, 1 - tx]
        x_copy.start()

    def reduce_z():
        x_copy.wait_recv()
        acc2[...] = acc1[:, tx] + rs2[...]
        for copy in z_copies:
            copy.start()

    core_copy.start()
    backward(1, (lambda: None, reduce_y))
    add_grad_normed(0, QUERY, first=True)
    add_grad_normed(0, KEY)
    reduce_x()
    add_grad_normed(0, VALUE)
    add_grad_normed(1, QUERY)
    reduce_z()

    head_out = dot_nn(hidden_ref[...], w_head_shuffled[...])
    head_out = jnp.concatenate(
        [
            jnp.concatenate(
                [
                    head_out[i * lon_cols : (i + 1) * lon_cols, b * width : (b + 1) * width]
                    for b in range(4)
                ],
                axis=0,
            )
            for i in range(lat_rows)
        ],
        axis=1,
    )
    shuffled_ref[...] = split_dot(dot_nn, head_out.T, to_phase) + residual_ref[...]
    for i in range(lat_rows):
        for a in range(4):
            fine_ref[fine_rows(i, a), :] = shuffled_ref[cell_rows(i, a), :]

    for copy in z_copies:
        copy.wait_recv()
    summed = acc2[me]
    for k in range(1, fsdp):
        summed = summed + rs3[k - 1]
    full_grad[core, ty, tx] = summed
    back[0].start()
    add_grad_normed(1, KEY)
    back[0].wait_recv()
    back[1].start()
    add_grad_normed(1, VALUE)
    back[1].wait_recv()
    back[2].start()

    _, inverse_dev = normalised()
    grad_input = norm_backward(gn_ref[...], standard_ref[...], inverse_dev, gain_ref[...])
    grad_tokens_ref[...] = (gh_ref[...] + grad_input).astype(bf16)

    back[2].wait_recv()
    grad_head_ref[...] = full_grad[...]

    for chunk in range(CHUNKS):
        for stage in range(4):
            for k in range(1, fsdp):
                weight_copy(chunk, stage, k).wait_send()
    for group in range(GROUPS):
        for which in range(2):
            for side in range(2):
                halo_copy(group, which, side).wait_send()
                grad_halo_copy(group, which, side).wait_send()
    for copy in coarse_copies + [core_copy, y_copy, x_copy] + z_copies + back:
        copy.wait_send()


def fused_shards(
    tokens, norm_gain, query_key_value_weight, out_weight, head_weight, coarse, grad_fine
):
    fsdp = lax.axis_size("fsdp")
    lat_rows, lon_cols = tokens.shape[1:3]
    row_count = lat_rows * lon_cols
    halo_rows = lat_rows * MARGIN
    key_count = row_count + 2 * halo_rows
    depth, qkv_width = query_key_value_weight.shape
    piece = depth // 8
    out_piece = out_weight.shape[0] // 4
    head_piece = HEAD_OUT // 8
    bf16, f32 = jnp.bfloat16, jnp.float32
    vmem = pl.BlockSpec(memory_space=pltpu.VMEM)
    hbm = pl.BlockSpec(memory_space=pl.ANY)
    coarse_rows = jnp.pad(
        coarse[0].transpose(2, 1, 0), ((0, 0), (0, 0), (0, PADDED - VARS))
    ).reshape(lon_cols, lat_rows * PADDED)

    def full(rows, columns):
        return pltpu.VMEM((fsdp, 2, 2, 2, rows, columns), bf16)

    fine_rows = VARS * 4 * lat_rows
    shuffled = 4 * lat_rows * PADDED
    fine_grid, grad_tokens, grad_head = pl.pallas_call(
        functools.partial(block_kernel, fsdp, lat_rows, lon_cols),
        out_shape=(
            jax.ShapeDtypeStruct((fine_rows, 4 * lon_cols), f32),
            jax.ShapeDtypeStruct((row_count, D), bf16),
            jax.ShapeDtypeStruct((2, 2, 2, head_piece, depth), f32),
        ),
        in_specs=[vmem, vmem, hbm, hbm, vmem, vmem, vmem],
        out_specs=(vmem, vmem, vmem),
        scratch_shapes=[
            full(out_piece, HALF),
            full(out_piece, HALF),
            full(piece, HEAD_OUT),
        ]
        + [full(piece, HALF)] * 6
        + [
            pltpu.VMEM((row_count, D), f32),
            pltpu.VMEM((row_count, D), bf16),
            pltpu.VMEM((GROUPS, row_count, HALF), bf16),
            pltpu.VMEM((GROUPS, key_count, HALF), bf16),
            pltpu.VMEM((GROUPS, key_count, HALF), bf16),
            pltpu.VMEM((HEADS, row_count, key_count), f32),
            pltpu.VMEM((row_count, INNER), bf16),
            pltpu.VMEM((row_count, INNER), bf16),
            pltpu.VMEM((row_count, D), f32),
            pltpu.VMEM((row_count, D), bf16),
            pltpu.VMEM((GROUPS, row_count, HALF), bf16),
            pltpu.VMEM((GROUPS, key_count, HALF), f32),
            pltpu.VMEM((GROUPS, key_count, HALF), f32),
            pltpu.VMEM((row_count, D), f32),
            pltpu.VMEM((row_count, HEAD_OUT), bf16),
            pltpu.VMEM((shuffled, 4 * lon_cols), f32),
            pltpu.VMEM((shuffled, 4 * lon_cols), f32),
            pltpu.VMEM((lon_cols + 2 * MARGIN, lat_rows * PADDED), f32),
            pltpu.VMEM((D, 16 * PADDED), bf16),
            pltpu.VMEM((GROUPS, 2, 2, halo_rows, HALF), bf16),
            pltpu.VMEM((GROUPS, 2, 2, halo_rows, HALF), bf16),
            pltpu.VMEM((GROUPS, 2, 2, halo_rows, HALF), bf16),
            pltpu.VMEM((fsdp, 2, 2, 2, head_piece, depth), f32),
            pltpu.VMEM((fsdp, 2, 2, head_piece, depth), f32),
            pltpu.VMEM((fsdp, 2 * head_piece, depth), bf16),
            pltpu.VMEM((fsdp, 2 * head_piece, depth), bf16),
            pltpu.VMEM((fsdp, 2, head_piece, depth), f32),
            pltpu.VMEM((fsdp, head_piece, depth), f32),
            pltpu.VMEM((fsdp, head_piece, depth), f32),
            pltpu.VMEM((fsdp, head_piece, depth), f32),
            pltpu.VMEM((fsdp - 1, head_piece, depth), f32),
            pltpu.VMEM((2, 2, 2, head_piece, depth), f32),
            pltpu.SemaphoreType.DMA((10,)),
            pltpu.SemaphoreType.DMA((CHUNKS, 4, fsdp - 1)),
            pltpu.SemaphoreType.DMA((CHUNKS, 4, fsdp - 1)),
            pltpu.SemaphoreType.DMA((2, GROUPS, 2, 2)),
            pltpu.SemaphoreType.DMA((2, GROUPS, 2, 2)),
            pltpu.SemaphoreType.DMA((2,)),
            pltpu.SemaphoreType.DMA((2,)),
            pltpu.SemaphoreType.DMA((5 + fsdp,)),
            pltpu.SemaphoreType.DMA((5 + fsdp,)),
        ],
        compiler_params=pltpu.CompilerParams(
            collective_id=0, has_side_effects=True, vmem_limit_bytes=58 * 1024 * 1024
        ),
        cost_estimate=pl.CostEstimate(
            flops=int(7e9), bytes_accessed=int(1e7), transcendentals=row_count * key_count * HEADS
        ),
    )(
        tokens.reshape(row_count, D),
        norm_gain.reshape(1, D),
        query_key_value_weight.reshape(2, 2, 2, piece, qkv_width),
        out_weight.reshape(2, 2, out_piece, D),
        head_weight.T,
        coarse_rows,
        grad_fine.reshape(fine_rows, 4 * lon_cols),
    )
    return (
        fine_grid.reshape(grad_fine.shape),
        grad_tokens.reshape(tokens.shape),
        grad_head.reshape(HEAD_OUT, depth).T,
    )


def fits_pieces(tokens, qkv, out_weight):
    if lax.axis_size("dp") != 2 or lax.axis_size("tile") != 4 or lax.axis_size("fsdp") < 2:
        return False
    lat_rows, lon_cols = tokens.shape[1:3]
    if lat_rows % 2 or 4 * lon_cols != 128 or VARS > PADDED or 16 * VARS != HEAD_OUT:
        return False
    return qkv.shape[0] % 128 == 0 and out_weight.shape[0] % 64 == 0


def any_shards(*arguments):
    if fits_pieces(arguments[0], arguments[2], arguments[3]):
        return fused_shards(*arguments)
    return shards(*arguments)


def shards(tokens, norm_gain, query_key_value_weight, out_weight, head_weight, coarse, grad_fine):
    lat_rows = tokens.shape[1]
    lon_cols = tokens.shape[2]
    row_count = lat_rows * lon_cols
    flattened_rows = tokens[0].reshape(row_count, D).astype(jnp.float32)
    standard, inverse_dev = layer_norm(flattened_rows)
    normed = (standard * norm_gain).astype(jnp.bfloat16)
    full_qkv = lax.all_gather(query_key_value_weight, "fsdp", axis=0, tiled=True)
    projected = jnp.dot(normed, full_qkv, preferred_element_type=jnp.float32).astype(jnp.bfloat16)
    queries = projected[:, :INNER]
    pairs_local = projected[:, INNER:]
    margin_pairs = with_halo(
        pairs_local.reshape(lat_rows, lon_cols, 2 * INNER), (("tile", 1),), MARGIN
    )
    keys_values = margin_pairs.reshape(lat_rows * (lon_cols + 2 * MARGIN), 2 * INNER)
    attended, softmax_out = attend_forward(queries, keys_values)
    full_out = lax.all_gather(out_weight, "fsdp", axis=0, tiled=True)
    mixed_out = jnp.dot(attended, full_out, preferred_element_type=jnp.float32)
    hidden = (flattened_rows + mixed_out).astype(jnp.bfloat16)
    full_head = lax.all_gather(head_weight, "fsdp", axis=0, tiled=True)
    head_out = jnp.dot(hidden, full_head, preferred_element_type=jnp.float32)
    fine_head = (
        head_out.reshape(lat_rows, lon_cols, VARS, 4, 4)
        .transpose(2, 0, 3, 1, 4)
        .reshape(VARS, 4 * lat_rows, 4 * lon_cols)
    )
    coarse_padded_grid = with_halo(coarse[0], (("tile", 2),), 1)
    lat_lower, lat_upper_weight = interp_weights(jnp.arange(4 * lat_rows, dtype=jnp.int32))
    latitude_matrix = build_matrix(
        jnp.clip(lat_lower, 0, lat_rows - 1),
        jnp.clip(lat_lower + 1, 0, lat_rows - 1),
        lat_upper_weight,
        lat_rows,
    )
    lon_lower, lon_upper_weight = interp_weights(jnp.arange(4 * lon_cols, dtype=jnp.int32))
    lon_matrix = build_matrix(lon_lower + 1, lon_lower + 2, lon_upper_weight, lon_cols + 2)
    incomplete_grid = jnp.einsum(
        "lj,kji->kli", latitude_matrix, coarse_padded_grid, precision=lax.Precision.HIGHEST
    )
    residual = jnp.einsum(
        "vrb,cb->vrc", incomplete_grid, lon_matrix, precision=lax.Precision.HIGHEST
    )
    fine_grid = fine_head + residual
    grad_rows = (
        grad_fine[0]
        .reshape(VARS, lat_rows, 4, lon_cols, 4)
        .transpose(1, 3, 0, 2, 4)
        .reshape(row_count, HEAD_OUT)
    )
    grad_rows = grad_rows.astype(jnp.bfloat16)
    head_term = lax.dot_general(
        hidden, grad_rows, (((0,), (0,)), ((), ())), preferred_element_type=jnp.float32
    )
    head_block = lax.psum_scatter(head_term, "fsdp", scatter_dimension=0, tiled=True)
    grad_head = lax.psum(head_block, ("dp", "tile"))
    grad_hidden = contract_last(grad_rows, full_head)
    grad_attended = contract_last(grad_hidden.astype(jnp.bfloat16), full_out).astype(jnp.bfloat16)
    grad_queries, pair_gradient_rows = attend_backward(
        softmax_out, queries, keys_values, grad_attended
    )
    pair_gradient_rows = pair_gradient_rows.reshape(lat_rows, lon_cols + 2 * MARGIN, 2 * INNER)
    from_left = from_behind(pair_gradient_rows[:, lon_cols + MARGIN :], "tile", 1)
    from_right = from_behind(pair_gradient_rows[:, :MARGIN], "tile", -1)
    own_cells = pair_gradient_rows[:, MARGIN : MARGIN + lon_cols]
    own_cells = own_cells + jnp.pad(from_left, ((0, 0), (0, lon_cols - MARGIN), (0, 0)))
    own_cells = own_cells + jnp.pad(from_right, ((0, 0), (lon_cols - MARGIN, 0), (0, 0)))
    grad_all = jnp.concatenate(
        [grad_queries, own_cells.reshape(row_count, 2 * INNER).astype(jnp.bfloat16)], axis=1
    )
    grad_normed = contract_last(grad_all, full_qkv)
    grad_input = grad_hidden + norm_backward(grad_normed, standard, inverse_dev, norm_gain)
    grad_tokens = grad_input.astype(jnp.bfloat16).reshape(1, lat_rows, lon_cols, D)
    return (fine_grid[None], grad_tokens, grad_head)


def solution(mesh):
    placed = (
        P(("dp", "fsdp"), None, "tile", None),
        P(),
        P("fsdp", None),
        P("fsdp", None),
        P("fsdp", None),
        P(("dp", "fsdp"), None, None, "tile"),
        P(("dp", "fsdp"), None, None, "tile"),
    )
    return jax.shard_map(
        any_shards,
        mesh=mesh,
        in_specs=placed,
        out_specs=(
            P(("dp", "fsdp"), None, None, "tile"),
            P(("dp", "fsdp"), None, "tile", None),
            P("fsdp", None),
        ),
        check_vma=False,
    )
```

```python
import functools

import jax
import jax.numpy as jnp
from jax import lax
from jax.experimental import pallas as pl
from jax.experimental.pallas import tpu as pltpu
from jax.sharding import PartitionSpec as P

D = 1536
HEADS = 8
HEAD_DIM = 96
VARS = 20
MARGIN = 8
INNER = 768
HEAD_OUT = 320


EPSILON = 1e-05


def with_halo(shard, sides, width):
    for axis, dim in sides:
        devices, length = (lax.axis_size(axis), shard.shape[dim])
        up = [(i, (i + 1) % devices) for i in range(devices)]
        down = [(j, i) for i, j in up]
        last = lax.slice_in_dim(shard, length - width, length, axis=dim)
        leading = lax.slice_in_dim(shard, 0, width, axis=dim)
        before = lax.ppermute(last, axis, up)
        after = lax.ppermute(leading, axis, down)
        shard = jnp.concatenate([before, shard, after], axis=dim)
    return shard


def from_behind(value, axis, steps):
    count = lax.axis_size(axis)
    pairs = [(source, (source + steps) % count) for source in range(count)]
    return lax.ppermute(value, axis, pairs)


def layer_norm(values):
    average = jnp.mean(values, axis=-1, keepdims=True)
    centred = values - average
    variance = jnp.mean(centred * centred, axis=-1, keepdims=True)
    inverse_dev = lax.rsqrt(variance + EPSILON)
    return (centred * inverse_dev, inverse_dev)


def norm_backward(grad_normed, standard, inverse_dev, norm_gain):
    grad_standard = grad_normed * norm_gain
    first_mean = jnp.mean(grad_standard, axis=-1, keepdims=True)
    second_mean = jnp.mean(grad_standard * standard, axis=-1, keepdims=True)
    return inverse_dev * (grad_standard - first_mean - standard * second_mean)


def attend_forward(queries, keys_values):
    query_count = queries.shape[0]
    key_count = keys_values.shape[0]
    score_scale = HEAD_DIM ** (-0.5)
    query_heads = queries.reshape(query_count, HEADS, HEAD_DIM)
    key_heads = keys_values[:, :INNER].reshape(key_count, HEADS, HEAD_DIM)
    value_heads = keys_values[:, INNER:].reshape(key_count, HEADS, HEAD_DIM)
    scores = (
        jnp.einsum("qhd,khd->hqk", query_heads, key_heads, preferred_element_type=jnp.float32)
        * score_scale
    )
    biggest = jnp.max(scores, axis=-1, keepdims=True)
    exponent = jnp.exp(scores - biggest)
    softmax_out = exponent / jnp.sum(exponent, axis=-1, keepdims=True)
    softmax_low = softmax_out.astype(jnp.bfloat16)
    attended = jnp.einsum(
        "hqk,khd->qhd", softmax_low, value_heads, preferred_element_type=jnp.float32
    )
    return (attended.astype(jnp.bfloat16).reshape(query_count, INNER), softmax_out)


def attend_backward(softmax_out, queries, keys_values, grad_attended):
    query_count = queries.shape[0]
    key_count = keys_values.shape[0]
    score_scale = HEAD_DIM ** (-0.5)
    query_heads = queries.reshape(query_count, HEADS, HEAD_DIM)
    key_heads = keys_values[:, :INNER].reshape(key_count, HEADS, HEAD_DIM)
    value_heads = keys_values[:, INNER:].reshape(key_count, HEADS, HEAD_DIM)
    grad_heads = grad_attended.reshape(query_count, HEADS, HEAD_DIM)
    softmax_low = softmax_out.astype(jnp.bfloat16)
    grad_values = jnp.einsum(
        "hqk,qhd->khd", softmax_low, grad_heads, preferred_element_type=jnp.float32
    )
    grad_weights = jnp.einsum(
        "qhd,khd->hqk", grad_heads, value_heads, preferred_element_type=jnp.float32
    )
    weighted = jnp.sum(softmax_out * grad_weights, axis=-1, keepdims=True)
    grad_scores = (softmax_out * (grad_weights - weighted)).astype(jnp.bfloat16)
    grad_queries = (
        jnp.einsum("hqk,khd->qhd", grad_scores, key_heads, preferred_element_type=jnp.float32)
        * score_scale
    )
    grad_keys = (
        jnp.einsum("hqk,qhd->khd", grad_scores, query_heads, preferred_element_type=jnp.float32)
        * score_scale
    )
    pair_gradient_rows = jnp.concatenate(
        [grad_keys.reshape(key_count, INNER), grad_values.reshape(key_count, INNER)], axis=1
    )
    return (grad_queries.astype(jnp.bfloat16).reshape(query_count, INNER), pair_gradient_rows)


def interp_weights(fine_index):
    coarse_cell = fine_index // 4
    phase_index = fine_index % 4
    lower_shift = (phase_index < 2).astype(jnp.int32)
    upper_weight = (2 * phase_index - 3 + 8 * lower_shift).astype(jnp.float32) / 8.0
    return (coarse_cell - lower_shift, upper_weight)


def build_matrix(lower_cell, upper_cell, upper_weight, count):
    columns = jnp.arange(count, dtype=jnp.int32)
    lower_part = jnp.where(
        columns[None, :] == lower_cell[:, None], 1.0 - upper_weight[:, None], 0.0
    )
    upper_portion = jnp.where(columns[None, :] == upper_cell[:, None], upper_weight[:, None], 0.0)
    return lower_part + upper_portion


def contract_last(left_side, right_side):
    return lax.dot_general(
        left_side, right_side, (((1,), (1,)), ((), ())), preferred_element_type=jnp.float32
    )


def dot_nt(left_side, right_side):
    return lax.dot_general(
        left_side, right_side, (((1,), (1,)), ((), ())), preferred_element_type=jnp.float32
    )


def dot_tn(left_side, right_side):
    return lax.dot_general(
        left_side, right_side, (((0,), (0,)), ((), ())), preferred_element_type=jnp.float32
    )


def dot_nn(left_side, right_side):
    return jnp.dot(left_side, right_side, preferred_element_type=jnp.float32)


OUT0, OUT1, HEAD = range(3)
KEY, VALUE, QUERY = range(3)
CHUNKS = 9
ROUTES = (0, 1, 0, 0, 1, 0, 1, 0, 1)
HALF = INNER // 2
GROUPS = 2
GROUP = HEADS // GROUPS
PADDED = 32
WINDOW = 3


def split_dot(dot, left_side, right_side):
    first = left_side.astype(jnp.bfloat16)
    remainder = left_side - first.astype(jnp.float32)
    second = remainder.astype(jnp.bfloat16)
    third = (remainder - second.astype(jnp.float32)).astype(jnp.bfloat16)
    return dot(third, right_side) + dot(second, right_side) + dot(first, right_side)


def spread(rows, columns, where):
    row = lax.broadcasted_iota(jnp.int32, (rows, columns), 0)
    column = lax.broadcasted_iota(jnp.int32, (rows, columns), 1)
    return where(row, column)


def block_kernel(
    fsdp,
    lat_rows,
    lon_cols,
    tokens_ref,
    gain_ref,
    qkv_ref,
    out_ref,
    head_ref,
    coarse_ref,
    fine_grad_ref,
    fine_ref,
    grad_tokens_ref,
    grad_head_ref,
    w_out0,
    w_out1,
    w_head,
    w_key0,
    w_value0,
    w_query0,
    w_key1,
    w_value1,
    w_query1,
    standard_ref,
    normed_ref,
    q_ref,
    k_ref,
    v_ref,
    p_ref,
    att_ref,
    ga_ref,
    gh_ref,
    hidden_ref,
    gq_ref,
    gk_ref,
    gv_ref,
    gn_ref,
    rows_ref,
    shuffled_ref,
    residual_ref,
    coarse_pad,
    w_head_shuffled,
    halo_out,
    grad_halo_out,
    grad_halo_in,
    term_ref,
    rs0,
    snd1,
    rs1,
    acc1,
    snd2,
    rs2,
    acc2,
    rs3,
    full_grad,
    local_sem,
    w_send,
    w_recv,
    halo_send,
    halo_recv,
    coarse_send,
    coarse_recv,
    rs_send,
    rs_recv,
    back_send,
    back_recv,
):
    row_count = lat_rows * lon_cols
    halo_rows = lat_rows * MARGIN
    fine_cols = 4 * lon_cols
    core = lax.axis_index("dp")
    me = lax.axis_index("fsdp")
    tile = lax.axis_index("tile")
    tiles = lax.axis_size("tile")
    ty, tx = tile // 2, tile % 2
    x_side = {"tile": tile + 1 - 2 * tx}
    y_side = {"tile": (tile + 2) % tiles}
    sibling = {"dp": 1 - core}
    right = {"tile": (tile + 1) % tiles}
    left = {"tile": (tile + tiles - 1) % tiles}
    weights = (w_out0, w_out1, w_head, w_key0, w_value0, w_query0, w_key1, w_value1, w_query1)
    depth = w_head.shape[1] * 4 * w_head.shape[4]
    bf16, f32 = jnp.bfloat16, jnp.float32

    def qkv_chunk(group, which):
        return 3 + 3 * group + which

    def qkv_columns(chunk):
        group, which = (chunk - 3) // 3, (chunk - 3) % 3
        return pl.ds({KEY: 1, VALUE: 2, QUERY: 0}[which] * INNER + group * HALF, HALF)

    def own_piece(chunk):
        if chunk == HEAD:
            return w_head.at[me, core, ty, tx]
        if chunk in (OUT0, OUT1):
            start = core * 2 * HALF + (chunk - OUT0) * HALF
            return out_ref.at[ty, tx, :, pl.ds(pl.multiple_of(start, 128), HALF)]
        return qkv_ref.at[core, ty, tx, :, qkv_columns(chunk)]

    def remote(src, dst, send, recv, device):
        return pltpu.make_async_remote_copy(
            src_ref=src,
            dst_ref=dst,
            send_sem=send,
            recv_sem=recv,
            device_id=device,
            device_id_type=pl.DeviceIdType.MESH,
        )

    def weight_copy(chunk, stage, k):
        full = weights[chunk]
        send, recv = w_send.at[chunk, stage, k - 1], w_recv.at[chunk, stage, k - 1]
        source = (me + fsdp - k) % fsdp
        if stage == 0:
            device = {"fsdp": (me + k) % fsdp}
            return remote(own_piece(chunk), full.at[me, core, ty, tx], send, recv, device)
        if stage == 1:
            part = full.at[source, core, ty, tx]
            device = x_side if ROUTES[chunk] == 0 else y_side
        elif stage == 2:
            if ROUTES[chunk] == 0:
                part, device = full.at[source, core, ty], y_side
            else:
                part, device = full.at[source, core, :, tx], x_side
        else:
            part, device = full.at[source, core], sibling
        return remote(part, part, send, recv, device)

    def advance(*steps):
        for chunk, stage in steps:
            for k in range(1, fsdp):
                if stage > 0:
                    weight_copy(chunk, stage - 1, k).wait_recv()
                if stage < 4:
                    weight_copy(chunk, stage, k).start()
            if stage == 1 and chunk + WINDOW < CHUNKS:
                advance((chunk + WINDOW, 0))

    def local_copies():
        pairs = []
        for d in range(2):
            for half, full in enumerate((w_out0, w_out1)):
                start = d * 2 * HALF + half * HALF
                pairs.append((out_ref.at[:, :, :, pl.ds(start, HALF)], full.at[me, d]))
        for chunk in range(3, CHUNKS):
            pairs.append((qkv_ref.at[:, :, :, :, qkv_columns(chunk)], weights[chunk].at[me]))
        return [
            pltpu.make_async_copy(src, dst, local_sem.at[i]) for i, (src, dst) in enumerate(pairs)
        ]

    copies = local_copies()
    for copy in copies:
        copy.start()
    coarse_pad[pl.ds(MARGIN, lon_cols), :] = coarse_ref[...]

    barrier = pltpu.get_barrier_semaphore()
    partners = [{"tile": (tile + i) % tiles} for i in range(1, 4)]
    partners += [{"fsdp": (me + i) % fsdp} for i in range(1, fsdp)]
    partners += [sibling]
    for partner in partners:
        pl.semaphore_signal(barrier, inc=1, device_id=partner, device_id_type=pl.DeviceIdType.MESH)
    pl.semaphore_wait(barrier, len(partners))

    advance((OUT0, 0), (OUT1, 0))
    eye = spread(depth, depth, lambda r, c: (r == c).astype(f32)).astype(bf16)
    w_head[me] = dot_nt(eye, head_ref[...]).astype(bf16).reshape(w_head.shape[1:])
    advance((HEAD, 0))
    coarse_copies = [
        remote(
            coarse_pad.at[pl.ds(lon_cols, MARGIN)],
            coarse_pad.at[pl.ds(0, MARGIN)],
            coarse_send.at[0],
            coarse_recv.at[0],
            right,
        ),
        remote(
            coarse_pad.at[pl.ds(MARGIN, MARGIN)],
            coarse_pad.at[pl.ds(MARGIN + lon_cols, MARGIN)],
            coarse_send.at[1],
            coarse_recv.at[1],
            left,
        ),
    ]
    for copy in coarse_copies:
        copy.start()

    scale = HEAD_DIM ** (-0.5)

    def normalised():
        return layer_norm(tokens_ref[...].astype(f32))

    standard, _ = normalised()
    standard_ref[...] = standard
    normed_ref[...] = (standard * gain_ref[...]).astype(bf16)

    advance((0, 1))

    def cell_rows(i, a):
        return pl.ds((i * 4 + a) * PADDED, VARS)

    def fine_rows(i, a):
        return pl.ds(4 * i + a, VARS, stride=4 * lat_rows)

    shuffled_ref[...] = jnp.zeros_like(shuffled_ref)
    for i in range(lat_rows):
        for a in range(4):
            shuffled_ref[cell_rows(i, a), :] = fine_grad_ref[fine_rows(i, a), :]
    by_phase = spread(
        fine_cols, fine_cols, lambda r, c: (r == 4 * (c % lon_cols) + c // lon_cols).astype(f32)
    ).astype(bf16)
    to_phase = spread(
        fine_cols, fine_cols, lambda r, c: (c == 4 * (r % lon_cols) + r // lon_cols).astype(f32)
    ).astype(bf16)
    to_feature = spread(
        16 * PADDED,
        HEAD_OUT,
        lambda r, c: (
            c == 16 * (r % PADDED) + 4 * (r // PADDED % 4) + r // (4 * PADDED)
        ).astype(f32),
    ).astype(bf16)
    width = 4 * PADDED
    turned = dot_nn(shuffled_ref[...].astype(bf16), by_phase).T
    turned = jnp.concatenate(
        [
            jnp.concatenate(
                [
                    turned[b * lon_cols : (b + 1) * lon_cols, i * width : (i + 1) * width]
                    for b in range(4)
                ],
                axis=1,
            )
            for i in range(lat_rows)
        ],
        axis=0,
    )
    rows_ref[...] = dot_nn(turned.astype(bf16), to_feature).astype(bf16)

    advance((1, 1), (0, 2), (2, 1), (1, 2), (0, 3), (3, 1), (2, 2))
    for copy in copies:
        copy.wait()

    for copy in coarse_copies:
        copy.wait_recv()

    def lon_weight(row, column):
        phase = column % 4
        lower_shift = (phase < 2).astype(jnp.int32)
        upper_weight = (2 * phase - 3 + 8 * lower_shift).astype(f32) / 8.0
        lower_cell = column // 4 - lower_shift + MARGIN
        return jnp.where(row == lower_cell, 1.0 - upper_weight, 0.0) + jnp.where(
            row == lower_cell + 1, upper_weight, 0.0
        )

    lon_matrix = spread(coarse_pad.shape[0], fine_cols, lon_weight).astype(bf16)
    incomplete = split_dot(dot_nn, coarse_pad[...].T, lon_matrix)
    for i in range(lat_rows):
        for a in range(4):
            low = i - 1 if a < 2 else i
            upper_weight = (5 / 8, 7 / 8, 1 / 8, 3 / 8)[a]
            lower, upper = (
                incomplete[cell * PADDED : (cell + 1) * PADDED]
                for cell in (max(low, 0), min(low + 1, lat_rows - 1))
            )
            residual_ref[pl.ds((i * 4 + a) * PADDED, PADDED), :] = (
                lower * (1.0 - upper_weight) + upper * upper_weight
            )

    advance((0, 4), (1, 3), (4, 1), (3, 2), (1, 4), (2, 3), (5, 1), (4, 2))

    def columns_of(f):
        return pl.ds(pl.multiple_of(f * depth, 128), depth)

    advance((2, 4))

    def grad_hidden_step(f, _):
        rows = w_head[f].reshape(depth, HEAD_OUT)
        gh_ref[:, columns_of(f)] = dot_nt(rows_ref[...], rows)
        w_head_shuffled[pl.ds(pl.multiple_of(f * depth, 128), depth), :] = dot_nt(
            rows, to_feature
        ).astype(bf16)
        return 0

    lax.fori_loop(0, fsdp, grad_hidden_step, 0)
    advance((3, 3), (6, 1), (5, 2))
    out_parts = [(d, half) for d in range(2) for half in range(2)]

    def out_block(d, half):
        full = (w_out0, w_out1)[half]
        return full[:, d].reshape(INNER, HALF)

    def out_columns(d, half):
        return pl.ds(d * 2 * HALF + half * HALF, HALF)

    grad_attended = jnp.zeros((row_count, INNER), f32)
    for d, half in out_parts:
        low = gh_ref[:, out_columns(d, half)].astype(bf16)
        grad_attended = grad_attended + dot_nt(low, out_block(d, half))
    ga_ref[...] = grad_attended.astype(bf16)

    advance((4, 3), (7, 1), (6, 2))

    def edge(rows, first):
        shaped = rows.reshape(lat_rows, lon_cols, rows.shape[-1])
        part = shaped[:, :MARGIN] if first else shaped[:, lon_cols - MARGIN :]
        return part.reshape(halo_rows, rows.shape[-1])

    def halo_copy(group, which, side):
        full = (k_ref, v_ref)[which]
        index = (0, group, which, side)
        return remote(
            halo_out.at[group, which, side],
            full.at[group, pl.ds(row_count + side * halo_rows, halo_rows)],
            halo_send.at[index],
            halo_recv.at[index],
            (right, left)[side],
        )

    def grad_halo_copy(group, which, side):
        index = (1, group, which, side)
        return remote(
            grad_halo_out.at[group, which, side],
            grad_halo_in.at[group, which, side],
            halo_send.at[index],
            halo_recv.at[index],
            (left, right)[side],
        )

    def project(group, which):
        full = weights[qkv_chunk(group, which)]
        product = dot_nn(normed_ref[...], full[...].reshape(-1, HALF))
        if which == QUERY:
            q_ref[group] = product.astype(bf16)
            return
        (k_ref, v_ref)[which][group, pl.ds(0, row_count)] = product.astype(bf16)
        for side in range(2):
            halo_out[group, which, side] = edge(product, side == 1).astype(bf16)
            halo_copy(group, which, side).start()

    def await_halos(group):
        for which in range(2):
            for side in range(2):
                halo_copy(group, which, side).wait_recv()

    def window(i):
        low, high = i * HEAD_DIM, (i + 1) * HEAD_DIM
        start, stop = low // 128 * 128, -(-high // 128) * 128
        lanes = lax.broadcasted_iota(jnp.int32, (1, stop - start), 1) + start
        return start, stop, ((lanes >= low) & (lanes < high)).astype(f32)

    def add_parts(parts, start, product):
        for j in range(product.shape[1] // 128):
            piece = product[:, j * 128 : (j + 1) * 128]
            at = start // 128 + j
            parts[at] = piece if parts[at] is None else parts[at] + piece

    def no_parts():
        return [None] * (HALF // 128)

    def forward(group, between=()):
        parts = no_parts()
        for i in range(GROUP):
            start, stop, mask = window(i)
            masked = q_ref[group, :, start:stop] * mask.astype(bf16)
            scores = dot_nt(masked, k_ref[group, :, start:stop]) * scale
            biggest = jnp.max(scores, axis=-1, keepdims=True)
            exponent = jnp.exp(scores - biggest)
            softmax = exponent / jnp.sum(exponent, axis=-1, keepdims=True)
            p_ref[group * GROUP + i] = softmax
            add_parts(parts, start, dot_nn(softmax.astype(bf16), v_ref[group, :, start:stop]) * mask)
            if i < len(between):
                between[i]()
        att_ref[:, pl.ds(group * HALF, HALF)] = jnp.concatenate(parts, axis=1).astype(bf16)

    def backward(group, between=()):
        query_parts, key_parts, value_parts = no_parts(), no_parts(), no_parts()
        for i in range(GROUP):
            start, stop, mask = window(i)
            softmax = p_ref[group * GROUP + i]
            grads = ga_ref[:, group * HALF + start : group * HALF + stop]
            weights_grad = dot_nt(grads * mask.astype(bf16), v_ref[group, :, start:stop])
            weighted = jnp.sum(softmax * weights_grad, axis=-1, keepdims=True)
            grad_scores = (softmax * (weights_grad - weighted)).astype(bf16)
            scaled = mask * scale
            add_parts(query_parts, start, dot_nn(grad_scores, k_ref[group, :, start:stop]) * scaled)
            add_parts(key_parts, start, dot_tn(grad_scores, q_ref[group, :, start:stop]) * scaled)
            add_parts(value_parts, start, dot_tn(softmax.astype(bf16), grads) * mask)
            if i < len(between):
                between[i]()
        gq_ref[group] = jnp.concatenate(query_parts, axis=1).astype(bf16)
        gk_ref[group] = jnp.concatenate(key_parts, axis=1)
        gv_ref[group] = jnp.concatenate(value_parts, axis=1)
        for which, full in enumerate((gk_ref, gv_ref)):
            for side in range(2):
                rows = full[group, pl.ds(row_count + side * halo_rows, halo_rows), :]
                grad_halo_out[group, which, side] = rows.astype(bf16)
                grad_halo_copy(group, which, side).start()

    def own_cells(group, which):
        full = (gk_ref, gv_ref)[which]
        for side in range(2):
            grad_halo_copy(group, which, side).wait_recv()
        rows = full[group, pl.ds(0, row_count), :].reshape(lat_rows, lon_cols, HALF)
        shape = (lat_rows, MARGIN, HALF)
        last = grad_halo_in[group, which, 0].astype(f32).reshape(shape)
        first = grad_halo_in[group, which, 1].astype(f32).reshape(shape)
        rows = jnp.concatenate(
            [
                rows[:, :MARGIN] + first,
                rows[:, MARGIN : lon_cols - MARGIN],
                rows[:, lon_cols - MARGIN :] + last,
            ],
            axis=1,
        )
        return rows.reshape(row_count, HALF).astype(bf16)

    def add_grad_normed(group, which, first=False):
        full = weights[qkv_chunk(group, which)]
        if which != QUERY:
            (k_ref, v_ref)[which][group, pl.ds(0, row_count)] = own_cells(group, which)

        def step(f, _):
            if which == QUERY:
                rows = gq_ref[group]
            else:
                rows = (k_ref, v_ref)[which][group, pl.ds(0, row_count)]
            product = dot_nt(rows, full[f].reshape(depth, HALF))
            if first:
                gn_ref[:, columns_of(f)] = product
            else:
                gn_ref[:, columns_of(f)] += product
            return 0

        lax.fori_loop(0, fsdp, step, 0)

    advance((3, 4))
    project(0, KEY)
    advance((4, 4))
    project(0, VALUE)
    advance((5, 3), (8, 1), (7, 2), (5, 4))
    project(0, QUERY)
    advance((6, 3))
    await_halos(0)
    forward(0, (lambda: None, lambda: advance((8, 2)), lambda: advance((7, 3))))
    advance((6, 4))
    project(1, KEY)

    def next_values():
        advance((7, 4))
        project(1, VALUE)

    backward(0, (lambda: advance((8, 3)), next_values))
    advance((8, 4))
    project(1, QUERY)
    for chunk in range(CHUNKS):
        for stage in range(4):
            for k in range(1, fsdp):
                weight_copy(chunk, stage, k).wait_send()
    await_halos(1)
    forward(1)
    for d, half in out_parts:
        columns = out_columns(d, half)
        mixed = dot_nn(att_ref[...], out_block(d, half))
        hidden_ref[:, columns] = (tokens_ref[:, columns].astype(f32) + mixed).astype(bf16)

    def term_step(f, _):
        term_ref[f] = dot_tn(rows_ref[...], hidden_ref[:, columns_of(f)]).reshape(
            term_ref.shape[1:]
        )
        return 0

    lax.fori_loop(0, fsdp, term_step, 0)

    core_copy = remote(term_ref.at[:, 1 - core], rs0, rs_send.at[0], rs_recv.at[0], sibling)
    y_copy = remote(snd1, rs1, rs_send.at[1], rs_recv.at[1], y_side)
    x_copy = remote(snd2, rs2, rs_send.at[2], rs_recv.at[2], x_side)
    z_copies = [
        remote(
            acc2.at[(me + k) % fsdp],
            rs3.at[k - 1],
            rs_send.at[5 + k],
            rs_recv.at[5 + k],
            {"fsdp": (me + k) % fsdp},
        )
        for k in range(1, fsdp)
    ]
    mine = full_grad.at[core, ty, tx]
    back = [
        remote(
            mine,
            mine,
            back_send.at[i - 1],
            back_recv.at[i - 1],
            {"tile": (tile + i) % tiles},
        )
        for i in range(1, 4)
    ]
    last_back = remote(
        full_grad.at[core], full_grad.at[core], rs_send.at[3], rs_recv.at[3], sibling
    )

    def reduce_y():
        core_copy.wait_recv()
        theirs = term_ref[:, core, 1 - ty] + rs0[:, 1 - ty]
        snd1[...] = theirs.reshape(snd1.shape).astype(bf16)
        y_copy.start()
        acc1[...] = term_ref[:, core, ty] + rs0[:, ty]

    def reduce_x():
        y_copy.wait_recv()
        acc1[...] = acc1[...] + rs1[...].astype(f32).reshape(acc1.shape)
        snd2[...] = acc1[:, 1 - tx]
        x_copy.start()

    def reduce_z():
        x_copy.wait_recv()
        acc2[...] = acc1[:, tx] + rs2[...]
        for copy in z_copies:
            copy.start()

    core_copy.start()
    backward(1, (lambda: None, reduce_y))
    add_grad_normed(0, QUERY, first=True)
    add_grad_normed(0, KEY)
    reduce_x()
    add_grad_normed(0, VALUE)
    add_grad_normed(1, QUERY)
    reduce_z()

    head_out = dot_nn(hidden_ref[...], w_head_shuffled[...])
    head_out = jnp.concatenate(
        [
            jnp.concatenate(
                [
                    head_out[i * lon_cols : (i + 1) * lon_cols, b * width : (b + 1) * width]
                    for b in range(4)
                ],
                axis=0,
            )
            for i in range(lat_rows)
        ],
        axis=1,
    )
    shuffled_ref[...] = split_dot(dot_nn, head_out.T, to_phase) + residual_ref[...]
    for i in range(lat_rows):
        for a in range(4):
            fine_ref[fine_rows(i, a), :] = shuffled_ref[cell_rows(i, a), :]

    for copy in z_copies:
        copy.wait_recv()
    summed = acc2[me]
    for k in range(1, fsdp):
        summed = summed + rs3[k - 1]
    full_grad[core, ty, tx] = summed
    for copy in back:
        copy.start()
    add_grad_normed(1, KEY)
    add_grad_normed(1, VALUE)
    for copy in back:
        copy.wait_recv()
    last_back.start()

    _, inverse_dev = normalised()
    grad_input = norm_backward(gn_ref[...], standard_ref[...], inverse_dev, gain_ref[...])
    grad_tokens_ref[...] = (gh_ref[...] + grad_input).astype(bf16)

    last_back.wait_recv()
    grad_head_ref[...] = full_grad[...]

    for group in range(GROUPS):
        for which in range(2):
            for side in range(2):
                halo_copy(group, which, side).wait_send()
                grad_halo_copy(group, which, side).wait_send()
    for copy in coarse_copies + [core_copy, y_copy, x_copy, last_back] + z_copies + back:
        copy.wait_send()


def fused_shards(
    tokens, norm_gain, query_key_value_weight, out_weight, head_weight, coarse, grad_fine
):
    fsdp = lax.axis_size("fsdp")
    lat_rows, lon_cols = tokens.shape[1:3]
    row_count = lat_rows * lon_cols
    halo_rows = lat_rows * MARGIN
    key_count = row_count + 2 * halo_rows
    depth, qkv_width = query_key_value_weight.shape
    piece = depth // 8
    out_piece = out_weight.shape[0] // 4
    head_piece = HEAD_OUT // 8
    bf16, f32 = jnp.bfloat16, jnp.float32
    vmem = pl.BlockSpec(memory_space=pltpu.VMEM)
    hbm = pl.BlockSpec(memory_space=pl.ANY)
    coarse_rows = jnp.pad(
        coarse[0].transpose(2, 1, 0), ((0, 0), (0, 0), (0, PADDED - VARS))
    ).reshape(lon_cols, lat_rows * PADDED)

    def full(rows, columns):
        return pltpu.VMEM((fsdp, 2, 2, 2, rows, columns), bf16)

    fine_rows = VARS * 4 * lat_rows
    shuffled = 4 * lat_rows * PADDED
    fine_grid, grad_tokens, grad_head = pl.pallas_call(
        functools.partial(block_kernel, fsdp, lat_rows, lon_cols),
        out_shape=(
            jax.ShapeDtypeStruct((fine_rows, 4 * lon_cols), f32),
            jax.ShapeDtypeStruct((row_count, D), bf16),
            jax.ShapeDtypeStruct((2, 2, 2, head_piece, depth), f32),
        ),
        in_specs=[vmem, vmem, hbm, hbm, vmem, vmem, vmem],
        out_specs=(vmem, vmem, vmem),
        scratch_shapes=[
            full(out_piece, HALF),
            full(out_piece, HALF),
            full(piece, HEAD_OUT),
        ]
        + [full(piece, HALF)] * 6
        + [
            pltpu.VMEM((row_count, D), f32),
            pltpu.VMEM((row_count, D), bf16),
            pltpu.VMEM((GROUPS, row_count, HALF), bf16),
            pltpu.VMEM((GROUPS, key_count, HALF), bf16),
            pltpu.VMEM((GROUPS, key_count, HALF), bf16),
            pltpu.VMEM((HEADS, row_count, key_count), f32),
            pltpu.VMEM((row_count, INNER), bf16),
            pltpu.VMEM((row_count, INNER), bf16),
            pltpu.VMEM((row_count, D), f32),
            pltpu.VMEM((row_count, D), bf16),
            pltpu.VMEM((GROUPS, row_count, HALF), bf16),
            pltpu.VMEM((GROUPS, key_count, HALF), f32),
            pltpu.VMEM((GROUPS, key_count, HALF), f32),
            pltpu.VMEM((row_count, D), f32),
            pltpu.VMEM((row_count, HEAD_OUT), bf16),
            pltpu.VMEM((shuffled, 4 * lon_cols), f32),
            pltpu.VMEM((shuffled, 4 * lon_cols), f32),
            pltpu.VMEM((lon_cols + 2 * MARGIN, lat_rows * PADDED), f32),
            pltpu.VMEM((D, 16 * PADDED), bf16),
            pltpu.VMEM((GROUPS, 2, 2, halo_rows, HALF), bf16),
            pltpu.VMEM((GROUPS, 2, 2, halo_rows, HALF), bf16),
            pltpu.VMEM((GROUPS, 2, 2, halo_rows, HALF), bf16),
            pltpu.VMEM((fsdp, 2, 2, 2, head_piece, depth), f32),
            pltpu.VMEM((fsdp, 2, 2, head_piece, depth), f32),
            pltpu.VMEM((fsdp, 2 * head_piece, depth), bf16),
            pltpu.VMEM((fsdp, 2 * head_piece, depth), bf16),
            pltpu.VMEM((fsdp, 2, head_piece, depth), f32),
            pltpu.VMEM((fsdp, head_piece, depth), f32),
            pltpu.VMEM((fsdp, head_piece, depth), f32),
            pltpu.VMEM((fsdp, head_piece, depth), f32),
            pltpu.VMEM((fsdp - 1, head_piece, depth), f32),
            pltpu.VMEM((2, 2, 2, head_piece, depth), f32),
            pltpu.SemaphoreType.DMA((10,)),
            pltpu.SemaphoreType.DMA((CHUNKS, 4, fsdp - 1)),
            pltpu.SemaphoreType.DMA((CHUNKS, 4, fsdp - 1)),
            pltpu.SemaphoreType.DMA((2, GROUPS, 2, 2)),
            pltpu.SemaphoreType.DMA((2, GROUPS, 2, 2)),
            pltpu.SemaphoreType.DMA((2,)),
            pltpu.SemaphoreType.DMA((2,)),
            pltpu.SemaphoreType.DMA((5 + fsdp,)),
            pltpu.SemaphoreType.DMA((5 + fsdp,)),
            pltpu.SemaphoreType.DMA((3,)),
            pltpu.SemaphoreType.DMA((3,)),
        ],
        compiler_params=pltpu.CompilerParams(
            collective_id=0, has_side_effects=True, vmem_limit_bytes=58 * 1024 * 1024
        ),
        cost_estimate=pl.CostEstimate(
            flops=int(7e9), bytes_accessed=int(1e7), transcendentals=row_count * key_count * HEADS
        ),
    )(
        tokens.reshape(row_count, D),
        norm_gain.reshape(1, D),
        query_key_value_weight.reshape(2, 2, 2, piece, qkv_width),
        out_weight.reshape(2, 2, out_piece, D),
        head_weight.T,
        coarse_rows,
        grad_fine.reshape(fine_rows, 4 * lon_cols),
    )
    return (
        fine_grid.reshape(grad_fine.shape),
        grad_tokens.reshape(tokens.shape),
        grad_head.reshape(HEAD_OUT, depth).T,
    )


def fits_pieces(tokens, qkv, out_weight):
    if lax.axis_size("dp") != 2 or lax.axis_size("tile") != 4 or lax.axis_size("fsdp") < 2:
        return False
    lat_rows, lon_cols = tokens.shape[1:3]
    if lat_rows % 2 or 4 * lon_cols != 128 or VARS > PADDED or 16 * VARS != HEAD_OUT:
        return False
    return qkv.shape[0] % 128 == 0 and out_weight.shape[0] % 64 == 0


def any_shards(*arguments):
    if fits_pieces(arguments[0], arguments[2], arguments[3]):
        return fused_shards(*arguments)
    return shards(*arguments)


def shards(tokens, norm_gain, query_key_value_weight, out_weight, head_weight, coarse, grad_fine):
    lat_rows = tokens.shape[1]
    lon_cols = tokens.shape[2]
    row_count = lat_rows * lon_cols
    flattened_rows = tokens[0].reshape(row_count, D).astype(jnp.float32)
    standard, inverse_dev = layer_norm(flattened_rows)
    normed = (standard * norm_gain).astype(jnp.bfloat16)
    full_qkv = lax.all_gather(query_key_value_weight, "fsdp", axis=0, tiled=True)
    projected = jnp.dot(normed, full_qkv, preferred_element_type=jnp.float32).astype(jnp.bfloat16)
    queries = projected[:, :INNER]
    pairs_local = projected[:, INNER:]
    margin_pairs = with_halo(
        pairs_local.reshape(lat_rows, lon_cols, 2 * INNER), (("tile", 1),), MARGIN
    )
    keys_values = margin_pairs.reshape(lat_rows * (lon_cols + 2 * MARGIN), 2 * INNER)
    attended, softmax_out = attend_forward(queries, keys_values)
    full_out = lax.all_gather(out_weight, "fsdp", axis=0, tiled=True)
    mixed_out = jnp.dot(attended, full_out, preferred_element_type=jnp.float32)
    hidden = (flattened_rows + mixed_out).astype(jnp.bfloat16)
    full_head = lax.all_gather(head_weight, "fsdp", axis=0, tiled=True)
    head_out = jnp.dot(hidden, full_head, preferred_element_type=jnp.float32)
    fine_head = (
        head_out.reshape(lat_rows, lon_cols, VARS, 4, 4)
        .transpose(2, 0, 3, 1, 4)
        .reshape(VARS, 4 * lat_rows, 4 * lon_cols)
    )
    coarse_padded_grid = with_halo(coarse[0], (("tile", 2),), 1)
    lat_lower, lat_upper_weight = interp_weights(jnp.arange(4 * lat_rows, dtype=jnp.int32))
    latitude_matrix = build_matrix(
        jnp.clip(lat_lower, 0, lat_rows - 1),
        jnp.clip(lat_lower + 1, 0, lat_rows - 1),
        lat_upper_weight,
        lat_rows,
    )
    lon_lower, lon_upper_weight = interp_weights(jnp.arange(4 * lon_cols, dtype=jnp.int32))
    lon_matrix = build_matrix(lon_lower + 1, lon_lower + 2, lon_upper_weight, lon_cols + 2)
    incomplete_grid = jnp.einsum(
        "lj,kji->kli", latitude_matrix, coarse_padded_grid, precision=lax.Precision.HIGHEST
    )
    residual = jnp.einsum(
        "vrb,cb->vrc", incomplete_grid, lon_matrix, precision=lax.Precision.HIGHEST
    )
    fine_grid = fine_head + residual
    grad_rows = (
        grad_fine[0]
        .reshape(VARS, lat_rows, 4, lon_cols, 4)
        .transpose(1, 3, 0, 2, 4)
        .reshape(row_count, HEAD_OUT)
    )
    grad_rows = grad_rows.astype(jnp.bfloat16)
    head_term = lax.dot_general(
        hidden, grad_rows, (((0,), (0,)), ((), ())), preferred_element_type=jnp.float32
    )
    head_block = lax.psum_scatter(head_term, "fsdp", scatter_dimension=0, tiled=True)
    grad_head = lax.psum(head_block, ("dp", "tile"))
    grad_hidden = contract_last(grad_rows, full_head)
    grad_attended = contract_last(grad_hidden.astype(jnp.bfloat16), full_out).astype(jnp.bfloat16)
    grad_queries, pair_gradient_rows = attend_backward(
        softmax_out, queries, keys_values, grad_attended
    )
    pair_gradient_rows = pair_gradient_rows.reshape(lat_rows, lon_cols + 2 * MARGIN, 2 * INNER)
    from_left = from_behind(pair_gradient_rows[:, lon_cols + MARGIN :], "tile", 1)
    from_right = from_behind(pair_gradient_rows[:, :MARGIN], "tile", -1)
    own_cells = pair_gradient_rows[:, MARGIN : MARGIN + lon_cols]
    own_cells = own_cells + jnp.pad(from_left, ((0, 0), (0, lon_cols - MARGIN), (0, 0)))
    own_cells = own_cells + jnp.pad(from_right, ((0, 0), (lon_cols - MARGIN, 0), (0, 0)))
    grad_all = jnp.concatenate(
        [grad_queries, own_cells.reshape(row_count, 2 * INNER).astype(jnp.bfloat16)], axis=1
    )
    grad_normed = contract_last(grad_all, full_qkv)
    grad_input = grad_hidden + norm_backward(grad_normed, standard, inverse_dev, norm_gain)
    grad_tokens = grad_input.astype(jnp.bfloat16).reshape(1, lat_rows, lon_cols, D)
    return (fine_grid[None], grad_tokens, grad_head)


def solution(mesh):
    placed = (
        P(("dp", "fsdp"), None, "tile", None),
        P(),
        P("fsdp", None),
        P("fsdp", None),
        P("fsdp", None),
        P(("dp", "fsdp"), None, None, "tile"),
        P(("dp", "fsdp"), None, None, "tile"),
    )
    return jax.shard_map(
        any_shards,
        mesh=mesh,
        in_specs=placed,
        out_specs=(
            P(("dp", "fsdp"), None, None, "tile"),
            P(("dp", "fsdp"), None, "tile", None),
            P("fsdp", None),
        ),
        check_vma=False,
    )
```

```python
import functools

import jax
import jax.numpy as jnp
from jax import lax
from jax.experimental import pallas as pl
from jax.experimental.pallas import tpu as pltpu
from jax.sharding import PartitionSpec as P

D = 1536
HEADS = 8
HEAD_DIM = 96
VARS = 20
MARGIN = 8
INNER = 768
HEAD_OUT = 320


EPSILON = 1e-05


def with_halo(shard, sides, width):
    for axis, dim in sides:
        devices, length = (lax.axis_size(axis), shard.shape[dim])
        up = [(i, (i + 1) % devices) for i in range(devices)]
        down = [(j, i) for i, j in up]
        last = lax.slice_in_dim(shard, length - width, length, axis=dim)
        leading = lax.slice_in_dim(shard, 0, width, axis=dim)
        before = lax.ppermute(last, axis, up)
        after = lax.ppermute(leading, axis, down)
        shard = jnp.concatenate([before, shard, after], axis=dim)
    return shard


def from_behind(value, axis, steps):
    count = lax.axis_size(axis)
    pairs = [(source, (source + steps) % count) for source in range(count)]
    return lax.ppermute(value, axis, pairs)


def layer_norm(values):
    average = jnp.mean(values, axis=-1, keepdims=True)
    centred = values - average
    variance = jnp.mean(centred * centred, axis=-1, keepdims=True)
    inverse_dev = lax.rsqrt(variance + EPSILON)
    return (centred * inverse_dev, inverse_dev)


def norm_backward(grad_normed, standard, inverse_dev, norm_gain):
    grad_standard = grad_normed * norm_gain
    first_mean = jnp.mean(grad_standard, axis=-1, keepdims=True)
    second_mean = jnp.mean(grad_standard * standard, axis=-1, keepdims=True)
    return inverse_dev * (grad_standard - first_mean - standard * second_mean)


def attend_forward(queries, keys_values):
    query_count = queries.shape[0]
    key_count = keys_values.shape[0]
    score_scale = HEAD_DIM ** (-0.5)
    query_heads = queries.reshape(query_count, HEADS, HEAD_DIM)
    key_heads = keys_values[:, :INNER].reshape(key_count, HEADS, HEAD_DIM)
    value_heads = keys_values[:, INNER:].reshape(key_count, HEADS, HEAD_DIM)
    scores = (
        jnp.einsum("qhd,khd->hqk", query_heads, key_heads, preferred_element_type=jnp.float32)
        * score_scale
    )
    biggest = jnp.max(scores, axis=-1, keepdims=True)
    exponent = jnp.exp(scores - biggest)
    softmax_out = exponent / jnp.sum(exponent, axis=-1, keepdims=True)
    softmax_low = softmax_out.astype(jnp.bfloat16)
    attended = jnp.einsum(
        "hqk,khd->qhd", softmax_low, value_heads, preferred_element_type=jnp.float32
    )
    return (attended.astype(jnp.bfloat16).reshape(query_count, INNER), softmax_out)


def attend_backward(softmax_out, queries, keys_values, grad_attended):
    query_count = queries.shape[0]
    key_count = keys_values.shape[0]
    score_scale = HEAD_DIM ** (-0.5)
    query_heads = queries.reshape(query_count, HEADS, HEAD_DIM)
    key_heads = keys_values[:, :INNER].reshape(key_count, HEADS, HEAD_DIM)
    value_heads = keys_values[:, INNER:].reshape(key_count, HEADS, HEAD_DIM)
    grad_heads = grad_attended.reshape(query_count, HEADS, HEAD_DIM)
    softmax_low = softmax_out.astype(jnp.bfloat16)
    grad_values = jnp.einsum(
        "hqk,qhd->khd", softmax_low, grad_heads, preferred_element_type=jnp.float32
    )
    grad_weights = jnp.einsum(
        "qhd,khd->hqk", grad_heads, value_heads, preferred_element_type=jnp.float32
    )
    weighted = jnp.sum(softmax_out * grad_weights, axis=-1, keepdims=True)
    grad_scores = (softmax_out * (grad_weights - weighted)).astype(jnp.bfloat16)
    grad_queries = (
        jnp.einsum("hqk,khd->qhd", grad_scores, key_heads, preferred_element_type=jnp.float32)
        * score_scale
    )
    grad_keys = (
        jnp.einsum("hqk,qhd->khd", grad_scores, query_heads, preferred_element_type=jnp.float32)
        * score_scale
    )
    pair_gradient_rows = jnp.concatenate(
        [grad_keys.reshape(key_count, INNER), grad_values.reshape(key_count, INNER)], axis=1
    )
    return (grad_queries.astype(jnp.bfloat16).reshape(query_count, INNER), pair_gradient_rows)


def interp_weights(fine_index):
    coarse_cell = fine_index // 4
    phase_index = fine_index % 4
    lower_shift = (phase_index < 2).astype(jnp.int32)
    upper_weight = (2 * phase_index - 3 + 8 * lower_shift).astype(jnp.float32) / 8.0
    return (coarse_cell - lower_shift, upper_weight)


def build_matrix(lower_cell, upper_cell, upper_weight, count):
    columns = jnp.arange(count, dtype=jnp.int32)
    lower_part = jnp.where(
        columns[None, :] == lower_cell[:, None], 1.0 - upper_weight[:, None], 0.0
    )
    upper_portion = jnp.where(columns[None, :] == upper_cell[:, None], upper_weight[:, None], 0.0)
    return lower_part + upper_portion


def contract_last(left_side, right_side):
    return lax.dot_general(
        left_side, right_side, (((1,), (1,)), ((), ())), preferred_element_type=jnp.float32
    )


def dot_nt(left_side, right_side):
    return lax.dot_general(
        left_side, right_side, (((1,), (1,)), ((), ())), preferred_element_type=jnp.float32
    )


def dot_tn(left_side, right_side):
    return lax.dot_general(
        left_side, right_side, (((0,), (0,)), ((), ())), preferred_element_type=jnp.float32
    )


def dot_nn(left_side, right_side):
    return jnp.dot(left_side, right_side, preferred_element_type=jnp.float32)


OUT0, OUT1, HEAD = range(3)
KEY, VALUE, QUERY = range(3)
CHUNKS = 9
ROUTES = (0, 1, 0, 0, 1, 0, 1, 0, 1)
HALF = INNER // 2
GROUPS = 2
GROUP = HEADS // GROUPS
PADDED = 32
WINDOW = 3


def split_dot(dot, left_side, right_side):
    first = left_side.astype(jnp.bfloat16)
    remainder = left_side - first.astype(jnp.float32)
    second = remainder.astype(jnp.bfloat16)
    third = (remainder - second.astype(jnp.float32)).astype(jnp.bfloat16)
    return dot(third, right_side) + dot(second, right_side) + dot(first, right_side)


def spread(rows, columns, where):
    row = lax.broadcasted_iota(jnp.int32, (rows, columns), 0)
    column = lax.broadcasted_iota(jnp.int32, (rows, columns), 1)
    return where(row, column)


def block_kernel(
    fsdp,
    lat_rows,
    lon_cols,
    tokens_ref,
    gain_ref,
    qkv_ref,
    out_ref,
    head_ref,
    coarse_ref,
    fine_grad_ref,
    fine_ref,
    grad_tokens_ref,
    grad_head_ref,
    w_out0,
    w_out1,
    w_head,
    w_key0,
    w_value0,
    w_query0,
    w_key1,
    w_value1,
    w_query1,
    standard_ref,
    inverse_ref,
    normed_ref,
    q_ref,
    k_ref,
    v_ref,
    p_ref,
    att_ref,
    ga_ref,
    gh_ref,
    hidden_ref,
    gq_ref,
    gk_ref,
    gv_ref,
    gn_ref,
    rows_ref,
    shuffled_ref,
    residual_ref,
    coarse_pad,
    w_head_shuffled,
    halo_out,
    grad_halo_out,
    grad_halo_in,
    term_ref,
    rs0,
    snd1,
    rs1,
    acc1,
    snd2,
    rs2,
    acc2,
    rs3,
    full_grad,
    local_sem,
    w_send,
    w_recv,
    halo_send,
    halo_recv,
    coarse_send,
    coarse_recv,
    rs_send,
    rs_recv,
    back_send,
    back_recv,
):
    row_count = lat_rows * lon_cols
    halo_rows = lat_rows * MARGIN
    fine_cols = 4 * lon_cols
    core = lax.axis_index("dp")
    me = lax.axis_index("fsdp")
    tile = lax.axis_index("tile")
    tiles = lax.axis_size("tile")
    ty, tx = tile // 2, tile % 2
    x_side = {"tile": tile + 1 - 2 * tx}
    y_side = {"tile": (tile + 2) % tiles}
    sibling = {"dp": 1 - core}
    right = {"tile": (tile + 1) % tiles}
    left = {"tile": (tile + tiles - 1) % tiles}
    weights = (w_out0, w_out1, w_head, w_key0, w_value0, w_query0, w_key1, w_value1, w_query1)
    depth = w_head.shape[1] * 4 * w_head.shape[4]
    bf16, f32 = jnp.bfloat16, jnp.float32

    def qkv_chunk(group, which):
        return 3 + 3 * group + which

    def qkv_columns(chunk):
        group, which = (chunk - 3) // 3, (chunk - 3) % 3
        return pl.ds({KEY: 1, VALUE: 2, QUERY: 0}[which] * INNER + group * HALF, HALF)

    def own_piece(chunk):
        if chunk == HEAD:
            return w_head.at[me, core, ty, tx]
        if chunk in (OUT0, OUT1):
            start = core * 2 * HALF + (chunk - OUT0) * HALF
            return out_ref.at[ty, tx, :, pl.ds(pl.multiple_of(start, 128), HALF)]
        return qkv_ref.at[core, ty, tx, :, qkv_columns(chunk)]

    def remote(src, dst, send, recv, device):
        return pltpu.make_async_remote_copy(
            src_ref=src,
            dst_ref=dst,
            send_sem=send,
            recv_sem=recv,
            device_id=device,
            device_id_type=pl.DeviceIdType.MESH,
        )

    def weight_copy(chunk, stage, k):
        full = weights[chunk]
        send, recv = w_send.at[chunk, stage, k - 1], w_recv.at[chunk, stage, k - 1]
        source = (me + fsdp - k) % fsdp
        if stage == 0:
            device = {"fsdp": (me + k) % fsdp}
            return remote(own_piece(chunk), full.at[me, core, ty, tx], send, recv, device)
        if stage == 1:
            part = full.at[source, core, ty, tx]
            device = x_side if ROUTES[chunk] == 0 else y_side
        elif stage == 2:
            if ROUTES[chunk] == 0:
                part, device = full.at[source, core, ty], y_side
            else:
                part, device = full.at[source, core, :, tx], x_side
        else:
            part, device = full.at[source, core], sibling
        return remote(part, part, send, recv, device)

    def advance(*steps):
        for chunk, stage in steps:
            for k in range(1, fsdp):
                if stage > 0:
                    weight_copy(chunk, stage - 1, k).wait_recv()
                if stage < 4:
                    weight_copy(chunk, stage, k).start()
            if stage == 1 and chunk + WINDOW < CHUNKS:
                advance((chunk + WINDOW, 0))

    def local_copies():
        pairs = []
        for d in range(2):
            for half, full in enumerate((w_out0, w_out1)):
                start = d * 2 * HALF + half * HALF
                pairs.append((out_ref.at[:, :, :, pl.ds(start, HALF)], full.at[me, d]))
        for chunk in range(3, CHUNKS):
            pairs.append((qkv_ref.at[:, :, :, :, qkv_columns(chunk)], weights[chunk].at[me]))
        return [
            pltpu.make_async_copy(src, dst, local_sem.at[i]) for i, (src, dst) in enumerate(pairs)
        ]

    copies = local_copies()
    for copy in copies:
        copy.start()

    barrier = pltpu.get_barrier_semaphore()
    partners = [{"tile": (tile + i) % tiles} for i in range(1, 4)]
    partners += [{"fsdp": (me + i) % fsdp} for i in range(1, fsdp)]
    partners += [sibling]
    for partner in partners:
        pl.semaphore_signal(barrier, inc=1, device_id=partner, device_id_type=pl.DeviceIdType.MESH)
    pl.semaphore_wait(barrier, len(partners))

    advance((OUT0, 0), (OUT1, 0))
    eye = spread(depth, depth, lambda r, c: (r == c).astype(f32)).astype(bf16)
    w_head[me] = dot_nt(eye, head_ref[...]).astype(bf16).reshape(w_head.shape[1:])
    advance((HEAD, 0))
    cells = lat_rows * PADDED
    shuffled_ref[pl.ds(0, cells), :] = jnp.zeros((cells, fine_cols), f32)
    shuffled_ref[pl.ds(0, VARS * lat_rows), pl.ds(0, lon_cols)] = coarse_ref[...]
    by_latitude = spread(
        cells, cells, lambda r, c: (c == (r % lat_rows) * PADDED + r // lat_rows).astype(f32)
    ).astype(bf16)
    coarse_pad[pl.ds(MARGIN, lon_cols), :] = split_dot(
        dot_nn, shuffled_ref[pl.ds(0, cells), :].T[:lon_cols], by_latitude
    )
    coarse_copies = [
        remote(
            coarse_pad.at[pl.ds(lon_cols, MARGIN)],
            coarse_pad.at[pl.ds(0, MARGIN)],
            coarse_send.at[0],
            coarse_recv.at[0],
            right,
        ),
        remote(
            coarse_pad.at[pl.ds(MARGIN, MARGIN)],
            coarse_pad.at[pl.ds(MARGIN + lon_cols, MARGIN)],
            coarse_send.at[1],
            coarse_recv.at[1],
            left,
        ),
    ]
    for copy in coarse_copies:
        copy.start()

    scale = HEAD_DIM ** (-0.5)

    def normalised():
        return layer_norm(tokens_ref[...].astype(f32))

    standard, inverse_dev = normalised()
    standard_ref[...] = standard
    inverse_ref[...] = inverse_dev
    normed_ref[...] = (standard * gain_ref[...][None, :]).astype(bf16)

    advance((0, 1))

    def cell_rows(i, a):
        return pl.ds((i * 4 + a) * PADDED, VARS)

    def fine_rows(i, a):
        return pl.ds(4 * i + a, VARS, stride=4 * lat_rows)

    shuffled_ref[...] = jnp.zeros_like(shuffled_ref)
    for i in range(lat_rows):
        for a in range(4):
            shuffled_ref[cell_rows(i, a), :] = fine_grad_ref[fine_rows(i, a), :]
    by_phase = spread(
        fine_cols, fine_cols, lambda r, c: (r == 4 * (c % lon_cols) + c // lon_cols).astype(f32)
    ).astype(bf16)
    to_phase = spread(
        fine_cols, fine_cols, lambda r, c: (c == 4 * (r % lon_cols) + r // lon_cols).astype(f32)
    ).astype(bf16)
    to_feature = spread(
        16 * PADDED,
        HEAD_OUT,
        lambda r, c: (
            c == 16 * (r % PADDED) + 4 * (r // PADDED % 4) + r // (4 * PADDED)
        ).astype(f32),
    ).astype(bf16)
    width = 4 * PADDED
    turned = dot_nn(shuffled_ref[...].astype(bf16), by_phase).T
    turned = jnp.concatenate(
        [
            jnp.concatenate(
                [
                    turned[b * lon_cols : (b + 1) * lon_cols, i * width : (i + 1) * width]
                    for b in range(4)
                ],
                axis=1,
            )
            for i in range(lat_rows)
        ],
        axis=0,
    )
    rows_ref[...] = dot_nn(turned.astype(bf16), to_feature).astype(bf16)

    advance((1, 1), (0, 2), (2, 1), (1, 2), (0, 3), (3, 1), (2, 2))
    for copy in copies:
        copy.wait()

    for copy in coarse_copies:
        copy.wait_recv()

    def lon_weight(row, column):
        phase = column % 4
        lower_shift = (phase < 2).astype(jnp.int32)
        upper_weight = (2 * phase - 3 + 8 * lower_shift).astype(f32) / 8.0
        lower_cell = column // 4 - lower_shift + MARGIN
        return jnp.where(row == lower_cell, 1.0 - upper_weight, 0.0) + jnp.where(
            row == lower_cell + 1, upper_weight, 0.0
        )

    lon_matrix = spread(coarse_pad.shape[0], fine_cols, lon_weight).astype(bf16)
    incomplete = split_dot(dot_nn, coarse_pad[...].T, lon_matrix)
    for i in range(lat_rows):
        for a in range(4):
            low = i - 1 if a < 2 else i
            upper_weight = (5 / 8, 7 / 8, 1 / 8, 3 / 8)[a]
            lower, upper = (
                incomplete[cell * PADDED : (cell + 1) * PADDED]
                for cell in (max(low, 0), min(low + 1, lat_rows - 1))
            )
            residual_ref[pl.ds((i * 4 + a) * PADDED, PADDED), :] = (
                lower * (1.0 - upper_weight) + upper * upper_weight
            )

    advance((0, 4), (1, 3), (4, 1), (3, 2), (1, 4), (2, 3), (5, 1), (4, 2))

    def columns_of(f):
        return pl.ds(pl.multiple_of(f * depth, 128), depth)

    advance((2, 4))

    def grad_hidden_step(f, _):
        rows = w_head[f].reshape(depth, HEAD_OUT)
        gh_ref[:, columns_of(f)] = dot_nt(rows_ref[...], rows)
        w_head_shuffled[pl.ds(pl.multiple_of(f * depth, 128), depth), :] = dot_nt(
            rows, to_feature
        ).astype(bf16)
        return 0

    lax.fori_loop(0, fsdp, grad_hidden_step, 0)
    advance((3, 3), (6, 1), (5, 2))
    out_parts = [(d, half) for d in range(2) for half in range(2)]

    def out_block(d, half):
        full = (w_out0, w_out1)[half]
        return full[:, d].reshape(INNER, HALF)

    def out_columns(d, half):
        return pl.ds(d * 2 * HALF + half * HALF, HALF)

    grad_attended = jnp.zeros((row_count, INNER), f32)
    for d, half in out_parts:
        low = gh_ref[:, out_columns(d, half)].astype(bf16)
        grad_attended = grad_attended + dot_nt(low, out_block(d, half))
    ga_ref[...] = grad_attended.astype(bf16)

    advance((4, 3), (7, 1), (6, 2))

    def edge(rows, first):
        shaped = rows.reshape(lat_rows, lon_cols, rows.shape[-1])
        part = shaped[:, :MARGIN] if first else shaped[:, lon_cols - MARGIN :]
        return part.reshape(halo_rows, rows.shape[-1])

    def halo_copy(group, which, side):
        full = (k_ref, v_ref)[which]
        index = (0, group, which, side)
        return remote(
            halo_out.at[group, which, side],
            full.at[group, pl.ds(row_count + side * halo_rows, halo_rows)],
            halo_send.at[index],
            halo_recv.at[index],
            (right, left)[side],
        )

    def grad_halo_copy(group, which, side):
        index = (1, group, which, side)
        return remote(
            grad_halo_out.at[group, which, side],
            grad_halo_in.at[group, which, side],
            halo_send.at[index],
            halo_recv.at[index],
            (left, right)[side],
        )

    def project(group, which):
        full = weights[qkv_chunk(group, which)]
        product = dot_nn(normed_ref[...], full[...].reshape(-1, HALF))
        if which == QUERY:
            q_ref[group] = product.astype(bf16)
            return
        (k_ref, v_ref)[which][group, pl.ds(0, row_count)] = product.astype(bf16)
        for side in range(2):
            halo_out[group, which, side] = edge(product, side == 1).astype(bf16)
            halo_copy(group, which, side).start()

    def await_halos(group):
        for which in range(2):
            for side in range(2):
                halo_copy(group, which, side).wait_recv()

    def window(i):
        low, high = i * HEAD_DIM, (i + 1) * HEAD_DIM
        start, stop = low // 128 * 128, -(-high // 128) * 128
        lanes = lax.broadcasted_iota(jnp.int32, (1, stop - start), 1) + start
        return start, stop, ((lanes >= low) & (lanes < high)).astype(f32)

    def add_parts(parts, start, product):
        for j in range(product.shape[1] // 128):
            piece = product[:, j * 128 : (j + 1) * 128]
            at = start // 128 + j
            parts[at] = piece if parts[at] is None else parts[at] + piece

    def no_parts():
        return [None] * (HALF // 128)

    def forward(group, between=()):
        parts = no_parts()
        for i in range(GROUP):
            start, stop, mask = window(i)
            masked = q_ref[group, :, start:stop] * mask.astype(bf16)
            scores = dot_nt(masked, k_ref[group, :, start:stop]) * scale
            biggest = jnp.max(scores, axis=-1, keepdims=True)
            exponent = jnp.exp(scores - biggest)
            softmax = exponent / jnp.sum(exponent, axis=-1, keepdims=True)
            p_ref[group * GROUP + i] = softmax
            add_parts(parts, start, dot_nn(softmax.astype(bf16), v_ref[group, :, start:stop]) * mask)
            if i < len(between):
                between[i]()
        att_ref[:, pl.ds(group * HALF, HALF)] = jnp.concatenate(parts, axis=1).astype(bf16)

    def backward(group, between=()):
        query_parts, key_parts, value_parts = no_parts(), no_parts(), no_parts()
        for i in range(GROUP):
            start, stop, mask = window(i)
            softmax = p_ref[group * GROUP + i]
            grads = ga_ref[:, group * HALF + start : group * HALF + stop]
            weights_grad = dot_nt(grads * mask.astype(bf16), v_ref[group, :, start:stop])
            weighted = jnp.sum(softmax * weights_grad, axis=-1, keepdims=True)
            grad_scores = (softmax * (weights_grad - weighted)).astype(bf16)
            scaled = mask * scale
            add_parts(query_parts, start, dot_nn(grad_scores, k_ref[group, :, start:stop]) * scaled)
            add_parts(key_parts, start, dot_tn(grad_scores, q_ref[group, :, start:stop]) * scaled)
            add_parts(value_parts, start, dot_tn(softmax.astype(bf16), grads) * mask)
            if i < len(between):
                between[i]()
        gq_ref[group] = jnp.concatenate(query_parts, axis=1).astype(bf16)
        gk_ref[group] = jnp.concatenate(key_parts, axis=1)
        gv_ref[group] = jnp.concatenate(value_parts, axis=1)
        for which, full in enumerate((gk_ref, gv_ref)):
            for side in range(2):
                rows = full[group, pl.ds(row_count + side * halo_rows, halo_rows), :]
                grad_halo_out[group, which, side] = rows.astype(bf16)
                grad_halo_copy(group, which, side).start()

    def own_cells(group, which):
        full = (gk_ref, gv_ref)[which]
        for side in range(2):
            grad_halo_copy(group, which, side).wait_recv()
        rows = full[group, pl.ds(0, row_count), :].reshape(lat_rows, lon_cols, HALF)
        shape = (lat_rows, MARGIN, HALF)
        last = grad_halo_in[group, which, 0].astype(f32).reshape(shape)
        first = grad_halo_in[group, which, 1].astype(f32).reshape(shape)
        rows = jnp.concatenate(
            [
                rows[:, :MARGIN] + first,
                rows[:, MARGIN : lon_cols - MARGIN],
                rows[:, lon_cols - MARGIN :] + last,
            ],
            axis=1,
        )
        return rows.reshape(row_count, HALF).astype(bf16)

    def add_grad_normed(group, which, first=False):
        full = weights[qkv_chunk(group, which)]
        if which != QUERY:
            (k_ref, v_ref)[which][group, pl.ds(0, row_count)] = own_cells(group, which)

        def step(f, _):
            if which == QUERY:
                rows = gq_ref[group]
            else:
                rows = (k_ref, v_ref)[which][group, pl.ds(0, row_count)]
            product = dot_nt(rows, full[f].reshape(depth, HALF))
            if first:
                gn_ref[:, columns_of(f)] = product
            else:
                gn_ref[:, columns_of(f)] += product
            return 0

        lax.fori_loop(0, fsdp, step, 0)

    advance((3, 4))
    project(0, KEY)
    advance((4, 4))
    project(0, VALUE)
    advance((5, 3), (8, 1), (7, 2), (5, 4))
    project(0, QUERY)
    advance((6, 3))
    await_halos(0)
    forward(0, (lambda: None, lambda: advance((8, 2)), lambda: advance((7, 3))))
    advance((6, 4))
    project(1, KEY)

    def next_values():
        advance((7, 4))
        project(1, VALUE)

    backward(0, (lambda: advance((8, 3)), next_values))
    advance((8, 4))
    project(1, QUERY)
    for chunk in range(CHUNKS):
        for stage in range(4):
            for k in range(1, fsdp):
                weight_copy(chunk, stage, k).wait_send()
    await_halos(1)
    forward(1)
    for d, half in out_parts:
        columns = out_columns(d, half)
        mixed = dot_nn(att_ref[...], out_block(d, half))
        hidden_ref[:, columns] = (tokens_ref[:, columns].astype(f32) + mixed).astype(bf16)

    def term_step(f, _):
        term_ref[f] = dot_tn(rows_ref[...], hidden_ref[:, columns_of(f)]).reshape(
            term_ref.shape[1:]
        )
        return 0

    lax.fori_loop(0, fsdp, term_step, 0)

    core_copy = remote(term_ref.at[:, 1 - core], rs0, rs_send.at[0], rs_recv.at[0], sibling)
    half = fsdp // 2
    routes = (
        (pl.ds(0, half), ty, tx, y_side, x_side),
        (pl.ds(half, fsdp - half), tx, ty, x_side, y_side),
    )
    first_copies = [
        remote(snd1.at[part], rs1.at[part], rs_send.at[1 + i], rs_recv.at[1 + i], near)
        for i, (part, _, _, near, _) in enumerate(routes)
    ]
    second_copies = [
        remote(snd2.at[part], rs2.at[part], rs_send.at[3 + i], rs_recv.at[3 + i], far)
        for i, (part, _, _, _, far) in enumerate(routes)
    ]
    on_second = me // half
    outer = ty + on_second * (tx - ty)
    inner = tx + on_second * (ty - tx)
    z_copies = [
        remote(
            acc2.at[(me + k) % fsdp],
            rs3.at[k - 1],
            rs_send.at[5 + k],
            rs_recv.at[5 + k],
            {"fsdp": (me + k) % fsdp},
        )
        for k in range(1, fsdp)
    ]
    mine = full_grad.at[core, outer, inner]
    back = [
        remote(
            mine,
            mine,
            back_send.at[i - 1],
            back_recv.at[i - 1],
            {"tile": (tile + i) % tiles},
        )
        for i in range(1, 4)
    ]
    last_back = remote(
        full_grad.at[core], full_grad.at[core], rs_send.at[5], rs_recv.at[5], sibling
    )

    def reduce_first():
        core_copy.wait_recv()
        for copy, (part, first, _, _, _) in zip(first_copies, routes):
            theirs = term_ref[part, core, 1 - first] + rs0[part, 1 - first]
            snd1[part] = theirs.reshape(-1, *snd1.shape[1:]).astype(bf16)
            copy.start()
        for part, first, _, _, _ in routes:
            acc1[part] = term_ref[part, core, first] + rs0[part, first]

    def reduce_second():
        for copy, (part, _, second, _, _) in zip(first_copies, routes):
            copy.wait_recv()
            arrived = rs1[part].astype(f32)
            acc1[part] = acc1[part] + arrived.reshape(-1, *acc1.shape[1:])
        for copy, (part, _, second, _, _) in zip(second_copies, routes):
            snd2[part] = acc1[part, 1 - second]
            copy.start()

    def reduce_z():
        for copy, (part, _, second, _, _) in zip(second_copies, routes):
            copy.wait_recv()
            acc2[part] = acc1[part, second] + rs2[part]
        for copy in z_copies:
            copy.start()

    core_copy.start()
    backward(1, (lambda: None, reduce_first))
    add_grad_normed(0, QUERY, first=True)
    add_grad_normed(0, KEY)
    reduce_second()
    add_grad_normed(0, VALUE)
    add_grad_normed(1, QUERY)
    reduce_z()

    head_out = dot_nn(hidden_ref[...], w_head_shuffled[...])
    head_out = jnp.concatenate(
        [
            jnp.concatenate(
                [
                    head_out[i * lon_cols : (i + 1) * lon_cols, b * width : (b + 1) * width]
                    for b in range(4)
                ],
                axis=0,
            )
            for i in range(lat_rows)
        ],
        axis=1,
    )
    shuffled_ref[...] = split_dot(dot_nn, head_out.T, to_phase) + residual_ref[...]
    for i in range(lat_rows):
        for a in range(4):
            fine_ref[fine_rows(i, a), :] = shuffled_ref[cell_rows(i, a), :]

    for copy in z_copies:
        copy.wait_recv()
    summed = acc2[me]
    for k in range(1, fsdp):
        summed = summed + rs3[k - 1]
    full_grad[core, outer, inner] = summed
    for copy in back:
        copy.start()
    add_grad_normed(1, KEY)
    add_grad_normed(1, VALUE)
    for copy in back:
        copy.wait_recv()
    last_back.start()

    grad_input = norm_backward(
        gn_ref[...], standard_ref[...], inverse_ref[...], gain_ref[...][None, :]
    )
    grad_tokens_ref[...] = (gh_ref[...] + grad_input).astype(bf16)

    last_back.wait_recv()
    grad_head_ref[...] = full_grad[...]

    for group in range(GROUPS):
        for which in range(2):
            for side in range(2):
                halo_copy(group, which, side).wait_send()
                grad_halo_copy(group, which, side).wait_send()
    for copy in coarse_copies + [core_copy, last_back] + first_copies + second_copies + z_copies + back:
        copy.wait_send()


def fused_shards(
    tokens, norm_gain, query_key_value_weight, out_weight, head_weight, coarse, grad_fine
):
    fsdp = lax.axis_size("fsdp")
    lat_rows, lon_cols = tokens.shape[1:3]
    row_count = lat_rows * lon_cols
    halo_rows = lat_rows * MARGIN
    key_count = row_count + 2 * halo_rows
    depth, qkv_width = query_key_value_weight.shape
    piece = depth // 8
    out_piece = out_weight.shape[0] // 4
    head_piece = HEAD_OUT // 8
    bf16, f32 = jnp.bfloat16, jnp.float32
    vmem = pl.BlockSpec(memory_space=pltpu.VMEM)
    hbm = pl.BlockSpec(memory_space=pl.ANY)
    def full(rows, columns):
        return pltpu.VMEM((fsdp, 2, 2, 2, rows, columns), bf16)

    fine_rows = VARS * 4 * lat_rows
    shuffled = 4 * lat_rows * PADDED
    fine_grid, grad_tokens, grad_head = pl.pallas_call(
        functools.partial(block_kernel, fsdp, lat_rows, lon_cols),
        out_shape=(
            jax.ShapeDtypeStruct((fine_rows, 4 * lon_cols), f32),
            jax.ShapeDtypeStruct((row_count, D), bf16),
            jax.ShapeDtypeStruct((2, 2, 2, head_piece, depth), f32),
        ),
        in_specs=[vmem, vmem, hbm, hbm, vmem, vmem, vmem],
        out_specs=(vmem, vmem, vmem),
        scratch_shapes=[
            full(out_piece, HALF),
            full(out_piece, HALF),
            full(piece, HEAD_OUT),
        ]
        + [full(piece, HALF)] * 6
        + [
            pltpu.VMEM((row_count, D), f32),
            pltpu.VMEM((row_count, 1), f32),
            pltpu.VMEM((row_count, D), bf16),
            pltpu.VMEM((GROUPS, row_count, HALF), bf16),
            pltpu.VMEM((GROUPS, key_count, HALF), bf16),
            pltpu.VMEM((GROUPS, key_count, HALF), bf16),
            pltpu.VMEM((HEADS, row_count, key_count), f32),
            pltpu.VMEM((row_count, INNER), bf16),
            pltpu.VMEM((row_count, INNER), bf16),
            pltpu.VMEM((row_count, D), f32),
            pltpu.VMEM((row_count, D), bf16),
            pltpu.VMEM((GROUPS, row_count, HALF), bf16),
            pltpu.VMEM((GROUPS, key_count, HALF), f32),
            pltpu.VMEM((GROUPS, key_count, HALF), f32),
            pltpu.VMEM((row_count, D), f32),
            pltpu.VMEM((row_count, HEAD_OUT), bf16),
            pltpu.VMEM((shuffled, 4 * lon_cols), f32),
            pltpu.VMEM((shuffled, 4 * lon_cols), f32),
            pltpu.VMEM((lon_cols + 2 * MARGIN, lat_rows * PADDED), f32),
            pltpu.VMEM((D, 16 * PADDED), bf16),
            pltpu.VMEM((GROUPS, 2, 2, halo_rows, HALF), bf16),
            pltpu.VMEM((GROUPS, 2, 2, halo_rows, HALF), bf16),
            pltpu.VMEM((GROUPS, 2, 2, halo_rows, HALF), bf16),
            pltpu.VMEM((fsdp, 2, 2, 2, head_piece, depth), f32),
            pltpu.VMEM((fsdp, 2, 2, head_piece, depth), f32),
            pltpu.VMEM((fsdp, 2 * head_piece, depth), bf16),
            pltpu.VMEM((fsdp, 2 * head_piece, depth), bf16),
            pltpu.VMEM((fsdp, 2, head_piece, depth), f32),
            pltpu.VMEM((fsdp, head_piece, depth), f32),
            pltpu.VMEM((fsdp, head_piece, depth), f32),
            pltpu.VMEM((fsdp, head_piece, depth), f32),
            pltpu.VMEM((fsdp - 1, head_piece, depth), f32),
            pltpu.VMEM((2, 2, 2, head_piece, depth), f32),
            pltpu.SemaphoreType.DMA((10,)),
            pltpu.SemaphoreType.DMA((CHUNKS, 4, fsdp - 1)),
            pltpu.SemaphoreType.DMA((CHUNKS, 4, fsdp - 1)),
            pltpu.SemaphoreType.DMA((2, GROUPS, 2, 2)),
            pltpu.SemaphoreType.DMA((2, GROUPS, 2, 2)),
            pltpu.SemaphoreType.DMA((2,)),
            pltpu.SemaphoreType.DMA((2,)),
            pltpu.SemaphoreType.DMA((5 + fsdp,)),
            pltpu.SemaphoreType.DMA((5 + fsdp,)),
            pltpu.SemaphoreType.DMA((3,)),
            pltpu.SemaphoreType.DMA((3,)),
        ],
        compiler_params=pltpu.CompilerParams(
            collective_id=0, has_side_effects=True, vmem_limit_bytes=58 * 1024 * 1024
        ),
        cost_estimate=pl.CostEstimate(
            flops=int(7e9), bytes_accessed=int(1e7), transcendentals=row_count * key_count * HEADS
        ),
    )(
        tokens.reshape(row_count, D),
        norm_gain,
        query_key_value_weight.reshape(2, 2, 2, piece, qkv_width),
        out_weight.reshape(2, 2, out_piece, D),
        head_weight.T,
        coarse.reshape(VARS * lat_rows, lon_cols),
        grad_fine.reshape(fine_rows, 4 * lon_cols),
    )
    return (
        fine_grid.reshape(grad_fine.shape),
        grad_tokens.reshape(tokens.shape),
        grad_head.reshape(HEAD_OUT, depth).T,
    )


def fits_pieces(tokens, qkv, out_weight):
    if lax.axis_size("dp") != 2 or lax.axis_size("tile") != 4 or lax.axis_size("fsdp") % 2:
        return False
    lat_rows, lon_cols = tokens.shape[1:3]
    if lat_rows % 2 or 4 * lon_cols != 128 or VARS > PADDED or 16 * VARS != HEAD_OUT:
        return False
    return qkv.shape[0] % 128 == 0 and out_weight.shape[0] % 64 == 0


def any_shards(*arguments):
    if fits_pieces(arguments[0], arguments[2], arguments[3]):
        return fused_shards(*arguments)
    return shards(*arguments)


def shards(tokens, norm_gain, query_key_value_weight, out_weight, head_weight, coarse, grad_fine):
    lat_rows = tokens.shape[1]
    lon_cols = tokens.shape[2]
    row_count = lat_rows * lon_cols
    flattened_rows = tokens[0].reshape(row_count, D).astype(jnp.float32)
    standard, inverse_dev = layer_norm(flattened_rows)
    normed = (standard * norm_gain).astype(jnp.bfloat16)
    full_qkv = lax.all_gather(query_key_value_weight, "fsdp", axis=0, tiled=True)
    projected = jnp.dot(normed, full_qkv, preferred_element_type=jnp.float32).astype(jnp.bfloat16)
    queries = projected[:, :INNER]
    pairs_local = projected[:, INNER:]
    margin_pairs = with_halo(
        pairs_local.reshape(lat_rows, lon_cols, 2 * INNER), (("tile", 1),), MARGIN
    )
    keys_values = margin_pairs.reshape(lat_rows * (lon_cols + 2 * MARGIN), 2 * INNER)
    attended, softmax_out = attend_forward(queries, keys_values)
    full_out = lax.all_gather(out_weight, "fsdp", axis=0, tiled=True)
    mixed_out = jnp.dot(attended, full_out, preferred_element_type=jnp.float32)
    hidden = (flattened_rows + mixed_out).astype(jnp.bfloat16)
    full_head = lax.all_gather(head_weight, "fsdp", axis=0, tiled=True)
    head_out = jnp.dot(hidden, full_head, preferred_element_type=jnp.float32)
    fine_head = (
        head_out.reshape(lat_rows, lon_cols, VARS, 4, 4)
        .transpose(2, 0, 3, 1, 4)
        .reshape(VARS, 4 * lat_rows, 4 * lon_cols)
    )
    coarse_padded_grid = with_halo(coarse[0], (("tile", 2),), 1)
    lat_lower, lat_upper_weight = interp_weights(jnp.arange(4 * lat_rows, dtype=jnp.int32))
    latitude_matrix = build_matrix(
        jnp.clip(lat_lower, 0, lat_rows - 1),
        jnp.clip(lat_lower + 1, 0, lat_rows - 1),
        lat_upper_weight,
        lat_rows,
    )
    lon_lower, lon_upper_weight = interp_weights(jnp.arange(4 * lon_cols, dtype=jnp.int32))
    lon_matrix = build_matrix(lon_lower + 1, lon_lower + 2, lon_upper_weight, lon_cols + 2)
    incomplete_grid = jnp.einsum(
        "lj,kji->kli", latitude_matrix, coarse_padded_grid, precision=lax.Precision.HIGHEST
    )
    residual = jnp.einsum(
        "vrb,cb->vrc", incomplete_grid, lon_matrix, precision=lax.Precision.HIGHEST
    )
    fine_grid = fine_head + residual
    grad_rows = (
        grad_fine[0]
        .reshape(VARS, lat_rows, 4, lon_cols, 4)
        .transpose(1, 3, 0, 2, 4)
        .reshape(row_count, HEAD_OUT)
    )
    grad_rows = grad_rows.astype(jnp.bfloat16)
    head_term = lax.dot_general(
        hidden, grad_rows, (((0,), (0,)), ((), ())), preferred_element_type=jnp.float32
    )
    head_block = lax.psum_scatter(head_term, "fsdp", scatter_dimension=0, tiled=True)
    grad_head = lax.psum(head_block, ("dp", "tile"))
    grad_hidden = contract_last(grad_rows, full_head)
    grad_attended = contract_last(grad_hidden.astype(jnp.bfloat16), full_out).astype(jnp.bfloat16)
    grad_queries, pair_gradient_rows = attend_backward(
        softmax_out, queries, keys_values, grad_attended
    )
    pair_gradient_rows = pair_gradient_rows.reshape(lat_rows, lon_cols + 2 * MARGIN, 2 * INNER)
    from_left = from_behind(pair_gradient_rows[:, lon_cols + MARGIN :], "tile", 1)
    from_right = from_behind(pair_gradient_rows[:, :MARGIN], "tile", -1)
    own_cells = pair_gradient_rows[:, MARGIN : MARGIN + lon_cols]
    own_cells = own_cells + jnp.pad(from_left, ((0, 0), (0, lon_cols - MARGIN), (0, 0)))
    own_cells = own_cells + jnp.pad(from_right, ((0, 0), (lon_cols - MARGIN, 0), (0, 0)))
    grad_all = jnp.concatenate(
        [grad_queries, own_cells.reshape(row_count, 2 * INNER).astype(jnp.bfloat16)], axis=1
    )
    grad_normed = contract_last(grad_all, full_qkv)
    grad_input = grad_hidden + norm_backward(grad_normed, standard, inverse_dev, norm_gain)
    grad_tokens = grad_input.astype(jnp.bfloat16).reshape(1, lat_rows, lon_cols, D)
    return (fine_grid[None], grad_tokens, grad_head)


def solution(mesh):
    placed = (
        P(("dp", "fsdp"), None, "tile", None),
        P(),
        P("fsdp", None),
        P("fsdp", None),
        P("fsdp", None),
        P(("dp", "fsdp"), None, None, "tile"),
        P(("dp", "fsdp"), None, None, "tile"),
    )
    return jax.shard_map(
        any_shards,
        mesh=mesh,
        in_specs=placed,
        out_specs=(
            P(("dp", "fsdp"), None, None, "tile"),
            P(("dp", "fsdp"), None, "tile", None),
            P("fsdp", None),
        ),
        check_vma=False,
    )
```

```python
import functools

import jax
import jax.numpy as jnp
from jax import lax
from jax.experimental import pallas as pl
from jax.experimental.pallas import tpu as pltpu
from jax.sharding import PartitionSpec as P

D = 1536
HEADS = 8
HEAD_DIM = 96
VARS = 20
MARGIN = 8
INNER = 768
HEAD_OUT = 320


EPSILON = 1e-05


def with_halo(shard, sides, width):
    for axis, dim in sides:
        devices, length = (lax.axis_size(axis), shard.shape[dim])
        up = [(i, (i + 1) % devices) for i in range(devices)]
        down = [(j, i) for i, j in up]
        last = lax.slice_in_dim(shard, length - width, length, axis=dim)
        leading = lax.slice_in_dim(shard, 0, width, axis=dim)
        before = lax.ppermute(last, axis, up)
        after = lax.ppermute(leading, axis, down)
        shard = jnp.concatenate([before, shard, after], axis=dim)
    return shard


def from_behind(value, axis, steps):
    count = lax.axis_size(axis)
    pairs = [(source, (source + steps) % count) for source in range(count)]
    return lax.ppermute(value, axis, pairs)


def layer_norm(values):
    average = jnp.mean(values, axis=-1, keepdims=True)
    centred = values - average
    variance = jnp.mean(centred * centred, axis=-1, keepdims=True)
    inverse_dev = lax.rsqrt(variance + EPSILON)
    return (centred * inverse_dev, inverse_dev)


def norm_backward(grad_normed, standard, inverse_dev, norm_gain):
    grad_standard = grad_normed * norm_gain
    first_mean = jnp.mean(grad_standard, axis=-1, keepdims=True)
    second_mean = jnp.mean(grad_standard * standard, axis=-1, keepdims=True)
    return inverse_dev * (grad_standard - first_mean - standard * second_mean)


def attend_forward(queries, keys_values):
    query_count = queries.shape[0]
    key_count = keys_values.shape[0]
    score_scale = HEAD_DIM ** (-0.5)
    query_heads = queries.reshape(query_count, HEADS, HEAD_DIM)
    key_heads = keys_values[:, :INNER].reshape(key_count, HEADS, HEAD_DIM)
    value_heads = keys_values[:, INNER:].reshape(key_count, HEADS, HEAD_DIM)
    scores = (
        jnp.einsum("qhd,khd->hqk", query_heads, key_heads, preferred_element_type=jnp.float32)
        * score_scale
    )
    biggest = jnp.max(scores, axis=-1, keepdims=True)
    exponent = jnp.exp(scores - biggest)
    softmax_out = exponent / jnp.sum(exponent, axis=-1, keepdims=True)
    softmax_low = softmax_out.astype(jnp.bfloat16)
    attended = jnp.einsum(
        "hqk,khd->qhd", softmax_low, value_heads, preferred_element_type=jnp.float32
    )
    return (attended.astype(jnp.bfloat16).reshape(query_count, INNER), softmax_out)


def attend_backward(softmax_out, queries, keys_values, grad_attended):
    query_count = queries.shape[0]
    key_count = keys_values.shape[0]
    score_scale = HEAD_DIM ** (-0.5)
    query_heads = queries.reshape(query_count, HEADS, HEAD_DIM)
    key_heads = keys_values[:, :INNER].reshape(key_count, HEADS, HEAD_DIM)
    value_heads = keys_values[:, INNER:].reshape(key_count, HEADS, HEAD_DIM)
    grad_heads = grad_attended.reshape(query_count, HEADS, HEAD_DIM)
    softmax_low = softmax_out.astype(jnp.bfloat16)
    grad_values = jnp.einsum(
        "hqk,qhd->khd", softmax_low, grad_heads, preferred_element_type=jnp.float32
    )
    grad_weights = jnp.einsum(
        "qhd,khd->hqk", grad_heads, value_heads, preferred_element_type=jnp.float32
    )
    weighted = jnp.sum(softmax_out * grad_weights, axis=-1, keepdims=True)
    grad_scores = (softmax_out * (grad_weights - weighted)).astype(jnp.bfloat16)
    grad_queries = (
        jnp.einsum("hqk,khd->qhd", grad_scores, key_heads, preferred_element_type=jnp.float32)
        * score_scale
    )
    grad_keys = (
        jnp.einsum("hqk,qhd->khd", grad_scores, query_heads, preferred_element_type=jnp.float32)
        * score_scale
    )
    pair_gradient_rows = jnp.concatenate(
        [grad_keys.reshape(key_count, INNER), grad_values.reshape(key_count, INNER)], axis=1
    )
    return (grad_queries.astype(jnp.bfloat16).reshape(query_count, INNER), pair_gradient_rows)


def interp_weights(fine_index):
    coarse_cell = fine_index // 4
    phase_index = fine_index % 4
    lower_shift = (phase_index < 2).astype(jnp.int32)
    upper_weight = (2 * phase_index - 3 + 8 * lower_shift).astype(jnp.float32) / 8.0
    return (coarse_cell - lower_shift, upper_weight)


def build_matrix(lower_cell, upper_cell, upper_weight, count):
    columns = jnp.arange(count, dtype=jnp.int32)
    lower_part = jnp.where(
        columns[None, :] == lower_cell[:, None], 1.0 - upper_weight[:, None], 0.0
    )
    upper_portion = jnp.where(columns[None, :] == upper_cell[:, None], upper_weight[:, None], 0.0)
    return lower_part + upper_portion


def contract_last(left_side, right_side):
    return lax.dot_general(
        left_side, right_side, (((1,), (1,)), ((), ())), preferred_element_type=jnp.float32
    )


def dot_nt(left_side, right_side):
    return lax.dot_general(
        left_side, right_side, (((1,), (1,)), ((), ())), preferred_element_type=jnp.float32
    )


def dot_tn(left_side, right_side):
    return lax.dot_general(
        left_side, right_side, (((0,), (0,)), ((), ())), preferred_element_type=jnp.float32
    )


def dot_nn(left_side, right_side):
    return jnp.dot(left_side, right_side, preferred_element_type=jnp.float32)


OUT0, OUT1, HEAD = range(3)
KEY, VALUE, QUERY = range(3)
CHUNKS = 9
ROUTES = (0, 1, 0, 0, 1, 0, 1, 0, 1)
HALF = INNER // 2
GROUPS = 2
GROUP = HEADS // GROUPS
PADDED = 32
WINDOW = 3


def split_dot(dot, left_side, right_side):
    first = left_side.astype(jnp.bfloat16)
    remainder = left_side - first.astype(jnp.float32)
    second = remainder.astype(jnp.bfloat16)
    third = (remainder - second.astype(jnp.float32)).astype(jnp.bfloat16)
    return dot(third, right_side) + dot(second, right_side) + dot(first, right_side)


def spread(rows, columns, where):
    row = lax.broadcasted_iota(jnp.int32, (rows, columns), 0)
    column = lax.broadcasted_iota(jnp.int32, (rows, columns), 1)
    return where(row, column)


def block_kernel(
    fsdp,
    lat_rows,
    lon_cols,
    tokens_ref,
    gain_ref,
    qkv_ref,
    out_ref,
    head_ref,
    coarse_ref,
    fine_grad_ref,
    fine_ref,
    grad_tokens_ref,
    grad_head_ref,
    w_out0,
    w_out1,
    w_head,
    w_key0,
    w_value0,
    w_query0,
    w_key1,
    w_value1,
    w_query1,
    standard_ref,
    inverse_ref,
    mixed_ref,
    normed_ref,
    q_ref,
    k_ref,
    v_ref,
    p_ref,
    att_ref,
    ga_ref,
    gh_ref,
    hidden_ref,
    gq_ref,
    gk_ref,
    gv_ref,
    gn_ref,
    rows_ref,
    shuffled_ref,
    residual_ref,
    coarse_pad,
    w_head_shuffled,
    halo_out,
    grad_halo_out,
    grad_halo_in,
    term_ref,
    rs0,
    snd1,
    rs1,
    acc1,
    snd2,
    rs2,
    acc2,
    rs3,
    full_grad,
    local_sem,
    w_send,
    w_recv,
    halo_send,
    halo_recv,
    coarse_send,
    coarse_recv,
    rs_send,
    rs_recv,
    back_send,
    back_recv,
):
    row_count = lat_rows * lon_cols
    halo_rows = lat_rows * MARGIN
    fine_cols = 4 * lon_cols
    core = lax.axis_index("dp")
    me = lax.axis_index("fsdp")
    tile = lax.axis_index("tile")
    tiles = lax.axis_size("tile")
    ty, tx = tile // 2, tile % 2
    x_side = {"tile": tile + 1 - 2 * tx}
    y_side = {"tile": (tile + 2) % tiles}
    sibling = {"dp": 1 - core}
    right = {"tile": (tile + 1) % tiles}
    left = {"tile": (tile + tiles - 1) % tiles}
    weights = (w_out0, w_out1, w_head, w_key0, w_value0, w_query0, w_key1, w_value1, w_query1)
    depth = w_head.shape[1] * 4 * w_head.shape[4]
    bf16, f32 = jnp.bfloat16, jnp.float32

    def qkv_chunk(group, which):
        return 3 + 3 * group + which

    def qkv_columns(chunk):
        group, which = (chunk - 3) // 3, (chunk - 3) % 3
        return pl.ds({KEY: 1, VALUE: 2, QUERY: 0}[which] * INNER + group * HALF, HALF)

    def own_piece(chunk):
        if chunk == HEAD:
            return w_head.at[me, core, ty, tx]
        if chunk in (OUT0, OUT1):
            start = core * 2 * HALF + (chunk - OUT0) * HALF
            return out_ref.at[ty, tx, :, pl.ds(pl.multiple_of(start, 128), HALF)]
        return qkv_ref.at[core, ty, tx, :, qkv_columns(chunk)]

    def remote(src, dst, send, recv, device):
        return pltpu.make_async_remote_copy(
            src_ref=src,
            dst_ref=dst,
            send_sem=send,
            recv_sem=recv,
            device_id=device,
            device_id_type=pl.DeviceIdType.MESH,
        )

    def weight_copy(chunk, stage, k):
        full = weights[chunk]
        send, recv = w_send.at[chunk, stage, k - 1], w_recv.at[chunk, stage, k - 1]
        source = (me + fsdp - k) % fsdp
        if stage == 0:
            device = {"fsdp": (me + k) % fsdp}
            return remote(own_piece(chunk), full.at[me, core, ty, tx], send, recv, device)
        if stage == 1:
            part = full.at[source, core, ty, tx]
            device = x_side if ROUTES[chunk] == 0 else y_side
        elif stage == 2:
            if ROUTES[chunk] == 0:
                part, device = full.at[source, core, ty], y_side
            else:
                part, device = full.at[source, core, :, tx], x_side
        else:
            part, device = full.at[source, core], sibling
        return remote(part, part, send, recv, device)

    def advance(*steps):
        for chunk, stage in steps:
            for k in range(1, fsdp):
                if stage > 0:
                    weight_copy(chunk, stage - 1, k).wait_recv()
                if stage < 4:
                    weight_copy(chunk, stage, k).start()
            if stage == 1 and chunk + WINDOW < CHUNKS:
                advance((chunk + WINDOW, 0))

    def local_copies():
        pairs = []
        for d in range(2):
            for half, full in enumerate((w_out0, w_out1)):
                start = d * 2 * HALF + half * HALF
                pairs.append((out_ref.at[:, :, :, pl.ds(start, HALF)], full.at[me, d]))
        for chunk in range(3, CHUNKS):
            pairs.append((qkv_ref.at[:, :, :, :, qkv_columns(chunk)], weights[chunk].at[me]))
        return [
            pltpu.make_async_copy(src, dst, local_sem.at[i]) for i, (src, dst) in enumerate(pairs)
        ]

    copies = local_copies()
    for copy in copies:
        copy.start()

    barrier = pltpu.get_barrier_semaphore()
    partners = [{"tile": (tile + i) % tiles} for i in range(1, 4)]
    partners += [{"fsdp": (me + i) % fsdp} for i in range(1, fsdp)]
    partners += [sibling]
    for partner in partners:
        pl.semaphore_signal(barrier, inc=1, device_id=partner, device_id_type=pl.DeviceIdType.MESH)
    pl.semaphore_wait(barrier, len(partners))

    advance((OUT0, 0), (OUT1, 0))
    eye = spread(depth, depth, lambda r, c: (r == c).astype(f32)).astype(bf16)
    w_head[me] = dot_nt(eye, head_ref[...]).astype(bf16).reshape(w_head.shape[1:])
    advance((HEAD, 0))
    cells = lat_rows * PADDED
    shuffled_ref[pl.ds(0, cells), :] = jnp.zeros((cells, fine_cols), f32)
    shuffled_ref[pl.ds(0, VARS * lat_rows), pl.ds(0, lon_cols)] = coarse_ref[...]
    by_latitude = spread(
        cells, cells, lambda r, c: (c == (r % lat_rows) * PADDED + r // lat_rows).astype(f32)
    ).astype(bf16)
    coarse_pad[pl.ds(MARGIN, lon_cols), :] = split_dot(
        dot_nn, shuffled_ref[pl.ds(0, cells), :].T[:lon_cols], by_latitude
    )
    coarse_copies = [
        remote(
            coarse_pad.at[pl.ds(lon_cols, MARGIN)],
            coarse_pad.at[pl.ds(0, MARGIN)],
            coarse_send.at[0],
            coarse_recv.at[0],
            right,
        ),
        remote(
            coarse_pad.at[pl.ds(MARGIN, MARGIN)],
            coarse_pad.at[pl.ds(MARGIN + lon_cols, MARGIN)],
            coarse_send.at[1],
            coarse_recv.at[1],
            left,
        ),
    ]
    for copy in coarse_copies:
        copy.start()

    scale = HEAD_DIM ** (-0.5)

    def normalised():
        return layer_norm(tokens_ref[...].astype(f32))

    standard, inverse_dev = normalised()
    standard_ref[...] = standard
    inverse_ref[...] = inverse_dev
    normed_ref[...] = (standard * gain_ref[...][None, :]).astype(bf16)

    advance((0, 1))

    def cell_rows(i, a):
        return pl.ds((i * 4 + a) * PADDED, VARS)

    def fine_rows(i, a):
        return pl.ds(4 * i + a, VARS, stride=4 * lat_rows)

    shuffled_ref[...] = jnp.zeros_like(shuffled_ref)
    for i in range(lat_rows):
        for a in range(4):
            shuffled_ref[cell_rows(i, a), :] = fine_grad_ref[fine_rows(i, a), :]
    by_phase = spread(
        fine_cols, fine_cols, lambda r, c: (r == 4 * (c % lon_cols) + c // lon_cols).astype(f32)
    ).astype(bf16)
    to_phase = spread(
        fine_cols, fine_cols, lambda r, c: (c == 4 * (r % lon_cols) + r // lon_cols).astype(f32)
    ).astype(bf16)
    to_feature = spread(
        16 * PADDED,
        HEAD_OUT,
        lambda r, c: (
            c == 16 * (r % PADDED) + 4 * (r // PADDED % 4) + r // (4 * PADDED)
        ).astype(f32),
    ).astype(bf16)
    width = 4 * PADDED
    turned = dot_nn(shuffled_ref[...].astype(bf16), by_phase).T
    turned = jnp.concatenate(
        [
            jnp.concatenate(
                [
                    turned[b * lon_cols : (b + 1) * lon_cols, i * width : (i + 1) * width]
                    for b in range(4)
                ],
                axis=1,
            )
            for i in range(lat_rows)
        ],
        axis=0,
    )
    rows_ref[...] = dot_nn(turned.astype(bf16), to_feature).astype(bf16)

    advance((1, 1), (0, 2), (2, 1), (1, 2), (0, 3), (3, 1), (2, 2))
    for copy in copies:
        copy.wait()

    for copy in coarse_copies:
        copy.wait_recv()

    def lon_weight(row, column):
        phase = column % 4
        lower_shift = (phase < 2).astype(jnp.int32)
        upper_weight = (2 * phase - 3 + 8 * lower_shift).astype(f32) / 8.0
        lower_cell = column // 4 - lower_shift + MARGIN
        return jnp.where(row == lower_cell, 1.0 - upper_weight, 0.0) + jnp.where(
            row == lower_cell + 1, upper_weight, 0.0
        )

    lon_matrix = spread(coarse_pad.shape[0], fine_cols, lon_weight).astype(bf16)
    incomplete = split_dot(dot_nn, coarse_pad[...].T, lon_matrix)
    for i in range(lat_rows):
        for a in range(4):
            low = i - 1 if a < 2 else i
            upper_weight = (5 / 8, 7 / 8, 1 / 8, 3 / 8)[a]
            lower, upper = (
                incomplete[cell * PADDED : (cell + 1) * PADDED]
                for cell in (max(low, 0), min(low + 1, lat_rows - 1))
            )
            residual_ref[pl.ds((i * 4 + a) * PADDED, PADDED), :] = (
                lower * (1.0 - upper_weight) + upper * upper_weight
            )

    advance((0, 4), (1, 3), (4, 1), (3, 2), (1, 4), (2, 3), (5, 1), (4, 2))

    def columns_of(f):
        return pl.ds(pl.multiple_of(f * depth, 128), depth)

    advance((2, 4))

    def grad_hidden_step(f, _):
        rows = w_head[f].reshape(depth, HEAD_OUT)
        gh_ref[:, columns_of(f)] = dot_nt(rows_ref[...], rows)
        w_head_shuffled[pl.ds(pl.multiple_of(f * depth, 128), depth), :] = dot_nt(
            rows, to_feature
        ).astype(bf16)
        return 0

    lax.fori_loop(0, fsdp, grad_hidden_step, 0)
    advance((3, 3), (6, 1), (5, 2))
    out_parts = [(d, half) for d in range(2) for half in range(2)]

    def out_block(d, half):
        full = (w_out0, w_out1)[half]
        return full[:, d].reshape(INNER, HALF)

    def out_columns(d, half):
        return pl.ds(d * 2 * HALF + half * HALF, HALF)

    grad_attended = jnp.zeros((row_count, INNER), f32)
    for d, half in out_parts:
        low = gh_ref[:, out_columns(d, half)].astype(bf16)
        grad_attended = grad_attended + dot_nt(low, out_block(d, half))
    ga_ref[...] = grad_attended.astype(bf16)

    advance((4, 3), (7, 1), (6, 2))

    def edge(rows, first):
        shaped = rows.reshape(lat_rows, lon_cols, rows.shape[-1])
        part = shaped[:, :MARGIN] if first else shaped[:, lon_cols - MARGIN :]
        return part.reshape(halo_rows, rows.shape[-1])

    def halo_copy(group, which, side):
        full = (k_ref, v_ref)[which]
        index = (0, group, which, side)
        return remote(
            halo_out.at[group, which, side],
            full.at[group, pl.ds(row_count + side * halo_rows, halo_rows)],
            halo_send.at[index],
            halo_recv.at[index],
            (right, left)[side],
        )

    def grad_halo_copy(group, which, side):
        index = (1, group, which, side)
        return remote(
            grad_halo_out.at[group, which, side],
            grad_halo_in.at[group, which, side],
            halo_send.at[index],
            halo_recv.at[index],
            (left, right)[side],
        )

    def project(group, which):
        full = weights[qkv_chunk(group, which)]
        product = dot_nn(normed_ref[...], full[...].reshape(-1, HALF))
        if which == QUERY:
            q_ref[group] = product.astype(bf16)
            return
        (k_ref, v_ref)[which][group, pl.ds(0, row_count)] = product.astype(bf16)
        for side in range(2):
            halo_out[group, which, side] = edge(product, side == 1).astype(bf16)
            halo_copy(group, which, side).start()

    def await_halos(group):
        for which in range(2):
            for side in range(2):
                halo_copy(group, which, side).wait_recv()

    def window(i):
        low, high = i * HEAD_DIM, (i + 1) * HEAD_DIM
        start, stop = low // 128 * 128, -(-high // 128) * 128
        lanes = lax.broadcasted_iota(jnp.int32, (1, stop - start), 1) + start
        return start, stop, ((lanes >= low) & (lanes < high)).astype(f32)

    def add_parts(parts, start, product):
        for j in range(product.shape[1] // 128):
            piece = product[:, j * 128 : (j + 1) * 128]
            at = start // 128 + j
            parts[at] = piece if parts[at] is None else parts[at] + piece

    def no_parts():
        return [None] * (HALF // 128)

    def forward(group, between=()):
        parts = no_parts()
        for i in range(GROUP):
            start, stop, mask = window(i)
            masked = q_ref[group, :, start:stop] * mask.astype(bf16)
            scores = dot_nt(masked, k_ref[group, :, start:stop]) * scale
            biggest = jnp.max(scores, axis=-1, keepdims=True)
            exponent = jnp.exp(scores - biggest)
            softmax = exponent / jnp.sum(exponent, axis=-1, keepdims=True)
            p_ref[group * GROUP + i] = softmax
            add_parts(parts, start, dot_nn(softmax.astype(bf16), v_ref[group, :, start:stop]) * mask)
            if i < len(between):
                between[i]()
        att_ref[:, pl.ds(group * HALF, HALF)] = jnp.concatenate(parts, axis=1).astype(bf16)

    def backward(group, between=()):
        query_parts, key_parts, value_parts = no_parts(), no_parts(), no_parts()
        for i in range(GROUP):
            start, stop, mask = window(i)
            softmax = p_ref[group * GROUP + i]
            grads = ga_ref[:, group * HALF + start : group * HALF + stop]
            weights_grad = dot_nt(grads * mask.astype(bf16), v_ref[group, :, start:stop])
            weighted = jnp.sum(softmax * weights_grad, axis=-1, keepdims=True)
            grad_scores = (softmax * (weights_grad - weighted)).astype(bf16)
            scaled = mask * scale
            add_parts(query_parts, start, dot_nn(grad_scores, k_ref[group, :, start:stop]) * scaled)
            add_parts(key_parts, start, dot_tn(grad_scores, q_ref[group, :, start:stop]) * scaled)
            add_parts(value_parts, start, dot_tn(softmax.astype(bf16), grads) * mask)
            if i < len(between):
                between[i]()
        gq_ref[group] = jnp.concatenate(query_parts, axis=1).astype(bf16)
        gk_ref[group] = jnp.concatenate(key_parts, axis=1)
        gv_ref[group] = jnp.concatenate(value_parts, axis=1)
        for which, full in enumerate((gk_ref, gv_ref)):
            for side in range(2):
                rows = full[group, pl.ds(row_count + side * halo_rows, halo_rows), :]
                grad_halo_out[group, which, side] = rows.astype(bf16)
                grad_halo_copy(group, which, side).start()

    def own_cells(group, which):
        full = (gk_ref, gv_ref)[which]
        for side in range(2):
            grad_halo_copy(group, which, side).wait_recv()
        rows = full[group, pl.ds(0, row_count), :].reshape(lat_rows, lon_cols, HALF)
        shape = (lat_rows, MARGIN, HALF)
        last = grad_halo_in[group, which, 0].astype(f32).reshape(shape)
        first = grad_halo_in[group, which, 1].astype(f32).reshape(shape)
        rows = jnp.concatenate(
            [
                rows[:, :MARGIN] + first,
                rows[:, MARGIN : lon_cols - MARGIN],
                rows[:, lon_cols - MARGIN :] + last,
            ],
            axis=1,
        )
        return rows.reshape(row_count, HALF).astype(bf16)

    def add_grad_normed(group, which, first=False):
        full = weights[qkv_chunk(group, which)]
        if which != QUERY:
            (k_ref, v_ref)[which][group, pl.ds(0, row_count)] = own_cells(group, which)

        def step(f, _):
            if which == QUERY:
                rows = gq_ref[group]
            else:
                rows = (k_ref, v_ref)[which][group, pl.ds(0, row_count)]
            product = dot_nt(rows, full[f].reshape(depth, HALF))
            if first:
                gn_ref[:, columns_of(f)] = product
            else:
                gn_ref[:, columns_of(f)] += product
            return 0

        lax.fori_loop(0, fsdp, step, 0)

    advance((3, 4))
    project(0, KEY)
    advance((4, 4))
    project(0, VALUE)
    advance((5, 3), (8, 1), (7, 2), (5, 4))
    project(0, QUERY)
    advance((6, 3))
    await_halos(0)
    forward(0, (lambda: None, lambda: advance((8, 2)), lambda: advance((7, 3))))
    advance((6, 4))
    project(1, KEY)

    def next_values():
        advance((7, 4))
        project(1, VALUE)

    backward(0, (lambda: advance((8, 3)), next_values))
    for d, half in out_parts:
        columns = out_columns(d, half)
        mixed = dot_nn(att_ref[:, pl.ds(0, HALF)], out_block(d, half)[:HALF])
        mixed_ref[:, columns] = tokens_ref[:, columns].astype(f32) + mixed
    add_grad_normed(0, QUERY, first=True)
    advance((8, 4))
    project(1, QUERY)
    for chunk in range(CHUNKS):
        for stage in range(4):
            for k in range(1, fsdp):
                weight_copy(chunk, stage, k).wait_send()
    await_halos(1)
    forward(1)
    for d, half in out_parts:
        columns = out_columns(d, half)
        mixed = dot_nn(att_ref[:, pl.ds(HALF, HALF)], out_block(d, half)[HALF:])
        hidden_ref[:, columns] = (mixed_ref[:, columns] + mixed).astype(bf16)

    def term_step(f, _):
        term_ref[f] = dot_tn(rows_ref[...], hidden_ref[:, columns_of(f)]).reshape(
            term_ref.shape[1:]
        )
        return 0

    lax.fori_loop(0, fsdp, term_step, 0)

    core_copy = remote(term_ref.at[:, 1 - core], rs0, rs_send.at[0], rs_recv.at[0], sibling)
    half = fsdp // 2
    routes = (
        (pl.ds(0, half), ty, tx, y_side, x_side),
        (pl.ds(half, fsdp - half), tx, ty, x_side, y_side),
    )
    first_copies = [
        remote(snd1.at[part], rs1.at[part], rs_send.at[1 + i], rs_recv.at[1 + i], near)
        for i, (part, _, _, near, _) in enumerate(routes)
    ]
    second_copies = [
        remote(snd2.at[part], rs2.at[part], rs_send.at[3 + i], rs_recv.at[3 + i], far)
        for i, (part, _, _, _, far) in enumerate(routes)
    ]
    on_second = me // half
    outer = ty + on_second * (tx - ty)
    inner = tx + on_second * (ty - tx)
    z_copies = [
        remote(
            acc2.at[(me + k) % fsdp],
            rs3.at[k - 1],
            rs_send.at[5 + k],
            rs_recv.at[5 + k],
            {"fsdp": (me + k) % fsdp},
        )
        for k in range(1, fsdp)
    ]
    mine = full_grad.at[core, outer, inner]
    back = [
        remote(
            mine,
            mine,
            back_send.at[i - 1],
            back_recv.at[i - 1],
            {"tile": (tile + i) % tiles},
        )
        for i in range(1, 4)
    ]
    last_back = remote(
        full_grad.at[core], full_grad.at[core], rs_send.at[5], rs_recv.at[5], sibling
    )

    def reduce_first():
        core_copy.wait_recv()
        for copy, (part, first, _, _, _) in zip(first_copies, routes):
            theirs = term_ref[part, core, 1 - first] + rs0[part, 1 - first]
            snd1[part] = theirs.reshape(-1, *snd1.shape[1:]).astype(bf16)
            copy.start()
        for part, first, _, _, _ in routes:
            acc1[part] = term_ref[part, core, first] + rs0[part, first]

    def reduce_second():
        for copy, (part, _, second, _, _) in zip(first_copies, routes):
            copy.wait_recv()
            arrived = rs1[part].astype(f32)
            acc1[part] = acc1[part] + arrived.reshape(-1, *acc1.shape[1:])
        for copy, (part, _, second, _, _) in zip(second_copies, routes):
            snd2[part] = acc1[part, 1 - second]
            copy.start()

    def reduce_z():
        for copy, (part, _, second, _, _) in zip(second_copies, routes):
            copy.wait_recv()
            acc2[part] = acc1[part, second] + rs2[part]
        for copy in z_copies:
            copy.start()

    core_copy.start()
    backward(1, (lambda: None, reduce_first))
    add_grad_normed(0, KEY)
    add_grad_normed(0, VALUE)
    reduce_second()
    add_grad_normed(1, QUERY)

    head_out = dot_nn(hidden_ref[...], w_head_shuffled[...])
    head_out = jnp.concatenate(
        [
            jnp.concatenate(
                [
                    head_out[i * lon_cols : (i + 1) * lon_cols, b * width : (b + 1) * width]
                    for b in range(4)
                ],
                axis=0,
            )
            for i in range(lat_rows)
        ],
        axis=1,
    )
    shuffled_ref[...] = split_dot(dot_nn, head_out.T, to_phase) + residual_ref[...]
    for i in range(lat_rows):
        for a in range(4):
            fine_ref[fine_rows(i, a), :] = shuffled_ref[cell_rows(i, a), :]

    reduce_z()
    add_grad_normed(1, KEY)
    for copy in z_copies:
        copy.wait_recv()
    summed = acc2[me]
    for k in range(1, fsdp):
        summed = summed + rs3[k - 1]
    full_grad[core, outer, inner] = summed
    for copy in back:
        copy.start()
    add_grad_normed(1, VALUE)
    for copy in back:
        copy.wait_recv()
    last_back.start()

    grad_input = norm_backward(
        gn_ref[...], standard_ref[...], inverse_ref[...], gain_ref[...][None, :]
    )
    grad_tokens_ref[...] = (gh_ref[...] + grad_input).astype(bf16)

    last_back.wait_recv()
    grad_head_ref[...] = full_grad[...]

    for group in range(GROUPS):
        for which in range(2):
            for side in range(2):
                halo_copy(group, which, side).wait_send()
                grad_halo_copy(group, which, side).wait_send()
    for copy in coarse_copies + [core_copy, last_back] + first_copies + second_copies + z_copies + back:
        copy.wait_send()


def fused_shards(
    tokens, norm_gain, query_key_value_weight, out_weight, head_weight, coarse, grad_fine
):
    fsdp = lax.axis_size("fsdp")
    lat_rows, lon_cols = tokens.shape[1:3]
    row_count = lat_rows * lon_cols
    halo_rows = lat_rows * MARGIN
    key_count = row_count + 2 * halo_rows
    depth, qkv_width = query_key_value_weight.shape
    piece = depth // 8
    out_piece = out_weight.shape[0] // 4
    head_piece = HEAD_OUT // 8
    bf16, f32 = jnp.bfloat16, jnp.float32
    vmem = pl.BlockSpec(memory_space=pltpu.VMEM)
    hbm = pl.BlockSpec(memory_space=pl.ANY)
    def full(rows, columns):
        return pltpu.VMEM((fsdp, 2, 2, 2, rows, columns), bf16)

    fine_rows = VARS * 4 * lat_rows
    shuffled = 4 * lat_rows * PADDED
    fine_grid, grad_tokens, grad_head = pl.pallas_call(
        functools.partial(block_kernel, fsdp, lat_rows, lon_cols),
        out_shape=(
            jax.ShapeDtypeStruct((fine_rows, 4 * lon_cols), f32),
            jax.ShapeDtypeStruct((row_count, D), bf16),
            jax.ShapeDtypeStruct((2, 2, 2, head_piece, depth), f32),
        ),
        in_specs=[vmem, vmem, hbm, hbm, vmem, vmem, vmem],
        out_specs=(vmem, vmem, vmem),
        scratch_shapes=[
            full(out_piece, HALF),
            full(out_piece, HALF),
            full(piece, HEAD_OUT),
        ]
        + [full(piece, HALF)] * 6
        + [
            pltpu.VMEM((row_count, D), f32),
            pltpu.VMEM((row_count, 1), f32),
            pltpu.VMEM((row_count, D), f32),
            pltpu.VMEM((row_count, D), bf16),
            pltpu.VMEM((GROUPS, row_count, HALF), bf16),
            pltpu.VMEM((GROUPS, key_count, HALF), bf16),
            pltpu.VMEM((GROUPS, key_count, HALF), bf16),
            pltpu.VMEM((HEADS, row_count, key_count), f32),
            pltpu.VMEM((row_count, INNER), bf16),
            pltpu.VMEM((row_count, INNER), bf16),
            pltpu.VMEM((row_count, D), f32),
            pltpu.VMEM((row_count, D), bf16),
            pltpu.VMEM((GROUPS, row_count, HALF), bf16),
            pltpu.VMEM((GROUPS, key_count, HALF), f32),
            pltpu.VMEM((GROUPS, key_count, HALF), f32),
            pltpu.VMEM((row_count, D), f32),
            pltpu.VMEM((row_count, HEAD_OUT), bf16),
            pltpu.VMEM((shuffled, 4 * lon_cols), f32),
            pltpu.VMEM((shuffled, 4 * lon_cols), f32),
            pltpu.VMEM((lon_cols + 2 * MARGIN, lat_rows * PADDED), f32),
            pltpu.VMEM((D, 16 * PADDED), bf16),
            pltpu.VMEM((GROUPS, 2, 2, halo_rows, HALF), bf16),
            pltpu.VMEM((GROUPS, 2, 2, halo_rows, HALF), bf16),
            pltpu.VMEM((GROUPS, 2, 2, halo_rows, HALF), bf16),
            pltpu.VMEM((fsdp, 2, 2, 2, head_piece, depth), f32),
            pltpu.VMEM((fsdp, 2, 2, head_piece, depth), f32),
            pltpu.VMEM((fsdp, 2 * head_piece, depth), bf16),
            pltpu.VMEM((fsdp, 2 * head_piece, depth), bf16),
            pltpu.VMEM((fsdp, 2, head_piece, depth), f32),
            pltpu.VMEM((fsdp, head_piece, depth), f32),
            pltpu.VMEM((fsdp, head_piece, depth), f32),
            pltpu.VMEM((fsdp, head_piece, depth), f32),
            pltpu.VMEM((fsdp - 1, head_piece, depth), f32),
            pltpu.VMEM((2, 2, 2, head_piece, depth), f32),
            pltpu.SemaphoreType.DMA((10,)),
            pltpu.SemaphoreType.DMA((CHUNKS, 4, fsdp - 1)),
            pltpu.SemaphoreType.DMA((CHUNKS, 4, fsdp - 1)),
            pltpu.SemaphoreType.DMA((2, GROUPS, 2, 2)),
            pltpu.SemaphoreType.DMA((2, GROUPS, 2, 2)),
            pltpu.SemaphoreType.DMA((2,)),
            pltpu.SemaphoreType.DMA((2,)),
            pltpu.SemaphoreType.DMA((5 + fsdp,)),
            pltpu.SemaphoreType.DMA((5 + fsdp,)),
            pltpu.SemaphoreType.DMA((3,)),
            pltpu.SemaphoreType.DMA((3,)),
        ],
        compiler_params=pltpu.CompilerParams(
            collective_id=0, has_side_effects=True, vmem_limit_bytes=58 * 1024 * 1024
        ),
        cost_estimate=pl.CostEstimate(
            flops=int(7e9), bytes_accessed=int(1e7), transcendentals=row_count * key_count * HEADS
        ),
    )(
        tokens.reshape(row_count, D),
        norm_gain,
        query_key_value_weight.reshape(2, 2, 2, piece, qkv_width),
        out_weight.reshape(2, 2, out_piece, D),
        head_weight.T,
        coarse.reshape(VARS * lat_rows, lon_cols),
        grad_fine.reshape(fine_rows, 4 * lon_cols),
    )
    return (
        fine_grid.reshape(grad_fine.shape),
        grad_tokens.reshape(tokens.shape),
        grad_head.reshape(HEAD_OUT, depth).T,
    )


def fits_pieces(tokens, qkv, out_weight):
    if lax.axis_size("dp") != 2 or lax.axis_size("tile") != 4 or lax.axis_size("fsdp") % 2:
        return False
    lat_rows, lon_cols = tokens.shape[1:3]
    if lat_rows % 2 or 4 * lon_cols != 128 or VARS > PADDED or 16 * VARS != HEAD_OUT:
        return False
    return qkv.shape[0] % 128 == 0 and out_weight.shape[0] % 64 == 0


def any_shards(*arguments):
    if fits_pieces(arguments[0], arguments[2], arguments[3]):
        return fused_shards(*arguments)
    return shards(*arguments)


def shards(tokens, norm_gain, query_key_value_weight, out_weight, head_weight, coarse, grad_fine):
    lat_rows = tokens.shape[1]
    lon_cols = tokens.shape[2]
    row_count = lat_rows * lon_cols
    flattened_rows = tokens[0].reshape(row_count, D).astype(jnp.float32)
    standard, inverse_dev = layer_norm(flattened_rows)
    normed = (standard * norm_gain).astype(jnp.bfloat16)
    full_qkv = lax.all_gather(query_key_value_weight, "fsdp", axis=0, tiled=True)
    projected = jnp.dot(normed, full_qkv, preferred_element_type=jnp.float32).astype(jnp.bfloat16)
    queries = projected[:, :INNER]
    pairs_local = projected[:, INNER:]
    margin_pairs = with_halo(
        pairs_local.reshape(lat_rows, lon_cols, 2 * INNER), (("tile", 1),), MARGIN
    )
    keys_values = margin_pairs.reshape(lat_rows * (lon_cols + 2 * MARGIN), 2 * INNER)
    attended, softmax_out = attend_forward(queries, keys_values)
    full_out = lax.all_gather(out_weight, "fsdp", axis=0, tiled=True)
    mixed_out = jnp.dot(attended, full_out, preferred_element_type=jnp.float32)
    hidden = (flattened_rows + mixed_out).astype(jnp.bfloat16)
    full_head = lax.all_gather(head_weight, "fsdp", axis=0, tiled=True)
    head_out = jnp.dot(hidden, full_head, preferred_element_type=jnp.float32)
    fine_head = (
        head_out.reshape(lat_rows, lon_cols, VARS, 4, 4)
        .transpose(2, 0, 3, 1, 4)
        .reshape(VARS, 4 * lat_rows, 4 * lon_cols)
    )
    coarse_padded_grid = with_halo(coarse[0], (("tile", 2),), 1)
    lat_lower, lat_upper_weight = interp_weights(jnp.arange(4 * lat_rows, dtype=jnp.int32))
    latitude_matrix = build_matrix(
        jnp.clip(lat_lower, 0, lat_rows - 1),
        jnp.clip(lat_lower + 1, 0, lat_rows - 1),
        lat_upper_weight,
        lat_rows,
    )
    lon_lower, lon_upper_weight = interp_weights(jnp.arange(4 * lon_cols, dtype=jnp.int32))
    lon_matrix = build_matrix(lon_lower + 1, lon_lower + 2, lon_upper_weight, lon_cols + 2)
    incomplete_grid = jnp.einsum(
        "lj,kji->kli", latitude_matrix, coarse_padded_grid, precision=lax.Precision.HIGHEST
    )
    residual = jnp.einsum(
        "vrb,cb->vrc", incomplete_grid, lon_matrix, precision=lax.Precision.HIGHEST
    )
    fine_grid = fine_head + residual
    grad_rows = (
        grad_fine[0]
        .reshape(VARS, lat_rows, 4, lon_cols, 4)
        .transpose(1, 3, 0, 2, 4)
        .reshape(row_count, HEAD_OUT)
    )
    grad_rows = grad_rows.astype(jnp.bfloat16)
    head_term = lax.dot_general(
        hidden, grad_rows, (((0,), (0,)), ((), ())), preferred_element_type=jnp.float32
    )
    head_block = lax.psum_scatter(head_term, "fsdp", scatter_dimension=0, tiled=True)
    grad_head = lax.psum(head_block, ("dp", "tile"))
    grad_hidden = contract_last(grad_rows, full_head)
    grad_attended = contract_last(grad_hidden.astype(jnp.bfloat16), full_out).astype(jnp.bfloat16)
    grad_queries, pair_gradient_rows = attend_backward(
        softmax_out, queries, keys_values, grad_attended
    )
    pair_gradient_rows = pair_gradient_rows.reshape(lat_rows, lon_cols + 2 * MARGIN, 2 * INNER)
    from_left = from_behind(pair_gradient_rows[:, lon_cols + MARGIN :], "tile", 1)
    from_right = from_behind(pair_gradient_rows[:, :MARGIN], "tile", -1)
    own_cells = pair_gradient_rows[:, MARGIN : MARGIN + lon_cols]
    own_cells = own_cells + jnp.pad(from_left, ((0, 0), (0, lon_cols - MARGIN), (0, 0)))
    own_cells = own_cells + jnp.pad(from_right, ((0, 0), (lon_cols - MARGIN, 0), (0, 0)))
    grad_all = jnp.concatenate(
        [grad_queries, own_cells.reshape(row_count, 2 * INNER).astype(jnp.bfloat16)], axis=1
    )
    grad_normed = contract_last(grad_all, full_qkv)
    grad_input = grad_hidden + norm_backward(grad_normed, standard, inverse_dev, norm_gain)
    grad_tokens = grad_input.astype(jnp.bfloat16).reshape(1, lat_rows, lon_cols, D)
    return (fine_grid[None], grad_tokens, grad_head)


def solution(mesh):
    placed = (
        P(("dp", "fsdp"), None, "tile", None),
        P(),
        P("fsdp", None),
        P("fsdp", None),
        P("fsdp", None),
        P(("dp", "fsdp"), None, None, "tile"),
        P(("dp", "fsdp"), None, None, "tile"),
    )
    return jax.shard_map(
        any_shards,
        mesh=mesh,
        in_specs=placed,
        out_specs=(
            P(("dp", "fsdp"), None, None, "tile"),
            P(("dp", "fsdp"), None, "tile", None),
            P("fsdp", None),
        ),
        check_vma=False,
    )
```
